32 devices in a mesh: groups: 2 (over y), dp: 8 (over z, x), layer: 2 (over core).
Axes of the slice: x: 2, y: 2, z: 4, core: 2. Of those that a mesh axis runs over, the one named last changes fastest.
Arguments:
- train_grads: bfloat16 [4096, 2, 4096], P(('groups', 'dp'), 'layer'), parts along dimension 0, as said below
- query_grads: bfloat16 [128, 2, 4096], P(('groups', 'dp'), 'layer'), parts along dimension 0, as said below
- listed: int32 [16, 4], P(('groups', 'dp')), parts along dimension 0, may hold values from 0 to 7, all different within a row; in each aligned block of 8 rows (0 to 7, 8 to 15, ...) at most 6 rows name the same one
Outputs:
- tiles: float32 [64, 8, 256], P(('groups', 'dp'), None, 'layer'), parts along dimension 0
The draws below stay inside these ranges and needn't reach their ends.
There are 2 independent parts, one for each index of `groups`. The reference program is written for one: setup_inputs(seed, part) draws one part's arguments, and reference() takes and returns one part's arrays. A program takes and returns all parts, laid end to end along the dimension named above; each array names one. Nothing has to cross between parts.
Inputs may be any that keep to these rules, and one draw needn't show every extreme that they name: `listed`: each row holds 4 different train shards; no train shard appears in more than 6 rows, and some train shard appears in exactly 6 rows. `train_grads`: draws of projected gradients: finite values of order 0.01 to 1. `query_grads`: draws of projected gradients: finite values of order 0.01 to 1.
All inputs are finite; a program needn't handle non-finite values.
Results may differ from the reference program's by a relative error of at most 0.0036.
Values may be sent and summed in bfloat16 or wider, within the bound.
No kernel may reach another device: no remote copies, remote signals or barrier semaphores. Data moves between devices by JAX's collectives and lax.ppermute only.
A program may use at most 64 MiB of HBM per device.

```python
import math
import jax
import jax.numpy as jnp
import numpy as np
from jax import lax

K_OUT = 64
K_IN = 64
E_DEV = 256
Q_DEV = 8
K = 4096
LAYERS = 2
SHARDS = 8
TRAIN = 2048
QUERIES = 64
R = 4
MOST = 6


def channel_scales(key, spread):
    key_rows = jax.random.fold_in(key, 101)
    key_cols = jax.random.fold_in(key, 102)
    rows_scale = jnp.exp(jax.random.uniform(key_rows, (LAYERS, K_OUT, 1), jnp.float32, 0.0, spread))
    cols_scale = jnp.exp(jax.random.uniform(key_cols, (LAYERS, 1, K_IN), jnp.float32, 0.0, spread))
    return (rows_scale, cols_scale)


def rough_field(base):
    return base + 0.6 * jnp.roll(base, 1, axis=3) + 0.4 * jnp.roll(base, 1, axis=2)


def draw_train_grads(key, part):
    spread = math.log(3.0)
    rows_scale, cols_scale = channel_scales(key, spread)
    key = jax.random.fold_in(key, 1)
    key_base = jax.random.fold_in(key, 11)
    key_examples = jax.random.fold_in(key, 12)
    base = jax.random.normal(key_base, (TRAIN, LAYERS, K_OUT, K_IN), jnp.float32)
    ramp = jnp.exp(math.log(3.0) * jnp.arange(TRAIN, dtype=jnp.float32) / TRAIN)
    example_scale = jnp.exp(jax.random.uniform(key_examples, (TRAIN,), jnp.float32, 0.0, math.log(4.0))) * ramp
    values = 0.1 * rough_field(base) * rows_scale[None] * cols_scale[None] * example_scale[:, None, None, None]
    return values.reshape(TRAIN, LAYERS, K_OUT * K_IN).astype(jnp.bfloat16)


def draw_query_grads(key, part):
    spread = math.log(3.0)
    rows_scale, cols_scale = channel_scales(key, spread)
    key = jax.random.fold_in(key, 2)
    key_base = jax.random.fold_in(key, 21)
    key_examples = jax.random.fold_in(key, 22)
    base = jax.random.normal(key_base, (QUERIES, LAYERS, K_OUT, K_IN), jnp.float32)
    example_scale = jnp.exp(jax.random.uniform(key_examples, (QUERIES,), jnp.float32, 0.0, math.log(4.0)))
    values = 0.1 * rough_field(base) * rows_scale[None] * cols_scale[None] * example_scale[:, None, None, None]
    return values.reshape(QUERIES, LAYERS, K_OUT * K_IN).astype(jnp.bfloat16)


def routed_block(key, own, number, rows, amount, top, bound, skew):
    order = jax.random.permutation(key, amount)
    heavy_load, usual = shares(amount, rows * top, bound, skew, True), shares(amount, rows * top, bound, skew, False)
    places = jnp.arange(amount)

    def named(lengths, turn):
        used = int((lengths > 0).sum())
        fixed = max(1, used // 4)
        moved = fixed + (places - fixed + turn * (used - fixed)) % max(1, amount - fixed)
        return jnp.zeros((amount,), jnp.int32).at[order[jnp.where(places < fixed, places, moved)]].set(jnp.asarray(lengths, jnp.int32))

    lengths = jnp.where(number % 4 == 0, named(heavy_load, number // 4), named(usual, number - number // 4 - 1))
    mixed = jax.random.permutation(jax.random.fold_in(own, 3), amount)
    giver, sink = mixed[0:amount // 2 * 2:2], mixed[1:amount // 2 * 2:2]
    room = jnp.minimum(lengths[giver] - 1, bound - lengths[sink]) // 2
    room = jnp.where((giver == order[0]) | (sink == order[0]) | (lengths[sink] == 0), 0, jnp.maximum(room, 0))
    moved = jax.random.randint(jax.random.fold_in(own, 4), (amount // 2,), 0, 1 << 20) % (room + 1)
    lengths = lengths.at[giver].add(-moved).at[sink].add(moved)
    labels = jnp.searchsorted(jnp.cumsum(lengths), jnp.arange(rows * top), side="right").astype(jnp.int32)
    listing = labels.reshape(top, rows).T
    listing = listing[jax.random.permutation(jax.random.fold_in(own, 1), rows)]
    turn = jax.random.randint(jax.random.fold_in(own, 2), (rows, 1), 0, top)
    return jnp.take_along_axis(listing, (jnp.arange(top)[None, :] + turn) % top, axis=1)


def shares(amount, total, most, slope, full):
    weights = [(1 << 20) // math.isqrt(standing ** slope) + 1 for standing in range(1, amount + 1)]
    largest = most if full else min(most, max(-(-total // amount), total * weights[0] // sum(weights)))
    least = 1 if total - largest >= amount - 1 else 0
    holding, spare = [largest] + [least] * (amount - 1), total - largest - least * (amount - 1)
    while spare > 0:
        movable = [i for i in range(1, amount) if holding[i] < largest] or [i for i in range(1, amount) if holding[i] < most]
        whole, budget = sum([weights[i] for i in movable]), spare
        for i in movable:
            addition = min(most - holding[i], max(1, budget * weights[i] // whole), spare)
            holding[i] = holding[i] + addition
            spare = spare - addition
    return np.array(holding)


def setup_inputs(seed: int = 0, part: int = 0) -> dict:
    arg_keys = jax.random.split(jax.random.key(seed), 4)
    part_keys = jax.random.split(jax.random.fold_in(arg_keys[3], part), 4)
    train_grads = draw_train_grads(jax.random.fold_in(jax.random.fold_in(arg_keys[3], part), 71), part)
    query_grads = draw_query_grads(jax.random.fold_in(jax.random.fold_in(arg_keys[3], part), 71), part)
    listed_keys = jax.random.split(jax.random.fold_in(part_keys[2], 1), SHARDS // SHARDS)
    listed_turns = jax.random.permutation(jax.random.fold_in(part_keys[2], 3), SHARDS // SHARDS)
    listed = jax.vmap(lambda own, number: routed_block(jax.random.fold_in(part_keys[2], 2), own, number, SHARDS, SHARDS, R, MOST, 1))(listed_keys, listed_turns).reshape((SHARDS, R))
    return dict(train_grads=train_grads, query_grads=query_grads, listed=listed)


def chol_solve(factor, right_side):
    lower_done = lax.linalg.triangular_solve(factor, right_side, left_side=True, lower=True)
    return lax.linalg.triangular_solve(factor, lower_done, left_side=True, lower=True, transpose_a=True)

def damped_factors(in_sum, out_sum, total_count):
    in_cov = in_sum / total_count
    out_cov = out_sum / total_count
    in_trace = jnp.trace(in_cov, axis1=1, axis2=2)
    out_trace = jnp.trace(out_cov, axis1=1, axis2=2)
    in_eye = jnp.eye(in_cov.shape[1], dtype=jnp.float32)
    out_eye = jnp.eye(out_cov.shape[1], dtype=jnp.float32)
    in_damped = in_cov / (in_trace / in_cov.shape[1])[:, None, None] + 0.1 * in_eye
    out_damped = out_cov + 0.1 * (out_trace / out_cov.shape[1])[:, None, None] * out_eye
    return (jnp.linalg.cholesky(in_damped), jnp.linalg.cholesky(out_damped))

def precondition(gradients, in_chol, out_chol):
    count = gradients.shape[0]
    layer_count = gradients.shape[1]
    rows_out = out_chol.shape[1]
    cols_in = in_chol.shape[1]
    field = gradients.astype(jnp.float32).reshape(count, layer_count, rows_out, cols_in)
    stacked = jnp.transpose(field, (1, 2, 0, 3)).reshape(layer_count, rows_out, count * cols_in)
    solved = jax.vmap(chol_solve)(out_chol, stacked)
    solved = jnp.transpose(solved.reshape(layer_count, rows_out, count, cols_in), (0, 3, 2, 1))
    solved = solved.reshape(layer_count, cols_in, count * rows_out)
    twice = jax.vmap(chol_solve)(in_chol, solved)
    twice = jnp.transpose(twice.reshape(layer_count, cols_in, count, rows_out), (2, 0, 3, 1))
    return twice.reshape(count, layer_count, rows_out * cols_in).astype(jnp.bfloat16)

def reference(train_grads, query_grads, listed):
    blocks = train_grads.reshape(SHARDS, E_DEV, LAYERS, K_OUT, K_IN)

    def accumulate(carry, block):
        field = block.astype(jnp.float32)
        in_part = jnp.einsum('nlij,nlik->ljk', field, field, precision=lax.Precision.HIGHEST)
        out_part = jnp.einsum('nlij,nlkj->lik', field, field, precision=lax.Precision.HIGHEST)
        return ((carry[0] + in_part, carry[1] + out_part), None)
    start_sums = (jnp.zeros((LAYERS, K_IN, K_IN), jnp.float32), jnp.zeros((LAYERS, K_OUT, K_OUT), jnp.float32))
    (in_sum, out_sum), _ = lax.scan(accumulate, start_sums, blocks)
    in_chol, out_chol = damped_factors(in_sum, out_sum, float(TRAIN))
    precond = precondition(query_grads, in_chol, out_chol)
    precond_shards = precond.reshape(SHARDS, Q_DEV, LAYERS, K)

    def per_owner(owner):
        owned = precond_shards[owner].astype(jnp.float32)

        def per_listed(target):
            begin = (target * E_DEV).astype(jnp.int32)
            block = lax.dynamic_slice_in_dim(train_grads, begin, E_DEV, 0).astype(jnp.float32)
            return jnp.einsum('qlk,elk->qe', owned, block, precision=lax.Precision.HIGHEST)
        return lax.map(per_listed, listed[owner])
    owners = jnp.arange(SHARDS, dtype=jnp.int32)
    tiles = lax.map(per_owner, owners)
    return tiles.reshape(SHARDS * R, Q_DEV, E_DEV)
```

```python
import functools
import jax
import jax.numpy as jnp
from jax import lax
from jax.experimental import pallas as pl
from jax.experimental.pallas import tpu as pltpu
from jax.sharding import PartitionSpec as P

K_OUT = 64
K_IN = 64
LANES = 128
CHUNK = 64
PIVOT = 4
F32 = jnp.float32
BF16 = jnp.bfloat16
VMEM_LIMIT = 48 * 1024 * 1024

NT = (((1,), (1,)), ((), ()))


def low_half(rows):
    return lax.broadcasted_iota(jnp.int32, (rows, LANES), 1) < LANES // 2


def swap_pair(first, second):
    low = low_half(first.shape[0])
    even = jnp.where(low, first, pltpu.roll(second, LANES // 2, 1))
    odd = jnp.where(low, pltpu.roll(first, LANES // 2, 1), second)
    return even, odd


def covariance_kernel(train_ref, cov_ref, turned, by_in, by_out):
    examples, width = train_ref.shape
    blocks = width // LANES
    parts = examples // LANES
    for c in range(blocks):
        block = train_ref[:, c * LANES:(c + 1) * LANES].astype(F32).T
        for part in range(parts):
            piece = block[:, part * LANES:(part + 1) * LANES]
            turned[part, c * LANES:(c + 1) * LANES, :] = piece
        small = block.astype(BF16)
        for half in range(2):
            start = (2 * c + half) * examples
            by_in[:, start:start + examples] = small[half * K_IN:(half + 1) * K_IN, :]
    for j in range(K_IN):
        for part in range(parts):
            start = j * examples + part * LANES
            for half in range(2):
                rows = turned[part, pl.ds(half * K_IN + j, blocks, stride=LANES), :]
                by_out[half * blocks:(half + 1) * blocks, start:start + LANES] = rows.astype(BF16)
    in_sum = lax.dot_general(by_in[...], by_in[...], NT, preferred_element_type=F32)
    out_sum = lax.dot_general(by_out[...], by_out[...], NT, preferred_element_type=F32)
    cov_ref[...] = jnp.concatenate([in_sum, out_sum], axis=1)


def covariance_sums(train):
    examples, width = train.shape
    return pl.pallas_call(
        covariance_kernel,
        out_shape=jax.ShapeDtypeStruct((K_OUT, 2 * K_IN), F32),
        in_specs=[pl.BlockSpec(memory_space=pltpu.VMEM)],
        out_specs=pl.BlockSpec(memory_space=pltpu.VMEM),
        scratch_shapes=[
            pltpu.VMEM((examples // LANES, width, LANES), F32),
            pltpu.VMEM((K_IN, K_OUT * examples), BF16),
            pltpu.VMEM((K_OUT, K_IN * examples), BF16),
        ],
        compiler_params=pltpu.CompilerParams(vmem_limit_bytes=VMEM_LIMIT),
        cost_estimate=pl.CostEstimate(flops=4 * examples * 64**3, bytes_accessed=2 * examples * width, transcendentals=0),
        name="covariance",
    )(train)


def turn_kernel(*refs):
    query_refs, out_ref, spread = refs[:-2], refs[-2], refs[-1]
    blocks = out_ref.shape[0] // 2
    half = CHUNK // 2
    for c in range(blocks):
        at = c * CHUNK
        for ref in query_refs:
            count = ref.shape[0]
            spread[at:at + count, :] = ref[:, c * LANES:(c + 1) * LANES].astype(F32)
            at = at + count
    for p in range(half):
        first = spread[pl.ds(p, blocks, stride=CHUNK), :]
        second = spread[pl.ds(p + half, blocks, stride=CHUNK), :]
        even, odd = swap_pair(first, second)
        out_ref[:blocks, p * LANES:(p + 1) * LANES] = even.astype(BF16)
        out_ref[blocks:, p * LANES:(p + 1) * LANES] = odd.astype(BF16)


def turned_queries(queries):
    width = queries[0].shape[1]
    total = sum(part.shape[0] for part in queries)
    steps = total // CHUNK
    if steps == 1:
        in_specs = [pl.BlockSpec(part.shape, lambda step: (0, 0)) for part in queries]
    else:
        in_specs = [pl.BlockSpec((CHUNK, width), lambda step: (step, 0))]
    return pl.pallas_call(
        turn_kernel,
        out_shape=jax.ShapeDtypeStruct((K_OUT, total * K_IN), BF16),
        grid=(steps,),
        in_specs=in_specs,
        out_specs=pl.BlockSpec((K_OUT, CHUNK * K_IN), lambda step: (0, step)),
        scratch_shapes=[pltpu.VMEM((width // LANES * CHUNK, LANES), F32)],
        compiler_params=pltpu.CompilerParams(vmem_limit_bytes=VMEM_LIMIT),
        cost_estimate=pl.CostEstimate(flops=total * width, bytes_accessed=4 * total * width, transcendentals=0),
        name="turn_queries",
    )(*queries)


def damped(cov, total_count):
    rows = lax.broadcasted_iota(jnp.int32, (K_OUT, LANES), 0)
    lanes = lax.broadcasted_iota(jnp.int32, (K_OUT, LANES), 1)
    low = lanes < K_IN
    diagonal = rows == jnp.where(low, lanes, lanes - K_IN)
    cov = cov * (1.0 / total_count)
    on_diagonal = jnp.sum(jnp.where(diagonal, cov, 0.0), axis=0, keepdims=True)
    low_row = low_half(1)
    in_mean = jnp.sum(jnp.where(low_row, on_diagonal, 0.0), axis=1, keepdims=True) / K_IN
    out_mean = jnp.sum(jnp.where(low_row, 0.0, on_diagonal), axis=1, keepdims=True) / K_OUT
    scale = jnp.where(low_row, 1.0 / in_mean, 1.0)
    added = jnp.where(low_row, 0.1, 0.1 * out_mean)
    return cov * scale + jnp.where(diagonal, added, 0.0)


def inverses(matrix):
    size = matrix.shape[0]
    lanes = lax.broadcasted_iota(jnp.int32, (size, LANES), 1)
    offset = jnp.where(lanes < size, 0, size)
    rows = lax.broadcasted_iota(jnp.int32, (size, LANES), 0)
    row_lanes = lax.broadcasted_iota(jnp.int32, (8, LANES), 1)
    row_place = jnp.where(row_lanes < size, row_lanes, row_lanes - size)
    place = lanes - offset

    def spread_row(values, row):
        return jnp.broadcast_to(values[row:row + 1, :], (8, LANES))

    for begin in range(0, size, PIVOT):
        columns = [jnp.take_along_axis(matrix, offset + begin + a, axis=1) for a in range(PIVOT)]
        p = [[spread_row(columns[b], begin + a) for b in range(PIVOT)] for a in range(PIVOT)]
        r = []
        for a in range(PIVOT):
            row = spread_row(matrix, begin + a)
            inside = (row_place >= begin) & (row_place < begin + PIVOT)
            unit = jnp.where(row_place == begin + a, 1.0, 0.0)
            r.append(jnp.where(inside, unit, row))
        det = 1.0 / (p[0][0] * p[1][1] - p[0][1] * p[1][0])
        e = [[p[1][1] * det, -p[0][1] * det], [-p[1][0] * det, p[0][0] * det]]
        u = [[e[a][0] * p[0][b] + e[a][1] * p[1][b] for b in (2, 3)] for a in (0, 1)]
        s = [[p[a][b + 2] - (p[a][0] * u[0][b] + p[a][1] * u[1][b]) for b in (0, 1)] for a in (2, 3)]
        det = 1.0 / (s[0][0] * s[1][1] - s[0][1] * s[1][0])
        f = [[s[1][1] * det, -s[0][1] * det], [-s[1][0] * det, s[0][0] * det]]
        w = [e[a][0] * r[0] + e[a][1] * r[1] for a in (0, 1)]
        t = [r[a] - (p[a][0] * w[0] + p[a][1] * w[1]) for a in (2, 3)]
        last = [f[a][0] * t[0] + f[a][1] * t[1] for a in (0, 1)]
        first = [w[a] - (u[a][0] * last[0] + u[a][1] * last[1]) for a in (0, 1)]
        solved = first + last
        inside = (place >= begin) & (place < begin + PIVOT)
        rest = jnp.where(inside, 0.0, matrix)
        tall = [jnp.concatenate([row] * (size // 8), axis=0) for row in solved]
        for a in range(PIVOT):
            rest = rest - columns[a] * tall[a]
        for a in range(PIVOT):
            rest = jnp.where(rows == begin + a, tall[a], rest)
        matrix = rest
    return matrix


def split(values, terms):
    parts = []
    for _ in range(terms):
        part = values.astype(BF16)
        parts.append(part)
        values = values - part.astype(F32)
    return parts


def score_kernel(total_count, route_ref, cov_ref, turned_ref, train_ref, out_ref, left, right, solved, ready):
    blocks = K_OUT // 2
    half = CHUNK // 2
    step = pl.program_id(0)

    @pl.when(step == 0)
    def _():
        inverse = inverses(damped(cov_ref[...], total_count))
        turned = pltpu.roll(inverse, LANES // 2, 1)
        low = low_half(K_OUT)
        left[...] = jnp.concatenate(split(turned[:, :K_OUT], 3), axis=1)
        double = jnp.concatenate([jnp.where(low, inverse, 0.0), jnp.where(low, 0.0, turned)], axis=0)
        high, small = split(double, 2)
        right[:LANES, :LANES] = high
        right[:LANES, LANES:] = small
        right[LANES:, :LANES] = high
        right[LANES:, LANES:] = jnp.zeros_like(small)

    group = 4
    for g in range(half // group):
        block = turned_ref[:, g * group * LANES:(g + 1) * group * LANES]
        tall = jnp.concatenate([block, block, block], axis=0)
        once = jnp.dot(left[...], tall, preferred_element_type=F32)
        once = jnp.concatenate([once[:, k * LANES:(k + 1) * LANES] for k in range(group)], axis=0)
        wide = jnp.concatenate(split(once, 2), axis=1)
        twice = jnp.dot(wide, right[...], preferred_element_type=F32)
        solved[g * group * K_OUT:(g + 1) * group * K_OUT, :] = twice[:, :LANES] + twice[:, LANES:]
    for c in range(blocks):
        first = solved[pl.ds(c, half, stride=K_OUT), :]
        second = solved[pl.ds(c + blocks, half, stride=K_OUT), :]
        even, odd = swap_pair(first, second)
        ready[:half, c * LANES:(c + 1) * LANES] = even.astype(BF16)
        ready[half:, c * LANES:(c + 1) * LANES] = odd.astype(BF16)
    scores = lax.dot_general(ready[...], train_ref[...], NT, preferred_element_type=F32)
    per_query = out_ref.shape[2]
    parts = out_ref.shape[1]
    for s in range(CHUNK // per_query):
        owner = route_ref[step * (CHUNK // per_query) + s]
        for part in range(parts):
            piece = scores[s * per_query:(s + 1) * per_query, part * LANES:(part + 1) * LANES]
            out_ref[owner, part, :, :] = piece


def all_scores(route, cov, turned, train, per_query, total_count):
    shard_count = route.shape[0]
    examples, width = train.shape
    steps = shard_count * per_query // CHUNK
    parts = examples // LANES
    return pl.pallas_call(
        functools.partial(score_kernel, total_count),
        out_shape=jax.ShapeDtypeStruct((shard_count, parts, per_query, LANES), F32),
        grid=(steps,),
        in_specs=[
            pl.BlockSpec(memory_space=pltpu.SMEM),
            pl.BlockSpec((K_OUT, 2 * K_IN), lambda step: (0, 0)),
            pl.BlockSpec((K_OUT, CHUNK * K_IN), lambda step: (0, step)),
            pl.BlockSpec((examples, width), lambda step: (0, 0)),
        ],
        out_specs=pl.BlockSpec((shard_count, parts, per_query, LANES), lambda step: (0, 0, 0, 0)),
        scratch_shapes=[
            pltpu.VMEM((K_OUT, 3 * K_OUT), BF16),
            pltpu.VMEM((2 * LANES, 2 * LANES), BF16),
            pltpu.VMEM((CHUNK // 2 * K_OUT, LANES), F32),
            pltpu.VMEM((CHUNK, width), BF16),
        ],
        compiler_params=pltpu.CompilerParams(vmem_limit_bytes=VMEM_LIMIT),
        cost_estimate=pl.CostEstimate(
            flops=2 * shard_count * per_query * width * (examples + 128), bytes_accessed=2 * examples * width, transcendentals=0
        ),
        name="solve_and_score",
    )(route, cov, turned, train)


def pick_kernel(listed_ref, received_ref, out_ref):
    for r in range(out_ref.shape[0]):
        shard = listed_ref[0, r]
        total = received_ref[shard, 0]
        for layer in range(1, received_ref.shape[1]):
            total = total + received_ref[shard, layer]
        out_ref[r] = total


def picked(listed, received):
    return pl.pallas_call(
        pick_kernel,
        out_shape=jax.ShapeDtypeStruct((listed.shape[1],) + received.shape[2:], F32),
        in_specs=[pl.BlockSpec(memory_space=pltpu.SMEM), pl.BlockSpec(memory_space=pltpu.VMEM)],
        out_specs=pl.BlockSpec(memory_space=pltpu.VMEM),
        compiler_params=pltpu.CompilerParams(vmem_limit_bytes=VMEM_LIMIT),
        name="pick_tiles",
    )(listed, received)


def exchange(values, distance, count):
    return lax.ppermute(values, "dp", [(k, k ^ distance) for k in range(count)])


def shards(train_grads, query_grads, listed):
    shard_count = lax.axis_size("dp")
    layers = lax.axis_size("layer")
    own_index = lax.axis_index("dp").astype(jnp.int32)
    examples = train_grads.shape[0]
    per_query = query_grads.shape[0]
    train = train_grads.reshape(examples, train_grads.shape[2])
    own_queries = query_grads.reshape(per_query, query_grads.shape[2])
    total_count = float(examples * shard_count)
    order = jnp.arange(shard_count, dtype=jnp.int32)
    if shard_count <= 8:
        queries = [own_queries] + [exchange(own_queries, d, shard_count) for d in range(1, shard_count)]
        cov = covariance_sums(train)
        distance = 1
        while distance < shard_count:
            cov = cov + exchange(cov, distance, shard_count)
            distance = 2 * distance
        route = own_index ^ order
    else:
        queries = [lax.all_gather(own_queries, "dp", axis=0, tiled=True)]
        cov = lax.psum(covariance_sums(train), "dp")
        route = order
    turned = turned_queries(queries)
    scores = all_scores(route, cov, turned, train, per_query, total_count)
    outgoing = scores.reshape(shard_count * layers, per_query, examples // layers)
    received = lax.all_to_all(outgoing, ("dp", "layer"), split_axis=0, concat_axis=0, tiled=True)
    received = received.reshape(shard_count, layers, per_query, examples // layers)
    return picked(listed, received)


def solution(mesh):
    in_specs = (
        P(("groups", "dp"), "layer", None),
        P(("groups", "dp"), "layer", None),
        P(("groups", "dp"), None),
    )
    out_specs = P(("groups", "dp"), None, "layer")
    return jax.shard_map(shards, mesh=mesh, in_specs=in_specs, out_specs=out_specs, check_vma=False)
```

```python
import functools
import jax
import jax.numpy as jnp
from jax import lax
from jax.experimental import pallas as pl
from jax.experimental.pallas import tpu as pltpu
from jax.sharding import PartitionSpec as P

K_OUT = 64
K_IN = 64
LANES = 128
CHUNK = 64
PIVOT = 4
F32 = jnp.float32
BF16 = jnp.bfloat16
VMEM_LIMIT = 48 * 1024 * 1024

NT = (((1,), (1,)), ((), ()))


def low_half(rows):
    return lax.broadcasted_iota(jnp.int32, (rows, LANES), 1) < LANES // 2


def swap_pair(first, second):
    low = low_half(first.shape[0])
    even = jnp.where(low, first, pltpu.roll(second, LANES // 2, 1))
    odd = jnp.where(low, pltpu.roll(first, LANES // 2, 1), second)
    return even, odd


def split(values, terms):
    parts = []
    for _ in range(terms):
        part = values.astype(BF16)
        parts.append(part)
        values = values - part.astype(F32)
    return parts


def stage_kernel(train_ref, in_ref, rows_ref, held, by_in, arrived):
    examples, width = train_ref.shape
    pair = 2 * LANES
    chunks, _, chunk = held.shape
    copies = []
    for g in range(chunks):
        source = train_ref.at[:, pl.ds(g * chunk, chunk)]
        copies.append(pltpu.make_async_copy(source, held.at[g], arrived.at[g]))
        copies[-1].start()
    for m in range(width // pair):
        if m * pair % chunk == 0:
            copies[m * pair // chunk].wait()
        begin = m * pair % chunk
        block = held[m * pair // chunk, :, begin:begin + pair].astype(F32).T
        for k in range(4):
            start = (4 * m + k) * examples
            by_in[:, start:start + examples] = block[k * K_IN:(k + 1) * K_IN, :].astype(BF16)
        for half in range(2):
            for j in range(K_IN // 8):
                first = half * K_IN + j * 8
                both = jnp.concatenate([block[first:first + 8, :], block[first + LANES:first + LANES + 8, :]], axis=0)
                at = half * K_OUT // 2 * 8 + m * 16
                rows_ref[at:at + 16, j * examples:(j + 1) * examples] = both.astype(BF16)
    in_ref[...] = lax.dot_general(by_in[...], by_in[...], NT, preferred_element_type=F32)


def gram_kernel(in_ref, rows_ref, cov_ref):
    count = rows_ref.shape[0]
    every = lax.dot_general(rows_ref[...], rows_ref[...], NT, preferred_element_type=F32)
    row = lax.broadcasted_iota(jnp.int32, (count, count), 0)
    lane = lax.broadcasted_iota(jnp.int32, (count, count), 1)
    every = jnp.where((row & 7) == (lane & 7), every, 0.0)
    summed = jnp.sum(every.reshape(count // 8, 8, count), axis=1)
    lane = lax.broadcasted_iota(jnp.int32, (count, count // 8), 0)
    column = lax.broadcasted_iota(jnp.int32, (count, count // 8), 1)
    merge = jnp.where(lane // 8 == column, 1.0, 0.0).astype(BF16)
    out_sum = sum(jnp.dot(part, merge, preferred_element_type=F32) for part in reversed(split(summed, 3)))
    cov_ref[...] = jnp.concatenate([in_ref[...], out_sum], axis=1)


def staged_rows(train):
    examples, width = train.shape
    chunks = 8 if width % (8 * 2 * LANES) == 0 else 1
    return pl.pallas_call(
        stage_kernel,
        out_shape=(
            jax.ShapeDtypeStruct((K_IN, K_IN), F32),
            jax.ShapeDtypeStruct((8 * K_OUT, K_IN // 8 * examples), BF16),
        ),
        in_specs=[pl.BlockSpec(memory_space=pltpu.HBM)],
        out_specs=(pl.BlockSpec(memory_space=pltpu.VMEM), pl.BlockSpec(memory_space=pltpu.VMEM)),
        scratch_shapes=[
            pltpu.VMEM((chunks, examples, width // chunks), BF16),
            pltpu.VMEM((K_IN, K_OUT * examples), BF16),
            pltpu.SemaphoreType.DMA((chunks,)),
        ],
        compiler_params=pltpu.CompilerParams(vmem_limit_bytes=VMEM_LIMIT),
        cost_estimate=pl.CostEstimate(flops=32 * examples * 64**3, bytes_accessed=2 * examples * width, transcendentals=0),
        name="stage_rows",
    )(train)


def covariance_sums(in_sum, rows):
    return pl.pallas_call(
        gram_kernel,
        out_shape=jax.ShapeDtypeStruct((K_OUT, 2 * K_IN), F32),
        in_specs=[pl.BlockSpec(memory_space=pltpu.VMEM), pl.BlockSpec(memory_space=pltpu.VMEM)],
        out_specs=pl.BlockSpec(memory_space=pltpu.VMEM),
        compiler_params=pltpu.CompilerParams(vmem_limit_bytes=VMEM_LIMIT),
        cost_estimate=pl.CostEstimate(flops=2 * rows.shape[0] * rows.size, bytes_accessed=2 * rows.size, transcendentals=0),
        name="covariance",
    )(in_sum, rows)


def turn_kernel(*refs):
    query_refs, out_ref, spread = refs[:-2], refs[-2], refs[-1]
    blocks = out_ref.shape[0] // 2
    half = CHUNK // 2
    for c in range(blocks):
        at = c * CHUNK
        for ref in query_refs:
            count = ref.shape[0]
            spread[at:at + count, :] = ref[:, c * LANES:(c + 1) * LANES].astype(F32)
            at = at + count
    for p in range(half):
        first = spread[pl.ds(p, blocks, stride=CHUNK), :]
        second = spread[pl.ds(p + half, blocks, stride=CHUNK), :]
        even, odd = swap_pair(first, second)
        out_ref[:blocks, p * LANES:(p + 1) * LANES] = even.astype(BF16)
        out_ref[blocks:, p * LANES:(p + 1) * LANES] = odd.astype(BF16)


def turned_queries(queries):
    width = queries[0].shape[1]
    total = sum(part.shape[0] for part in queries)
    steps = total // CHUNK
    if steps == 1:
        in_specs = [pl.BlockSpec(part.shape, lambda step: (0, 0)) for part in queries]
    else:
        in_specs = [pl.BlockSpec((CHUNK, width), lambda step: (step, 0))]
    return pl.pallas_call(
        turn_kernel,
        out_shape=jax.ShapeDtypeStruct((K_OUT, total * K_IN), BF16),
        grid=(steps,),
        in_specs=in_specs,
        out_specs=pl.BlockSpec((K_OUT, CHUNK * K_IN), lambda step: (0, step)),
        scratch_shapes=[pltpu.VMEM((width // LANES * CHUNK, LANES), F32)],
        compiler_params=pltpu.CompilerParams(vmem_limit_bytes=VMEM_LIMIT),
        cost_estimate=pl.CostEstimate(flops=total * width, bytes_accessed=4 * total * width, transcendentals=0),
        name="turn_queries",
    )(*queries)


def damped(cov, total_count):
    rows = lax.broadcasted_iota(jnp.int32, (K_OUT, LANES), 0)
    lanes = lax.broadcasted_iota(jnp.int32, (K_OUT, LANES), 1)
    low = lanes < K_IN
    diagonal = rows == jnp.where(low, lanes, lanes - K_IN)
    cov = cov * (1.0 / total_count)
    on_diagonal = jnp.sum(jnp.where(diagonal, cov, 0.0), axis=0, keepdims=True)
    low_row = low_half(1)
    in_mean = jnp.sum(jnp.where(low_row, on_diagonal, 0.0), axis=1, keepdims=True) / K_IN
    out_mean = jnp.sum(jnp.where(low_row, 0.0, on_diagonal), axis=1, keepdims=True) / K_OUT
    scale = jnp.where(low_row, 1.0 / in_mean, 1.0)
    added = jnp.where(low_row, 0.1, 0.1 * out_mean)
    return cov * scale + jnp.where(diagonal, added, 0.0)


def inverses(matrix):
    size = matrix.shape[0]
    lanes = lax.broadcasted_iota(jnp.int32, (size, LANES), 1)
    offset = jnp.where(lanes < size, 0, size)
    rows = lax.broadcasted_iota(jnp.int32, (size, LANES), 0)
    row_lanes = lax.broadcasted_iota(jnp.int32, (8, LANES), 1)
    row_place = jnp.where(row_lanes < size, row_lanes, row_lanes - size)
    place = lanes - offset

    def spread_row(values, row):
        return jnp.broadcast_to(values[row:row + 1, :], (8, LANES))

    for begin in range(0, size, PIVOT):
        columns = [jnp.take_along_axis(matrix, offset + begin + a, axis=1) for a in range(PIVOT)]
        p = [[spread_row(columns[b], begin + a) for b in range(PIVOT)] for a in range(PIVOT)]
        r = []
        for a in range(PIVOT):
            row = spread_row(matrix, begin + a)
            inside = (row_place >= begin) & (row_place < begin + PIVOT)
            unit = jnp.where(row_place == begin + a, 1.0, 0.0)
            r.append(jnp.where(inside, unit, row))
        det = 1.0 / (p[0][0] * p[1][1] - p[0][1] * p[1][0])
        e = [[p[1][1] * det, -p[0][1] * det], [-p[1][0] * det, p[0][0] * det]]
        u = [[e[a][0] * p[0][b] + e[a][1] * p[1][b] for b in (2, 3)] for a in (0, 1)]
        s = [[p[a][b + 2] - (p[a][0] * u[0][b] + p[a][1] * u[1][b]) for b in (0, 1)] for a in (2, 3)]
        det = 1.0 / (s[0][0] * s[1][1] - s[0][1] * s[1][0])
        f = [[s[1][1] * det, -s[0][1] * det], [-s[1][0] * det, s[0][0] * det]]
        w = [e[a][0] * r[0] + e[a][1] * r[1] for a in (0, 1)]
        t = [r[a] - (p[a][0] * w[0] + p[a][1] * w[1]) for a in (2, 3)]
        last = [f[a][0] * t[0] + f[a][1] * t[1] for a in (0, 1)]
        first = [w[a] - (u[a][0] * last[0] + u[a][1] * last[1]) for a in (0, 1)]
        solved = first + last
        inside = (place >= begin) & (place < begin + PIVOT)
        rest = jnp.where(inside, 0.0, matrix)
        tall = [jnp.concatenate([row] * (size // 8), axis=0) for row in solved]
        for a in range(PIVOT):
            rest = rest - columns[a] * tall[a]
        for a in range(PIVOT):
            rest = jnp.where(rows == begin + a, tall[a], rest)
        matrix = rest
    return matrix


def score_kernel(total_count, route_ref, cov_ref, turned_ref, train_ref, out_ref, left, right, solved, ready):
    blocks = K_OUT // 2
    half = CHUNK // 2
    step = pl.program_id(0)

    @pl.when(step == 0)
    def _():
        inverse = inverses(damped(cov_ref[...], total_count))
        turned = pltpu.roll(inverse, LANES // 2, 1)
        low = low_half(K_OUT)
        left[...] = jnp.concatenate(split(turned[:, :K_OUT], 3), axis=1)
        double = jnp.concatenate([jnp.where(low, inverse, 0.0), jnp.where(low, 0.0, turned)], axis=0)
        high, small = split(double, 2)
        right[:LANES, :LANES] = high
        right[:LANES, LANES:] = small
        right[LANES:, :LANES] = high
        right[LANES:, LANES:] = jnp.zeros_like(small)

    group = 4
    for g in range(half // group):
        block = turned_ref[:, g * group * LANES:(g + 1) * group * LANES]
        tall = jnp.concatenate([block, block, block], axis=0)
        once = jnp.dot(left[...], tall, preferred_element_type=F32)
        once = jnp.concatenate([once[:, k * LANES:(k + 1) * LANES] for k in range(group)], axis=0)
        wide = jnp.concatenate(split(once, 2), axis=1)
        twice = jnp.dot(wide, right[...], preferred_element_type=F32)
        solved[g * group * K_OUT:(g + 1) * group * K_OUT, :] = twice[:, :LANES] + twice[:, LANES:]
    for c in range(blocks):
        first = solved[pl.ds(c, half, stride=K_OUT), :]
        second = solved[pl.ds(c + blocks, half, stride=K_OUT), :]
        even, odd = swap_pair(first, second)
        ready[:half, c * LANES:(c + 1) * LANES] = even.astype(BF16)
        ready[half:, c * LANES:(c + 1) * LANES] = odd.astype(BF16)
    scores = lax.dot_general(ready[...], train_ref[...], NT, preferred_element_type=F32)
    per_query = out_ref.shape[2]
    parts = out_ref.shape[1]
    for s in range(CHUNK // per_query):
        owner = route_ref[step * (CHUNK // per_query) + s]
        for part in range(parts):
            piece = scores[s * per_query:(s + 1) * per_query, part * LANES:(part + 1) * LANES]
            out_ref[owner, part, :, :] = piece


def all_scores(route, cov, turned, train, per_query, total_count):
    shard_count = route.shape[0]
    examples, width = train.shape
    steps = shard_count * per_query // CHUNK
    parts = examples // LANES
    return pl.pallas_call(
        functools.partial(score_kernel, total_count),
        out_shape=jax.ShapeDtypeStruct((shard_count, parts, per_query, LANES), F32),
        grid=(steps,),
        in_specs=[
            pl.BlockSpec(memory_space=pltpu.SMEM),
            pl.BlockSpec((K_OUT, 2 * K_IN), lambda step: (0, 0)),
            pl.BlockSpec((K_OUT, CHUNK * K_IN), lambda step: (0, step)),
            pl.BlockSpec((examples, width), lambda step: (0, 0)),
        ],
        out_specs=pl.BlockSpec((shard_count, parts, per_query, LANES), lambda step: (0, 0, 0, 0)),
        scratch_shapes=[
            pltpu.VMEM((K_OUT, 3 * K_OUT), BF16),
            pltpu.VMEM((2 * LANES, 2 * LANES), BF16),
            pltpu.VMEM((CHUNK // 2 * K_OUT, LANES), F32),
            pltpu.VMEM((CHUNK, width), BF16),
        ],
        compiler_params=pltpu.CompilerParams(vmem_limit_bytes=VMEM_LIMIT),
        cost_estimate=pl.CostEstimate(
            flops=2 * shard_count * per_query * width * (examples + 128), bytes_accessed=2 * examples * width, transcendentals=0
        ),
        name="solve_and_score",
    )(route, cov, turned, train)


def pick_kernel(listed_ref, received_ref, out_ref):
    for r in range(out_ref.shape[0]):
        shard = listed_ref[0, r]
        total = received_ref[shard, 0]
        for layer in range(1, received_ref.shape[1]):
            total = total + received_ref[shard, layer]
        out_ref[r] = total


def picked(listed, received):
    return pl.pallas_call(
        pick_kernel,
        out_shape=jax.ShapeDtypeStruct((listed.shape[1],) + received.shape[2:], F32),
        in_specs=[pl.BlockSpec(memory_space=pltpu.SMEM), pl.BlockSpec(memory_space=pltpu.VMEM)],
        out_specs=pl.BlockSpec(memory_space=pltpu.VMEM),
        compiler_params=pltpu.CompilerParams(vmem_limit_bytes=VMEM_LIMIT),
        name="pick_tiles",
    )(listed, received)


def exchange(values, distance, count):
    return lax.ppermute(values, "dp", [(k, k ^ distance) for k in range(count)])


def shards(train_grads, query_grads, listed):
    shard_count = lax.axis_size("dp")
    layers = lax.axis_size("layer")
    own_index = lax.axis_index("dp").astype(jnp.int32)
    examples = train_grads.shape[0]
    per_query = query_grads.shape[0]
    train = train_grads.reshape(examples, train_grads.shape[2])
    own_queries = query_grads.reshape(per_query, query_grads.shape[2])
    total_count = float(examples * shard_count)
    order = jnp.arange(shard_count, dtype=jnp.int32)
    if shard_count == 8:
        queries = {0: own_queries}
        queries[4] = exchange(queries[0], 4, shard_count)
        queries[1] = exchange(queries[0], 1, shard_count)
        in_sum, rows = staged_rows(train)
        queries[4], queries[1], in_sum = lax.optimization_barrier((queries[4], queries[1], in_sum))
        queries[2] = exchange(queries[0], 2, shard_count)
        queries[6] = exchange(queries[4], 2, shard_count)
        queries[5] = exchange(queries[4], 1, shard_count)
        cov = covariance_sums(in_sum, rows)
        queries[2], queries[6], cov = lax.optimization_barrier((queries[2], queries[6], cov))
        queries[3] = exchange(queries[2], 1, shard_count)
        queries[7] = exchange(queries[6], 1, shard_count)
        for distance in (4, 2, 1):
            cov = cov + exchange(cov, distance, shard_count)
        queries = [queries[d] for d in range(shard_count)]
        route = own_index ^ order
    else:
        queries = [lax.all_gather(own_queries, "dp", axis=0, tiled=True)]
        cov = lax.psum(covariance_sums(*staged_rows(train)), "dp")
        route = order
    turned = turned_queries(queries)
    scores = all_scores(route, cov, turned, train, per_query, total_count)
    outgoing = scores.reshape(shard_count * layers, per_query, examples // layers)
    received = lax.all_to_all(outgoing, ("dp", "layer"), split_axis=0, concat_axis=0, tiled=True)
    received = received.reshape(shard_count, layers, per_query, examples // layers)
    return picked(listed, received)


def solution(mesh):
    in_specs = (
        P(("groups", "dp"), "layer", None),
        P(("groups", "dp"), "layer", None),
        P(("groups", "dp"), None),
    )
    out_specs = P(("groups", "dp"), None, "layer")
    return jax.shard_map(shards, mesh=mesh, in_specs=in_specs, out_specs=out_specs, check_vma=False)
```

```python
import functools
import jax
import jax.numpy as jnp
from jax import lax
from jax.experimental import pallas as pl
from jax.experimental.pallas import tpu as pltpu
from jax.sharding import PartitionSpec as P

K_OUT = 64
K_IN = 64
LANES = 128
CHUNK = 64
PIVOT = 4
F32 = jnp.float32
BF16 = jnp.bfloat16
VMEM_LIMIT = 48 * 1024 * 1024
STAGE_VMEM_LIMIT = 50 * 1024 * 1024

NT = (((1,), (1,)), ((), ()))


def low_half(rows):
    return lax.broadcasted_iota(jnp.int32, (rows, LANES), 1) < LANES // 2


def swap_pair(first, second):
    low = low_half(first.shape[0])
    even = jnp.where(low, first, pltpu.roll(second, LANES // 2, 1))
    odd = jnp.where(low, pltpu.roll(first, LANES // 2, 1), second)
    return even, odd


def split(values, terms):
    parts = []
    for _ in range(terms):
        part = values.astype(BF16)
        parts.append(part)
        values = values - part.astype(F32)
    return parts


def stage_kernel(train_ref, in_ref, rows_ref, held, by_in, arrived):
    examples, width = train_ref.shape
    pair = 2 * LANES
    chunks, _, chunk = held.shape
    copies = []
    for g in range(chunks):
        source = train_ref.at[:, pl.ds(g * chunk, chunk)]
        copies.append(pltpu.make_async_copy(source, held.at[g], arrived.at[g]))
        copies[-1].start()
    for m in range(width // pair):
        if m * pair % chunk == 0:
            copies[m * pair // chunk].wait()
        begin = m * pair % chunk
        block = held[m * pair // chunk, :, begin:begin + pair].astype(F32).T
        for k in range(4):
            start = (4 * m + k) * examples
            by_in[:, start:start + examples] = block[k * K_IN:(k + 1) * K_IN, :].astype(BF16)
        for half in range(2):
            for j in range(K_IN // 8):
                first = half * K_IN + j * 8
                both = jnp.concatenate([block[first:first + 8, :], block[first + LANES:first + LANES + 8, :]], axis=0)
                at = half * K_OUT // 2 * 8 + m * 16
                rows_ref[at:at + 16, j * examples:(j + 1) * examples] = both.astype(BF16)
    in_ref[...] = lax.dot_general(by_in[...], by_in[...], NT, preferred_element_type=F32)


def gram_kernel(in_ref, rows_ref, cov_ref):
    count = rows_ref.shape[0]
    every = lax.dot_general(rows_ref[...], rows_ref[...], NT, preferred_element_type=F32)
    row = lax.broadcasted_iota(jnp.int32, (count, count), 0)
    lane = lax.broadcasted_iota(jnp.int32, (count, count), 1)
    every = jnp.where((row & 7) == (lane & 7), every, 0.0)
    summed = jnp.sum(every.reshape(count // 8, 8, count), axis=1)
    lane = lax.broadcasted_iota(jnp.int32, (count, count // 8), 0)
    column = lax.broadcasted_iota(jnp.int32, (count, count // 8), 1)
    merge = jnp.where(lane // 8 == column, 1.0, 0.0).astype(BF16)
    out_sum = sum(jnp.dot(part, merge, preferred_element_type=F32) for part in reversed(split(summed, 3)))
    cov_ref[...] = jnp.concatenate([in_ref[...], out_sum], axis=1)


def staged_rows(train):
    examples, width = train.shape
    chunks = 8 if width % (8 * 2 * LANES) == 0 else 1
    return pl.pallas_call(
        stage_kernel,
        out_shape=(
            jax.ShapeDtypeStruct((K_IN, K_IN), F32),
            jax.ShapeDtypeStruct((8 * K_OUT, K_IN // 8 * examples), BF16),
        ),
        in_specs=[pl.BlockSpec(memory_space=pltpu.HBM)],
        out_specs=(pl.BlockSpec(memory_space=pltpu.VMEM), pl.BlockSpec(memory_space=pltpu.VMEM)),
        scratch_shapes=[
            pltpu.VMEM((chunks, examples, width // chunks), BF16),
            pltpu.VMEM((K_IN, K_OUT * examples), BF16),
            pltpu.SemaphoreType.DMA((chunks,)),
        ],
        compiler_params=pltpu.CompilerParams(vmem_limit_bytes=STAGE_VMEM_LIMIT),
        cost_estimate=pl.CostEstimate(flops=32 * examples * 64**3, bytes_accessed=2 * examples * width, transcendentals=0),
        name="stage_rows",
    )(train)


def covariance_sums(in_sum, rows):
    return pl.pallas_call(
        gram_kernel,
        out_shape=jax.ShapeDtypeStruct((K_OUT, 2 * K_IN), F32),
        in_specs=[pl.BlockSpec(memory_space=pltpu.VMEM), pl.BlockSpec(memory_space=pltpu.VMEM)],
        out_specs=pl.BlockSpec(memory_space=pltpu.VMEM),
        compiler_params=pltpu.CompilerParams(vmem_limit_bytes=VMEM_LIMIT),
        cost_estimate=pl.CostEstimate(flops=2 * rows.shape[0] * rows.size, bytes_accessed=2 * rows.size, transcendentals=0),
        name="covariance",
    )(in_sum, rows)


def turn_kernel(*refs):
    query_refs, out_ref, spread = refs[:-2], refs[-2], refs[-1]
    blocks = out_ref.shape[0] // 2
    half = CHUNK // 2
    for c in range(blocks):
        at = c * CHUNK
        for ref in query_refs:
            count = ref.shape[0]
            spread[at:at + count, :] = ref[:, c * LANES:(c + 1) * LANES].astype(F32)
            at = at + count
    for p in range(half):
        first = spread[pl.ds(p, blocks, stride=CHUNK), :]
        second = spread[pl.ds(p + half, blocks, stride=CHUNK), :]
        even, odd = swap_pair(first, second)
        out_ref[:blocks, p * LANES:(p + 1) * LANES] = even.astype(BF16)
        out_ref[blocks:, p * LANES:(p + 1) * LANES] = odd.astype(BF16)


def turned_queries(queries):
    width = queries[0].shape[1]
    total = sum(part.shape[0] for part in queries)
    steps = total // CHUNK
    if steps == 1:
        in_specs = [pl.BlockSpec(part.shape, lambda step: (0, 0)) for part in queries]
    else:
        in_specs = [pl.BlockSpec((CHUNK, width), lambda step: (step, 0))]
    return pl.pallas_call(
        turn_kernel,
        out_shape=jax.ShapeDtypeStruct((K_OUT, total * K_IN), BF16),
        grid=(steps,),
        in_specs=in_specs,
        out_specs=pl.BlockSpec((K_OUT, CHUNK * K_IN), lambda step: (0, step)),
        scratch_shapes=[pltpu.VMEM((width // LANES * CHUNK, LANES), F32)],
        compiler_params=pltpu.CompilerParams(vmem_limit_bytes=VMEM_LIMIT),
        cost_estimate=pl.CostEstimate(flops=4096 * total * width, bytes_accessed=4 * total * width, transcendentals=0),
        name="turn_queries",
    )(*queries)


def damped(cov, total_count):
    rows = lax.broadcasted_iota(jnp.int32, (K_OUT, LANES), 0)
    lanes = lax.broadcasted_iota(jnp.int32, (K_OUT, LANES), 1)
    low = lanes < K_IN
    diagonal = rows == jnp.where(low, lanes, lanes - K_IN)
    cov = cov * (1.0 / total_count)
    on_diagonal = jnp.sum(jnp.where(diagonal, cov, 0.0), axis=0, keepdims=True)
    low_row = low_half(1)
    in_mean = jnp.sum(jnp.where(low_row, on_diagonal, 0.0), axis=1, keepdims=True) / K_IN
    out_mean = jnp.sum(jnp.where(low_row, 0.0, on_diagonal), axis=1, keepdims=True) / K_OUT
    scale = jnp.where(low_row, 1.0 / in_mean, 1.0)
    added = jnp.where(low_row, 0.1, 0.1 * out_mean)
    return cov * scale + jnp.where(diagonal, added, 0.0)


def inverses(matrix):
    size = matrix.shape[0]
    lanes = lax.broadcasted_iota(jnp.int32, (size, LANES), 1)
    offset = jnp.where(lanes < size, 0, size)
    rows = lax.broadcasted_iota(jnp.int32, (size, LANES), 0)
    row_lanes = lax.broadcasted_iota(jnp.int32, (8, LANES), 1)
    row_place = jnp.where(row_lanes < size, row_lanes, row_lanes - size)
    place = lanes - offset

    def spread_row(values, row):
        return jnp.broadcast_to(values[row:row + 1, :], (8, LANES))

    for begin in range(0, size, PIVOT):
        columns = [jnp.take_along_axis(matrix, offset + begin + a, axis=1) for a in range(PIVOT)]
        p = [[spread_row(columns[b], begin + a) for b in range(PIVOT)] for a in range(PIVOT)]
        r = []
        for a in range(PIVOT):
            row = spread_row(matrix, begin + a)
            inside = (row_place >= begin) & (row_place < begin + PIVOT)
            unit = jnp.where(row_place == begin + a, 1.0, 0.0)
            r.append(jnp.where(inside, unit, row))
        det = 1.0 / (p[0][0] * p[1][1] - p[0][1] * p[1][0])
        e = [[p[1][1] * det, -p[0][1] * det], [-p[1][0] * det, p[0][0] * det]]
        u = [[e[a][0] * p[0][b] + e[a][1] * p[1][b] for b in (2, 3)] for a in (0, 1)]
        s = [[p[a][b + 2] - (p[a][0] * u[0][b] + p[a][1] * u[1][b]) for b in (0, 1)] for a in (2, 3)]
        det = 1.0 / (s[0][0] * s[1][1] - s[0][1] * s[1][0])
        f = [[s[1][1] * det, -s[0][1] * det], [-s[1][0] * det, s[0][0] * det]]
        w = [e[a][0] * r[0] + e[a][1] * r[1] for a in (0, 1)]
        t = [r[a] - (p[a][0] * w[0] + p[a][1] * w[1]) for a in (2, 3)]
        last = [f[a][0] * t[0] + f[a][1] * t[1] for a in (0, 1)]
        first = [w[a] - (u[a][0] * last[0] + u[a][1] * last[1]) for a in (0, 1)]
        solved = first + last
        inside = (place >= begin) & (place < begin + PIVOT)
        rest = jnp.where(inside, 0.0, matrix)
        tall = [jnp.concatenate([row] * (size // 8), axis=0) for row in solved]
        for a in range(PIVOT):
            rest = rest - columns[a] * tall[a]
        for a in range(PIVOT):
            rest = jnp.where(rows == begin + a, tall[a], rest)
        matrix = rest
    return matrix


def score_kernel(total_count, route_ref, cov_ref, turned_ref, train_ref, out_ref, left, right, solved, ready):
    blocks = K_OUT // 2
    half = CHUNK // 2
    step = pl.program_id(0)

    @pl.when(step == 0)
    def _():
        inverse = inverses(damped(cov_ref[...], total_count))
        turned = pltpu.roll(inverse, LANES // 2, 1)
        low = low_half(K_OUT)
        left[...] = jnp.concatenate(split(turned[:, :K_OUT], 3), axis=1)
        double = jnp.concatenate([jnp.where(low, inverse, 0.0), jnp.where(low, 0.0, turned)], axis=0)
        high, small = split(double, 2)
        right[:LANES, :LANES] = high
        right[:LANES, LANES:] = small
        right[LANES:, :LANES] = high
        right[LANES:, LANES:] = jnp.zeros_like(small)

    group = 4
    for g in range(half // group):
        block = turned_ref[:, g * group * LANES:(g + 1) * group * LANES]
        tall = jnp.concatenate([block, block, block], axis=0)
        once = jnp.dot(left[...], tall, preferred_element_type=F32)
        once = jnp.concatenate([once[:, k * LANES:(k + 1) * LANES] for k in range(group)], axis=0)
        wide = jnp.concatenate(split(once, 2), axis=1)
        twice = jnp.dot(wide, right[...], preferred_element_type=F32)
        solved[g * group * K_OUT:(g + 1) * group * K_OUT, :] = twice[:, :LANES] + twice[:, LANES:]
    for c in range(blocks):
        first = solved[pl.ds(c, half, stride=K_OUT), :]
        second = solved[pl.ds(c + blocks, half, stride=K_OUT), :]
        even, odd = swap_pair(first, second)
        ready[:half, c * LANES:(c + 1) * LANES] = even.astype(BF16)
        ready[half:, c * LANES:(c + 1) * LANES] = odd.astype(BF16)
    scores = lax.dot_general(ready[...], train_ref[...], NT, preferred_element_type=F32)
    per_query = out_ref.shape[2]
    parts = out_ref.shape[1]
    for s in range(CHUNK // per_query):
        owner = route_ref[step * (CHUNK // per_query) + s]
        for part in range(parts):
            piece = scores[s * per_query:(s + 1) * per_query, part * LANES:(part + 1) * LANES]
            out_ref[owner, part, :, :] = piece


def all_scores(route, cov, turned, train, per_query, total_count):
    shard_count = route.shape[0]
    examples, width = train.shape
    steps = shard_count * per_query // CHUNK
    parts = examples // LANES
    return pl.pallas_call(
        functools.partial(score_kernel, total_count),
        out_shape=jax.ShapeDtypeStruct((shard_count, parts, per_query, LANES), F32),
        grid=(steps,),
        in_specs=[
            pl.BlockSpec(memory_space=pltpu.SMEM),
            pl.BlockSpec((K_OUT, 2 * K_IN), lambda step: (0, 0)),
            pl.BlockSpec((K_OUT, CHUNK * K_IN), lambda step: (0, step)),
            pl.BlockSpec((examples, width), lambda step: (0, 0)),
        ],
        out_specs=pl.BlockSpec((shard_count, parts, per_query, LANES), lambda step: (0, 0, 0, 0)),
        scratch_shapes=[
            pltpu.VMEM((K_OUT, 3 * K_OUT), BF16),
            pltpu.VMEM((2 * LANES, 2 * LANES), BF16),
            pltpu.VMEM((CHUNK // 2 * K_OUT, LANES), F32),
            pltpu.VMEM((CHUNK, width), BF16),
        ],
        compiler_params=pltpu.CompilerParams(vmem_limit_bytes=VMEM_LIMIT),
        cost_estimate=pl.CostEstimate(
            flops=2 * shard_count * per_query * width * (examples + 128), bytes_accessed=2 * examples * width, transcendentals=0
        ),
        name="solve_and_score",
    )(route, cov, turned, train)


def pick_kernel(listed_ref, received_ref, out_ref):
    for r in range(out_ref.shape[0]):
        shard = listed_ref[0, r]
        total = received_ref[shard, 0]
        for layer in range(1, received_ref.shape[1]):
            total = total + received_ref[shard, layer]
        out_ref[r] = total


def picked(listed, received):
    return pl.pallas_call(
        pick_kernel,
        out_shape=jax.ShapeDtypeStruct((listed.shape[1],) + received.shape[2:], F32),
        in_specs=[pl.BlockSpec(memory_space=pltpu.SMEM), pl.BlockSpec(memory_space=pltpu.VMEM)],
        out_specs=pl.BlockSpec(memory_space=pltpu.VMEM),
        compiler_params=pltpu.CompilerParams(vmem_limit_bytes=VMEM_LIMIT),
        name="pick_tiles",
    )(listed, received)


def exchange(values, distance, count):
    return lax.ppermute(values, "dp", [(k, k ^ distance) for k in range(count)])


def shards(train_grads, query_grads, listed):
    shard_count = lax.axis_size("dp")
    layers = lax.axis_size("layer")
    own_index = lax.axis_index("dp").astype(jnp.int32)
    examples = train_grads.shape[0]
    per_query = query_grads.shape[0]
    train = train_grads.reshape(examples, train_grads.shape[2])
    own_queries = query_grads.reshape(per_query, query_grads.shape[2])
    total_count = float(examples * shard_count)
    order = jnp.arange(shard_count, dtype=jnp.int32)
    if shard_count == 8:
        quarter = exchange(own_queries, 4, shard_count)
        in_sum, rows = staged_rows(train)
        quarter, in_sum = lax.optimization_barrier((quarter, in_sum))
        column = jnp.concatenate([own_queries, quarter], axis=0)
        other = exchange(column, 2, shard_count)
        cov = covariance_sums(in_sum, rows)
        other, cov = lax.optimization_barrier((other, cov))
        column = jnp.concatenate([column, other], axis=0)
        queries = [column, exchange(column, 1, shard_count)]
        for distance in (1, 4):
            cov = cov + exchange(cov, distance, shard_count)
        last = exchange(cov, 2, shard_count)
        turned, cov = lax.optimization_barrier((turned_queries(queries), cov))
        cov = cov + last
        order = jnp.array([0, 4, 2, 6, 1, 5, 3, 7], jnp.int32)
        route = own_index ^ order
    else:
        turned = turned_queries([lax.all_gather(own_queries, "dp", axis=0, tiled=True)])
        cov = lax.psum(covariance_sums(*staged_rows(train)), "dp")
        route = order
    scores = all_scores(route, cov, turned, train, per_query, total_count)
    outgoing = scores.reshape(shard_count * layers, per_query, examples // layers)
    received = lax.all_to_all(outgoing, ("dp", "layer"), split_axis=0, concat_axis=0, tiled=True)
    received = received.reshape(shard_count, layers, per_query, examples // layers)
    return picked(listed, received)


def solution(mesh):
    in_specs = (
        P(("groups", "dp"), "layer", None),
        P(("groups", "dp"), "layer", None),
        P(("groups", "dp"), None),
    )
    out_specs = P(("groups", "dp"), None, "layer")
    return jax.shard_map(shards, mesh=mesh, in_specs=in_specs, out_specs=out_specs, check_vma=False)
```

```python
import functools
import jax
import jax.numpy as jnp
from jax import lax
from jax.experimental import pallas as pl
from jax.experimental.pallas import tpu as pltpu
from jax.sharding import PartitionSpec as P

K_OUT = 64
K_IN = 64
LANES = 128
CHUNK = 64
PIVOT = 4
F32 = jnp.float32
BF16 = jnp.bfloat16
VMEM_LIMIT = 48 * 1024 * 1024
STAGE_VMEM_LIMIT = 50 * 1024 * 1024

NT = (((1,), (1,)), ((), ()))


def low_half(rows):
    return lax.broadcasted_iota(jnp.int32, (rows, LANES), 1) < LANES // 2


def swap_pair(first, second):
    low = low_half(first.shape[0])
    even = jnp.where(low, first, pltpu.roll(second, LANES // 2, 1))
    odd = jnp.where(low, pltpu.roll(first, LANES // 2, 1), second)
    return even, odd


def split(values, terms):
    parts = []
    for _ in range(terms):
        part = values.astype(BF16)
        parts.append(part)
        values = values - part.astype(F32)
    return parts


def stage_kernel(train_ref, in_ref, rows_ref, held, by_in, arrived):
    examples, width = train_ref.shape
    pair = 2 * LANES
    chunks, _, chunk = held.shape
    copies = []
    for g in range(chunks):
        source = train_ref.at[:, pl.ds(g * chunk, chunk)]
        copies.append(pltpu.make_async_copy(source, held.at[g], arrived.at[g]))
        copies[-1].start()
    for m in range(width // pair):
        if m * pair % chunk == 0:
            copies[m * pair // chunk].wait()
        begin = m * pair % chunk
        block = held[m * pair // chunk, :, begin:begin + pair].astype(F32).T
        for k in range(4):
            start = (4 * m + k) * examples
            by_in[:, start:start + examples] = block[k * K_IN:(k + 1) * K_IN, :].astype(BF16)
        for half in range(2):
            for j in range(K_IN // 8):
                first = half * K_IN + j * 8
                both = jnp.concatenate([block[first:first + 8, :], block[first + LANES:first + LANES + 8, :]], axis=0)
                at = half * K_OUT // 2 * 8 + m * 16
                rows_ref[at:at + 16, j * examples:(j + 1) * examples] = both.astype(BF16)
    in_ref[...] = lax.dot_general(by_in[...], by_in[...], NT, preferred_element_type=F32)


def gram_kernel(in_ref, rows_ref, cov_ref):
    count = rows_ref.shape[0]
    every = lax.dot_general(rows_ref[...], rows_ref[...], NT, preferred_element_type=F32)
    row = lax.broadcasted_iota(jnp.int32, (count, count), 0)
    lane = lax.broadcasted_iota(jnp.int32, (count, count), 1)
    every = jnp.where((row & 7) == (lane & 7), every, 0.0)
    summed = jnp.sum(every.reshape(count // 8, 8, count), axis=1)
    lane = lax.broadcasted_iota(jnp.int32, (count, count // 8), 0)
    column = lax.broadcasted_iota(jnp.int32, (count, count // 8), 1)
    merge = jnp.where(lane // 8 == column, 1.0, 0.0).astype(BF16)
    out_sum = sum(jnp.dot(part, merge, preferred_element_type=F32) for part in reversed(split(summed, 3)))
    cov_ref[...] = jnp.concatenate([in_ref[...], out_sum], axis=1)


def staged_rows(train):
    examples, width = train.shape
    chunks = 8 if width % (8 * 2 * LANES) == 0 else 1
    return pl.pallas_call(
        stage_kernel,
        out_shape=(
            jax.ShapeDtypeStruct((K_IN, K_IN), F32),
            jax.ShapeDtypeStruct((8 * K_OUT, K_IN // 8 * examples), BF16),
        ),
        in_specs=[pl.BlockSpec(memory_space=pltpu.HBM)],
        out_specs=(pl.BlockSpec(memory_space=pltpu.VMEM), pl.BlockSpec(memory_space=pltpu.VMEM)),
        scratch_shapes=[
            pltpu.VMEM((chunks, examples, width // chunks), BF16),
            pltpu.VMEM((K_IN, K_OUT * examples), BF16),
            pltpu.SemaphoreType.DMA((chunks,)),
        ],
        compiler_params=pltpu.CompilerParams(vmem_limit_bytes=STAGE_VMEM_LIMIT),
        cost_estimate=pl.CostEstimate(flops=32 * examples * 64**3, bytes_accessed=2 * examples * width, transcendentals=0),
        name="stage_rows",
    )(train)


def covariance_sums(in_sum, rows):
    return pl.pallas_call(
        gram_kernel,
        out_shape=jax.ShapeDtypeStruct((K_OUT, 2 * K_IN), F32),
        in_specs=[pl.BlockSpec(memory_space=pltpu.VMEM), pl.BlockSpec(memory_space=pltpu.VMEM)],
        out_specs=pl.BlockSpec(memory_space=pltpu.VMEM),
        compiler_params=pltpu.CompilerParams(vmem_limit_bytes=VMEM_LIMIT),
        cost_estimate=pl.CostEstimate(flops=2 * rows.shape[0] * rows.size, bytes_accessed=2 * rows.size, transcendentals=0),
        name="covariance",
    )(in_sum, rows)


def turn_kernel(*refs):
    query_refs, out_ref, spread = refs[:-2], refs[-2], refs[-1]
    blocks = out_ref.shape[0] // 2
    half = CHUNK // 2
    for c in range(blocks):
        at = c * CHUNK
        for ref in query_refs:
            count = ref.shape[0]
            spread[at:at + count, :] = ref[:, c * LANES:(c + 1) * LANES].astype(F32)
            at = at + count
    for p in range(half):
        first = spread[pl.ds(p, blocks, stride=CHUNK), :]
        second = spread[pl.ds(p + half, blocks, stride=CHUNK), :]
        even, odd = swap_pair(first, second)
        out_ref[:blocks, p * LANES:(p + 1) * LANES] = even.astype(BF16)
        out_ref[blocks:, p * LANES:(p + 1) * LANES] = odd.astype(BF16)


def turned_queries(queries):
    width = queries[0].shape[1]
    total = sum(part.shape[0] for part in queries)
    steps = total // CHUNK
    if steps == 1:
        in_specs = [pl.BlockSpec(part.shape, lambda step: (0, 0)) for part in queries]
    else:
        in_specs = [pl.BlockSpec((CHUNK, width), lambda step: (step, 0))]
    return pl.pallas_call(
        turn_kernel,
        out_shape=jax.ShapeDtypeStruct((K_OUT, total * K_IN), BF16),
        grid=(steps,),
        in_specs=in_specs,
        out_specs=pl.BlockSpec((K_OUT, CHUNK * K_IN), lambda step: (0, step)),
        scratch_shapes=[pltpu.VMEM((width // LANES * CHUNK, LANES), F32)],
        compiler_params=pltpu.CompilerParams(vmem_limit_bytes=VMEM_LIMIT),
        cost_estimate=pl.CostEstimate(flops=4096 * total * width, bytes_accessed=4 * total * width, transcendentals=0),
        name="turn_queries",
    )(*queries)


def damped(cov, total_count):
    rows = lax.broadcasted_iota(jnp.int32, (K_OUT, LANES), 0)
    lanes = lax.broadcasted_iota(jnp.int32, (K_OUT, LANES), 1)
    low = lanes < K_IN
    diagonal = rows == jnp.where(low, lanes, lanes - K_IN)
    cov = cov * (1.0 / total_count)
    on_diagonal = jnp.sum(jnp.where(diagonal, cov, 0.0), axis=0, keepdims=True)
    low_row = low_half(1)
    in_mean = jnp.sum(jnp.where(low_row, on_diagonal, 0.0), axis=1, keepdims=True) / K_IN
    out_mean = jnp.sum(jnp.where(low_row, 0.0, on_diagonal), axis=1, keepdims=True) / K_OUT
    scale = jnp.where(low_row, 1.0 / in_mean, 1.0)
    added = jnp.where(low_row, 0.1, 0.1 * out_mean)
    return cov * scale + jnp.where(diagonal, added, 0.0)


def inverses(matrix):
    size = matrix.shape[0]
    lanes = lax.broadcasted_iota(jnp.int32, (size, LANES), 1)
    offset = jnp.where(lanes < size, 0, size)
    rows = lax.broadcasted_iota(jnp.int32, (size, LANES), 0)
    row_lanes = lax.broadcasted_iota(jnp.int32, (8, LANES), 1)
    row_place = jnp.where(row_lanes < size, row_lanes, row_lanes - size)
    place = lanes - offset

    def spread_row(values, row):
        return jnp.broadcast_to(values[row:row + 1, :], (8, LANES))

    for begin in range(0, size, PIVOT):
        columns = [jnp.take_along_axis(matrix, offset + begin + a, axis=1) for a in range(PIVOT)]
        p = [[spread_row(columns[b], begin + a) for b in range(PIVOT)] for a in range(PIVOT)]
        r = []
        for a in range(PIVOT):
            row = spread_row(matrix, begin + a)
            inside = (row_place >= begin) & (row_place < begin + PIVOT)
            unit = jnp.where(row_place == begin + a, 1.0, 0.0)
            r.append(jnp.where(inside, unit, row))
        det = 1.0 / (p[0][0] * p[1][1] - p[0][1] * p[1][0])
        e = [[p[1][1] * det, -p[0][1] * det], [-p[1][0] * det, p[0][0] * det]]
        u = [[e[a][0] * p[0][b] + e[a][1] * p[1][b] for b in (2, 3)] for a in (0, 1)]
        s = [[p[a][b + 2] - (p[a][0] * u[0][b] + p[a][1] * u[1][b]) for b in (0, 1)] for a in (2, 3)]
        det = 1.0 / (s[0][0] * s[1][1] - s[0][1] * s[1][0])
        f = [[s[1][1] * det, -s[0][1] * det], [-s[1][0] * det, s[0][0] * det]]
        w = [e[a][0] * r[0] + e[a][1] * r[1] for a in (0, 1)]
        t = [r[a] - (p[a][0] * w[0] + p[a][1] * w[1]) for a in (2, 3)]
        last = [f[a][0] * t[0] + f[a][1] * t[1] for a in (0, 1)]
        first = [w[a] - (u[a][0] * last[0] + u[a][1] * last[1]) for a in (0, 1)]
        solved = first + last
        inside = (place >= begin) & (place < begin + PIVOT)
        rest = jnp.where(inside, 0.0, matrix)
        tall = [jnp.concatenate([row] * (size // 8), axis=0) for row in solved]
        for a in range(PIVOT):
            rest = rest - columns[a] * tall[a]
        for a in range(PIVOT):
            rest = jnp.where(rows == begin + a, tall[a], rest)
        matrix = rest
    return matrix


def score_kernel(total_count, route_ref, cov_ref, turned_ref, train_ref, out_ref, left, right, solved, ready):
    blocks = K_OUT // 2
    half = CHUNK // 2
    step = pl.program_id(0)

    @pl.when(step == 0)
    def _():
        inverse = inverses(damped(cov_ref[...], total_count))
        turned = pltpu.roll(inverse, LANES // 2, 1)
        low = low_half(K_OUT)
        left[...] = jnp.concatenate(split(turned[:, :K_OUT], 3), axis=1)
        double = jnp.concatenate([jnp.where(low, inverse, 0.0), jnp.where(low, 0.0, turned)], axis=0)
        high, small = split(double, 2)
        right[:LANES, :LANES] = high
        right[:LANES, LANES:] = small
        right[LANES:, :LANES] = high
        right[LANES:, LANES:] = jnp.zeros_like(small)

    group = 4
    for g in range(half // group):
        block = turned_ref[:, g * group * LANES:(g + 1) * group * LANES]
        tall = jnp.concatenate([block, block, block], axis=0)
        once = jnp.dot(left[...], tall, preferred_element_type=F32)
        once = jnp.concatenate([once[:, k * LANES:(k + 1) * LANES] for k in range(group)], axis=0)
        wide = jnp.concatenate(split(once, 2), axis=1)
        twice = jnp.dot(wide, right[...], preferred_element_type=F32)
        solved[g * group * K_OUT:(g + 1) * group * K_OUT, :] = twice[:, :LANES] + twice[:, LANES:]
    for c in range(blocks):
        first = solved[pl.ds(c, half, stride=K_OUT), :]
        second = solved[pl.ds(c + blocks, half, stride=K_OUT), :]
        even, odd = swap_pair(first, second)
        ready[:half, c * LANES:(c + 1) * LANES] = even.astype(BF16)
        ready[half:, c * LANES:(c + 1) * LANES] = odd.astype(BF16)
    scores = lax.dot_general(ready[...], train_ref[...], NT, preferred_element_type=F32)
    per_query = out_ref.shape[2]
    parts = out_ref.shape[1]
    for s in range(CHUNK // per_query):
        owner = route_ref[step * (CHUNK // per_query) + s]
        for part in range(parts):
            piece = scores[s * per_query:(s + 1) * per_query, part * LANES:(part + 1) * LANES]
            out_ref[owner, part, :, :] = piece


def all_scores(route, cov, turned, train, per_query, total_count):
    shard_count = route.shape[0]
    examples, width = train.shape
    steps = shard_count * per_query // CHUNK
    parts = examples // LANES
    return pl.pallas_call(
        functools.partial(score_kernel, total_count),
        out_shape=jax.ShapeDtypeStruct((shard_count, parts, per_query, LANES), F32),
        grid=(steps,),
        in_specs=[
            pl.BlockSpec(memory_space=pltpu.SMEM),
            pl.BlockSpec((K_OUT, 2 * K_IN), lambda step: (0, 0)),
            pl.BlockSpec((K_OUT, CHUNK * K_IN), lambda step: (0, step)),
            pl.BlockSpec((examples, width), lambda step: (0, 0)),
        ],
        out_specs=pl.BlockSpec((shard_count, parts, per_query, LANES), lambda step: (0, 0, 0, 0)),
        scratch_shapes=[
            pltpu.VMEM((K_OUT, 3 * K_OUT), BF16),
            pltpu.VMEM((2 * LANES, 2 * LANES), BF16),
            pltpu.VMEM((CHUNK // 2 * K_OUT, LANES), F32),
            pltpu.VMEM((CHUNK, width), BF16),
        ],
        compiler_params=pltpu.CompilerParams(vmem_limit_bytes=VMEM_LIMIT),
        cost_estimate=pl.CostEstimate(
            flops=2 * shard_count * per_query * width * (examples + 128), bytes_accessed=2 * examples * width, transcendentals=0
        ),
        name="solve_and_score",
    )(route, cov, turned, train)


def pick_kernel(listed_ref, received_ref, out_ref):
    for r in range(out_ref.shape[0]):
        shard = listed_ref[0, r]
        total = received_ref[shard, 0]
        for layer in range(1, received_ref.shape[1]):
            total = total + received_ref[shard, layer]
        out_ref[r] = total


def picked(listed, received):
    return pl.pallas_call(
        pick_kernel,
        out_shape=jax.ShapeDtypeStruct((listed.shape[1],) + received.shape[2:], F32),
        in_specs=[pl.BlockSpec(memory_space=pltpu.SMEM), pl.BlockSpec(memory_space=pltpu.VMEM)],
        out_specs=pl.BlockSpec(memory_space=pltpu.VMEM),
        compiler_params=pltpu.CompilerParams(vmem_limit_bytes=VMEM_LIMIT),
        name="pick_tiles",
    )(listed, received)


def exchange(values, distance, count):
    return lax.ppermute(values, "dp", [(k, k ^ distance) for k in range(count)])


def shards(train_grads, query_grads, listed):
    shard_count = lax.axis_size("dp")
    layers = lax.axis_size("layer")
    own_index = lax.axis_index("dp").astype(jnp.int32)
    examples = train_grads.shape[0]
    per_query = query_grads.shape[0]
    train = train_grads.reshape(examples, train_grads.shape[2])
    own_queries = query_grads.reshape(per_query, query_grads.shape[2])
    total_count = float(examples * shard_count)
    order = jnp.arange(shard_count, dtype=jnp.int32)
    if shard_count == 8:
        far = exchange(own_queries, 4, shard_count)
        beside = exchange(own_queries, 1, shard_count)
        in_sum, rows = staged_rows(train)
        far, beside, in_sum = lax.optimization_barrier((far, beside, in_sum))
        near = exchange(jnp.concatenate([own_queries, far], axis=0), 2, shard_count)
        far_beside = exchange(far, 1, shard_count)
        cov = covariance_sums(in_sum, rows)
        near, cov = lax.optimization_barrier((near, cov))
        near_beside = exchange(near, 1, shard_count)
        queries = [own_queries, far, near, beside, far_beside, near_beside]
        for distance in (4, 2):
            cov = cov + exchange(cov, distance, shard_count)
        last = exchange(cov, 1, shard_count)
        turned, cov = lax.optimization_barrier((turned_queries(queries), cov))
        cov = cov + last
        order = jnp.array([0, 4, 2, 6, 1, 5, 3, 7], jnp.int32)
        route = own_index ^ order
    else:
        turned = turned_queries([lax.all_gather(own_queries, "dp", axis=0, tiled=True)])
        cov = lax.psum(covariance_sums(*staged_rows(train)), "dp")
        route = order
    scores = all_scores(route, cov, turned, train, per_query, total_count)
    outgoing = scores.reshape(shard_count * layers, per_query, examples // layers)
    received = lax.all_to_all(outgoing, ("dp", "layer"), split_axis=0, concat_axis=0, tiled=True)
    received = received.reshape(shard_count, layers, per_query, examples // layers)
    return picked(listed, received)


def solution(mesh):
    in_specs = (
        P(("groups", "dp"), "layer", None),
        P(("groups", "dp"), "layer", None),
        P(("groups", "dp"), None),
    )
    out_specs = P(("groups", "dp"), None, "layer")
    return jax.shard_map(shards, mesh=mesh, in_specs=in_specs, out_specs=out_specs, check_vma=False)
```

```python
import functools
import jax
import jax.numpy as jnp
from jax import lax
from jax.experimental import pallas as pl
from jax.experimental.pallas import tpu as pltpu
from jax.sharding import PartitionSpec as P

K_OUT = 64
K_IN = 64
LANES = 128
CHUNK = 64
PIVOT = 4
F32 = jnp.float32
BF16 = jnp.bfloat16
VMEM_LIMIT = 48 * 1024 * 1024
STAGE_VMEM_LIMIT = 50 * 1024 * 1024

NT = (((1,), (1,)), ((), ()))


def low_half(rows):
    return lax.broadcasted_iota(jnp.int32, (rows, LANES), 1) < LANES // 2


def swap_pair(first, second):
    low = low_half(first.shape[0])
    even = jnp.where(low, first, pltpu.roll(second, LANES // 2, 1))
    odd = jnp.where(low, pltpu.roll(first, LANES // 2, 1), second)
    return even, odd


def split(values, terms):
    parts = []
    for _ in range(terms):
        part = values.astype(BF16)
        parts.append(part)
        values = values - part.astype(F32)
    return parts


def stage_kernel(train_ref, in_ref, rows_ref, held, by_in, arrived):
    examples, width = train_ref.shape
    pair = 2 * LANES
    chunks, _, chunk = held.shape
    copies = []
    for g in range(chunks):
        source = train_ref.at[:, pl.ds(g * chunk, chunk)]
        copies.append(pltpu.make_async_copy(source, held.at[g], arrived.at[g]))
        copies[-1].start()
    for m in range(width // pair):
        if m * pair % chunk == 0:
            copies[m * pair // chunk].wait()
        begin = m * pair % chunk
        block = held[m * pair // chunk, :, begin:begin + pair].astype(F32).T
        for k in range(4):
            start = (4 * m + k) * examples
            by_in[:, start:start + examples] = block[k * K_IN:(k + 1) * K_IN, :].astype(BF16)
        for half in range(2):
            for j in range(K_IN // 8):
                first = half * K_IN + j * 8
                both = jnp.concatenate([block[first:first + 8, :], block[first + LANES:first + LANES + 8, :]], axis=0)
                at = half * K_OUT // 2 * 8 + m * 16
                rows_ref[at:at + 16, j * examples:(j + 1) * examples] = both.astype(BF16)
    in_ref[...] = lax.dot_general(by_in[...], by_in[...], NT, preferred_element_type=F32)


def gram_kernel(in_ref, rows_ref, cov_ref):
    count = rows_ref.shape[0]
    every = lax.dot_general(rows_ref[...], rows_ref[...], NT, preferred_element_type=F32)
    row = lax.broadcasted_iota(jnp.int32, (count, count), 0)
    lane = lax.broadcasted_iota(jnp.int32, (count, count), 1)
    every = jnp.where((row & 7) == (lane & 7), every, 0.0)
    summed = jnp.sum(every.reshape(count // 8, 8, count), axis=1)
    lane = lax.broadcasted_iota(jnp.int32, (count, count // 8), 0)
    column = lax.broadcasted_iota(jnp.int32, (count, count // 8), 1)
    merge = jnp.where(lane // 8 == column, 1.0, 0.0).astype(BF16)
    out_sum = sum(jnp.dot(part, merge, preferred_element_type=F32) for part in reversed(split(summed, 3)))
    cov_ref[...] = jnp.concatenate([in_ref[...], out_sum], axis=1)


def staged_rows(train):
    examples, width = train.shape
    chunks = 8 if width % (8 * 2 * LANES) == 0 else 1
    return pl.pallas_call(
        stage_kernel,
        out_shape=(
            jax.ShapeDtypeStruct((K_IN, K_IN), F32),
            jax.ShapeDtypeStruct((8 * K_OUT, K_IN // 8 * examples), BF16),
        ),
        in_specs=[pl.BlockSpec(memory_space=pltpu.HBM)],
        out_specs=(pl.BlockSpec(memory_space=pltpu.VMEM), pl.BlockSpec(memory_space=pltpu.VMEM)),
        scratch_shapes=[
            pltpu.VMEM((chunks, examples, width // chunks), BF16),
            pltpu.VMEM((K_IN, K_OUT * examples), BF16),
            pltpu.SemaphoreType.DMA((chunks,)),
        ],
        compiler_params=pltpu.CompilerParams(vmem_limit_bytes=STAGE_VMEM_LIMIT),
        cost_estimate=pl.CostEstimate(flops=32 * examples * 64**3, bytes_accessed=2 * examples * width, transcendentals=0),
        name="stage_rows",
    )(train)


def covariance_sums(in_sum, rows):
    return pl.pallas_call(
        gram_kernel,
        out_shape=jax.ShapeDtypeStruct((K_OUT, 2 * K_IN), F32),
        in_specs=[pl.BlockSpec(memory_space=pltpu.VMEM), pl.BlockSpec(memory_space=pltpu.VMEM)],
        out_specs=pl.BlockSpec(memory_space=pltpu.VMEM),
        compiler_params=pltpu.CompilerParams(vmem_limit_bytes=VMEM_LIMIT),
        cost_estimate=pl.CostEstimate(flops=2 * rows.shape[0] * rows.size, bytes_accessed=2 * rows.size, transcendentals=0),
        name="covariance",
    )(in_sum, rows)


def turn_kernel(*refs):
    query_refs, out_ref, spread = refs[:-2], refs[-2], refs[-1]
    blocks = out_ref.shape[0] // 2
    half = CHUNK // 2
    for c in range(blocks):
        at = c * CHUNK
        for ref in query_refs:
            count = ref.shape[0]
            spread[at:at + count, :] = ref[:, c * LANES:(c + 1) * LANES].astype(F32)
            at = at + count
    for p in range(half):
        first = spread[pl.ds(p, blocks, stride=CHUNK), :]
        second = spread[pl.ds(p + half, blocks, stride=CHUNK), :]
        even, odd = swap_pair(first, second)
        out_ref[:blocks, p * LANES:(p + 1) * LANES] = even.astype(BF16)
        out_ref[blocks:, p * LANES:(p + 1) * LANES] = odd.astype(BF16)


def turned_queries(queries):
    width = queries[0].shape[1]
    total = sum(part.shape[0] for part in queries)
    steps = total // CHUNK
    if steps == 1:
        in_specs = [pl.BlockSpec(part.shape, lambda step: (0, 0)) for part in queries]
    else:
        in_specs = [pl.BlockSpec((CHUNK, width), lambda step: (step, 0))]
    return pl.pallas_call(
        turn_kernel,
        out_shape=jax.ShapeDtypeStruct((K_OUT, total * K_IN), BF16),
        grid=(steps,),
        in_specs=in_specs,
        out_specs=pl.BlockSpec((K_OUT, CHUNK * K_IN), lambda step: (0, step)),
        scratch_shapes=[pltpu.VMEM((width // LANES * CHUNK, LANES), F32)],
        compiler_params=pltpu.CompilerParams(vmem_limit_bytes=VMEM_LIMIT),
        cost_estimate=pl.CostEstimate(flops=4096 * total * width, bytes_accessed=4 * total * width, transcendentals=0),
        name="turn_queries",
    )(*queries)


def damped(cov, total_count):
    rows = lax.broadcasted_iota(jnp.int32, (K_OUT, LANES), 0)
    lanes = lax.broadcasted_iota(jnp.int32, (K_OUT, LANES), 1)
    low = lanes < K_IN
    diagonal = rows == jnp.where(low, lanes, lanes - K_IN)
    cov = cov * (1.0 / total_count)
    on_diagonal = jnp.sum(jnp.where(diagonal, cov, 0.0), axis=0, keepdims=True)
    low_row = low_half(1)
    in_mean = jnp.sum(jnp.where(low_row, on_diagonal, 0.0), axis=1, keepdims=True) / K_IN
    out_mean = jnp.sum(jnp.where(low_row, 0.0, on_diagonal), axis=1, keepdims=True) / K_OUT
    scale = jnp.where(low_row, 1.0 / in_mean, 1.0)
    added = jnp.where(low_row, 0.1, 0.1 * out_mean)
    return cov * scale + jnp.where(diagonal, added, 0.0)


def inverses(matrix):
    size = matrix.shape[0]
    lanes = lax.broadcasted_iota(jnp.int32, (size, LANES), 1)
    offset = jnp.where(lanes < size, 0, size)
    rows = lax.broadcasted_iota(jnp.int32, (size, LANES), 0)
    row_lanes = lax.broadcasted_iota(jnp.int32, (8, LANES), 1)
    row_place = jnp.where(row_lanes < size, row_lanes, row_lanes - size)
    place = lanes - offset

    def spread_row(values, row):
        return jnp.broadcast_to(values[row:row + 1, :], (8, LANES))

    for begin in range(0, size, PIVOT):
        columns = [jnp.take_along_axis(matrix, offset + begin + a, axis=1) for a in range(PIVOT)]
        p = [[spread_row(columns[b], begin + a) for b in range(PIVOT)] for a in range(PIVOT)]
        r = []
        for a in range(PIVOT):
            row = spread_row(matrix, begin + a)
            inside = (row_place >= begin) & (row_place < begin + PIVOT)
            unit = jnp.where(row_place == begin + a, 1.0, 0.0)
            r.append(jnp.where(inside, unit, row))
        det = 1.0 / (p[0][0] * p[1][1] - p[0][1] * p[1][0])
        e = [[p[1][1] * det, -p[0][1] * det], [-p[1][0] * det, p[0][0] * det]]
        u = [[e[a][0] * p[0][b] + e[a][1] * p[1][b] for b in (2, 3)] for a in (0, 1)]
        s = [[p[a][b + 2] - (p[a][0] * u[0][b] + p[a][1] * u[1][b]) for b in (0, 1)] for a in (2, 3)]
        det = 1.0 / (s[0][0] * s[1][1] - s[0][1] * s[1][0])
        f = [[s[1][1] * det, -s[0][1] * det], [-s[1][0] * det, s[0][0] * det]]
        w = [e[a][0] * r[0] + e[a][1] * r[1] for a in (0, 1)]
        t = [r[a] - (p[a][0] * w[0] + p[a][1] * w[1]) for a in (2, 3)]
        last = [f[a][0] * t[0] + f[a][1] * t[1] for a in (0, 1)]
        first = [w[a] - (u[a][0] * last[0] + u[a][1] * last[1]) for a in (0, 1)]
        solved = first + last
        inside = (place >= begin) & (place < begin + PIVOT)
        rest = jnp.where(inside, 0.0, matrix)
        tall = [jnp.concatenate([row] * (size // 8), axis=0) for row in solved]
        for a in range(PIVOT):
            rest = rest - columns[a] * tall[a]
        for a in range(PIVOT):
            rest = jnp.where(rows == begin + a, tall[a], rest)
        matrix = rest
    return matrix


def score_kernel(total_count, route_ref, cov_ref, turned_ref, train_ref, out_ref, left, right, solved, ready):
    blocks = K_OUT // 2
    half = CHUNK // 2
    step = pl.program_id(0)

    @pl.when(step == 0)
    def _():
        inverse = inverses(damped(cov_ref[...], total_count))
        turned = pltpu.roll(inverse, LANES // 2, 1)
        low = low_half(K_OUT)
        left[...] = jnp.concatenate(split(turned[:, :K_OUT], 3), axis=1)
        double = jnp.concatenate([jnp.where(low, inverse, 0.0), jnp.where(low, 0.0, turned)], axis=0)
        high, small = split(double, 2)
        right[:LANES, :LANES] = high
        right[:LANES, LANES:] = small
        right[LANES:, :LANES] = high
        right[LANES:, LANES:] = jnp.zeros_like(small)

    group = 4
    for g in range(half // group):
        block = turned_ref[:, g * group * LANES:(g + 1) * group * LANES]
        tall = jnp.concatenate([block, block, block], axis=0)
        once = jnp.dot(left[...], tall, preferred_element_type=F32)
        once = jnp.concatenate([once[:, k * LANES:(k + 1) * LANES] for k in range(group)], axis=0)
        wide = jnp.concatenate(split(once, 2), axis=1)
        twice = jnp.dot(wide, right[...], preferred_element_type=F32)
        solved[g * group * K_OUT:(g + 1) * group * K_OUT, :] = twice[:, :LANES] + twice[:, LANES:]
    for c in range(blocks):
        first = solved[pl.ds(c, half, stride=K_OUT), :]
        second = solved[pl.ds(c + blocks, half, stride=K_OUT), :]
        even, odd = swap_pair(first, second)
        ready[:half, c * LANES:(c + 1) * LANES] = even.astype(BF16)
        ready[half:, c * LANES:(c + 1) * LANES] = odd.astype(BF16)
    scores = lax.dot_general(ready[...], train_ref[...], NT, preferred_element_type=F32)
    per_query = out_ref.shape[2]
    parts = out_ref.shape[1]
    for s in range(CHUNK // per_query):
        owner = route_ref[step * (CHUNK // per_query) + s]
        for part in range(parts):
            piece = scores[s * per_query:(s + 1) * per_query, part * LANES:(part + 1) * LANES]
            out_ref[owner, part, :, :] = piece


def all_scores(route, cov, turned, train, per_query, total_count):
    shard_count = route.shape[0]
    examples, width = train.shape
    steps = shard_count * per_query // CHUNK
    parts = examples // LANES
    return pl.pallas_call(
        functools.partial(score_kernel, total_count),
        out_shape=jax.ShapeDtypeStruct((shard_count, parts, per_query, LANES), F32),
        grid=(steps,),
        in_specs=[
            pl.BlockSpec(memory_space=pltpu.SMEM),
            pl.BlockSpec((K_OUT, 2 * K_IN), lambda step: (0, 0)),
            pl.BlockSpec((K_OUT, CHUNK * K_IN), lambda step: (0, step)),
            pl.BlockSpec((examples, width), lambda step: (0, 0)),
        ],
        out_specs=pl.BlockSpec((shard_count, parts, per_query, LANES), lambda step: (0, 0, 0, 0)),
        scratch_shapes=[
            pltpu.VMEM((K_OUT, 3 * K_OUT), BF16),
            pltpu.VMEM((2 * LANES, 2 * LANES), BF16),
            pltpu.VMEM((CHUNK // 2 * K_OUT, LANES), F32),
            pltpu.VMEM((CHUNK, width), BF16),
        ],
        compiler_params=pltpu.CompilerParams(vmem_limit_bytes=VMEM_LIMIT),
        cost_estimate=pl.CostEstimate(
            flops=2 * shard_count * per_query * width * (examples + 128), bytes_accessed=2 * examples * width, transcendentals=0
        ),
        name="solve_and_score",
    )(route, cov, turned, train)


def pick_kernel(listed_ref, received_ref, out_ref):
    for r in range(out_ref.shape[0]):
        shard = listed_ref[0, r]
        total = received_ref[shard, 0]
        for layer in range(1, received_ref.shape[1]):
            total = total + received_ref[shard, layer]
        out_ref[r] = total


def picked(listed, received):
    return pl.pallas_call(
        pick_kernel,
        out_shape=jax.ShapeDtypeStruct((listed.shape[1],) + received.shape[2:], F32),
        in_specs=[pl.BlockSpec(memory_space=pltpu.SMEM), pl.BlockSpec(memory_space=pltpu.VMEM)],
        out_specs=pl.BlockSpec(memory_space=pltpu.VMEM),
        compiler_params=pltpu.CompilerParams(vmem_limit_bytes=VMEM_LIMIT),
        name="pick_tiles",
    )(listed, received)


def exchange(values, distance, count):
    return lax.ppermute(values, "dp", [(k, k ^ distance) for k in range(count)])


def shards(train_grads, query_grads, listed):
    shard_count = lax.axis_size("dp")
    layers = lax.axis_size("layer")
    own_index = lax.axis_index("dp").astype(jnp.int32)
    examples = train_grads.shape[0]
    per_query = query_grads.shape[0]
    train = train_grads.reshape(examples, train_grads.shape[2])
    own_queries = query_grads.reshape(per_query, query_grads.shape[2])
    total_count = float(examples * shard_count)
    order = jnp.arange(shard_count, dtype=jnp.int32)
    if shard_count == 8:
        beside = exchange(own_queries, 1, shard_count)
        column = [exchange(own_queries, distance, shard_count) for distance in (4, 6, 2)]
        cov = covariance_sums(*staged_rows(train))
        beside, column, cov = lax.optimization_barrier((beside, column, cov))
        column = jnp.concatenate(column, axis=0)
        queries = [own_queries, column, beside, exchange(column, 1, shard_count)]
        for distance in (4, 2):
            cov = cov + exchange(cov, distance, shard_count)
        last = exchange(cov, 1, shard_count)
        turned, cov = lax.optimization_barrier((turned_queries(queries), cov))
        cov = cov + last
        order = jnp.array([0, 4, 6, 2, 1, 5, 7, 3], jnp.int32)
        route = own_index ^ order
    else:
        turned = turned_queries([lax.all_gather(own_queries, "dp", axis=0, tiled=True)])
        cov = lax.psum(covariance_sums(*staged_rows(train)), "dp")
        route = order
    scores = all_scores(route, cov, turned, train, per_query, total_count)
    outgoing = scores.reshape(shard_count * layers, per_query, examples // layers)
    received = lax.all_to_all(outgoing, ("dp", "layer"), split_axis=0, concat_axis=0, tiled=True)
    received = received.reshape(shard_count, layers, per_query, examples // layers)
    return picked(listed, received)


def solution(mesh):
    in_specs = (
        P(("groups", "dp"), "layer", None),
        P(("groups", "dp"), "layer", None),
        P(("groups", "dp"), None),
    )
    out_specs = P(("groups", "dp"), None, "layer")
    return jax.shard_map(shards, mesh=mesh, in_specs=in_specs, out_specs=out_specs, check_vma=False)
```

```python
import functools
import jax
import jax.numpy as jnp
from jax import lax
from jax.experimental import pallas as pl
from jax.experimental.pallas import tpu as pltpu
from jax.sharding import PartitionSpec as P

K_OUT = 64
K_IN = 64
LANES = 128
CHUNK = 64
PIVOT = 4
F32 = jnp.float32
BF16 = jnp.bfloat16
VMEM_LIMIT = 48 * 1024 * 1024
STAGE_VMEM_LIMIT = 50 * 1024 * 1024

NT = (((1,), (1,)), ((), ()))


def low_half(rows):
    return lax.broadcasted_iota(jnp.int32, (rows, LANES), 1) < LANES // 2


def swap_pair(first, second):
    low = low_half(first.shape[0])
    even = jnp.where(low, first, pltpu.roll(second, LANES // 2, 1))
    odd = jnp.where(low, pltpu.roll(first, LANES // 2, 1), second)
    return even, odd


def split(values, terms):
    parts = []
    for _ in range(terms):
        part = values.astype(BF16)
        parts.append(part)
        values = values - part.astype(F32)
    return parts


def stage_kernel(train_ref, in_ref, rows_ref, held, by_in, arrived):
    examples, width = train_ref.shape
    pair = 2 * LANES
    chunks, _, chunk = held.shape
    copies = []
    for g in range(chunks):
        source = train_ref.at[:, pl.ds(g * chunk, chunk)]
        copies.append(pltpu.make_async_copy(source, held.at[g], arrived.at[g]))
        copies[-1].start()
    for m in range(width // pair):
        if m * pair % chunk == 0:
            copies[m * pair // chunk].wait()
        begin = m * pair % chunk
        block = held[m * pair // chunk, :, begin:begin + pair].astype(F32).T
        for k in range(4):
            start = (4 * m + k) * examples
            by_in[:, start:start + examples] = block[k * K_IN:(k + 1) * K_IN, :].astype(BF16)
        for half in range(2):
            for j in range(K_IN // 8):
                first = half * K_IN + j * 8
                both = jnp.concatenate([block[first:first + 8, :], block[first + LANES:first + LANES + 8, :]], axis=0)
                at = half * K_OUT // 2 * 8 + m * 16
                rows_ref[at:at + 16, j * examples:(j + 1) * examples] = both.astype(BF16)
    in_ref[...] = lax.dot_general(by_in[...], by_in[...], NT, preferred_element_type=F32)


def gram_kernel(in_ref, rows_ref, cov_ref):
    count = rows_ref.shape[0]
    every = lax.dot_general(rows_ref[...], rows_ref[...], NT, preferred_element_type=F32)
    row = lax.broadcasted_iota(jnp.int32, (count, count), 0)
    lane = lax.broadcasted_iota(jnp.int32, (count, count), 1)
    every = jnp.where((row & 7) == (lane & 7), every, 0.0)
    summed = jnp.sum(every.reshape(count // 8, 8, count), axis=1)
    lane = lax.broadcasted_iota(jnp.int32, (count, count // 8), 0)
    column = lax.broadcasted_iota(jnp.int32, (count, count // 8), 1)
    merge = jnp.where(lane // 8 == column, 1.0, 0.0).astype(BF16)
    out_sum = sum(jnp.dot(part, merge, preferred_element_type=F32) for part in reversed(split(summed, 3)))
    cov_ref[...] = jnp.concatenate([in_ref[...], out_sum], axis=1)


def staged_rows(train):
    examples, width = train.shape
    chunks = 8 if width % (8 * 2 * LANES) == 0 else 1
    return pl.pallas_call(
        stage_kernel,
        out_shape=(
            jax.ShapeDtypeStruct((K_IN, K_IN), F32),
            jax.ShapeDtypeStruct((8 * K_OUT, K_IN // 8 * examples), BF16),
        ),
        in_specs=[pl.BlockSpec(memory_space=pltpu.HBM)],
        out_specs=(pl.BlockSpec(memory_space=pltpu.VMEM), pl.BlockSpec(memory_space=pltpu.VMEM)),
        scratch_shapes=[
            pltpu.VMEM((chunks, examples, width // chunks), BF16),
            pltpu.VMEM((K_IN, K_OUT * examples), BF16),
            pltpu.SemaphoreType.DMA((chunks,)),
        ],
        compiler_params=pltpu.CompilerParams(vmem_limit_bytes=STAGE_VMEM_LIMIT),
        cost_estimate=pl.CostEstimate(flops=32 * examples * 64**3, bytes_accessed=2 * examples * width, transcendentals=0),
        name="stage_rows",
    )(train)


def covariance_sums(in_sum, rows):
    return pl.pallas_call(
        gram_kernel,
        out_shape=jax.ShapeDtypeStruct((K_OUT, 2 * K_IN), F32),
        in_specs=[pl.BlockSpec(memory_space=pltpu.VMEM), pl.BlockSpec(memory_space=pltpu.VMEM)],
        out_specs=pl.BlockSpec(memory_space=pltpu.VMEM),
        compiler_params=pltpu.CompilerParams(vmem_limit_bytes=VMEM_LIMIT),
        cost_estimate=pl.CostEstimate(flops=2 * rows.shape[0] * rows.size, bytes_accessed=2 * rows.size, transcendentals=0),
        name="covariance",
    )(in_sum, rows)


def turn_kernel(*refs):
    query_refs, out_ref, spread = refs[:-2], refs[-2], refs[-1]
    blocks = out_ref.shape[0] // 2
    half = CHUNK // 2
    for c in range(blocks):
        at = c * CHUNK
        for ref in query_refs:
            count = ref.shape[0]
            spread[at:at + count, :] = ref[:, c * LANES:(c + 1) * LANES].astype(F32)
            at = at + count
    for p in range(half):
        first = spread[pl.ds(p, blocks, stride=CHUNK), :]
        second = spread[pl.ds(p + half, blocks, stride=CHUNK), :]
        even, odd = swap_pair(first, second)
        out_ref[:blocks, p * LANES:(p + 1) * LANES] = even.astype(BF16)
        out_ref[blocks:, p * LANES:(p + 1) * LANES] = odd.astype(BF16)


def turned_queries(queries):
    width = queries[0].shape[1]
    total = sum(part.shape[0] for part in queries)
    steps = total // CHUNK
    if steps == 1:
        in_specs = [pl.BlockSpec(part.shape, lambda step: (0, 0)) for part in queries]
    else:
        in_specs = [pl.BlockSpec((CHUNK, width), lambda step: (step, 0))]
    return pl.pallas_call(
        turn_kernel,
        out_shape=jax.ShapeDtypeStruct((K_OUT, total * K_IN), BF16),
        grid=(steps,),
        in_specs=in_specs,
        out_specs=pl.BlockSpec((K_OUT, CHUNK * K_IN), lambda step: (0, step)),
        scratch_shapes=[pltpu.VMEM((width // LANES * CHUNK, LANES), F32)],
        compiler_params=pltpu.CompilerParams(vmem_limit_bytes=VMEM_LIMIT),
        cost_estimate=pl.CostEstimate(flops=4096 * total * width, bytes_accessed=4 * total * width, transcendentals=0),
        name="turn_queries",
    )(*queries)


def damped(cov, total_count):
    rows = lax.broadcasted_iota(jnp.int32, (K_OUT, LANES), 0)
    lanes = lax.broadcasted_iota(jnp.int32, (K_OUT, LANES), 1)
    low = lanes < K_IN
    diagonal = rows == jnp.where(low, lanes, lanes - K_IN)
    cov = cov * (1.0 / total_count)
    on_diagonal = jnp.sum(jnp.where(diagonal, cov, 0.0), axis=0, keepdims=True)
    low_row = low_half(1)
    in_mean = jnp.sum(jnp.where(low_row, on_diagonal, 0.0), axis=1, keepdims=True) / K_IN
    out_mean = jnp.sum(jnp.where(low_row, 0.0, on_diagonal), axis=1, keepdims=True) / K_OUT
    scale = jnp.where(low_row, 1.0 / in_mean, 1.0)
    added = jnp.where(low_row, 0.1, 0.1 * out_mean)
    return cov * scale + jnp.where(diagonal, added, 0.0)


def inverses(matrix):
    size = matrix.shape[0]
    lanes = lax.broadcasted_iota(jnp.int32, (size, LANES), 1)
    offset = jnp.where(lanes < size, 0, size)
    rows = lax.broadcasted_iota(jnp.int32, (size, LANES), 0)
    row_lanes = lax.broadcasted_iota(jnp.int32, (8, LANES), 1)
    row_place = jnp.where(row_lanes < size, row_lanes, row_lanes - size)
    place = lanes - offset

    def spread_row(values, row):
        return jnp.broadcast_to(values[row:row + 1, :], (8, LANES))

    for begin in range(0, size, PIVOT):
        columns = [jnp.take_along_axis(matrix, offset + begin + a, axis=1) for a in range(PIVOT)]
        p = [[spread_row(columns[b], begin + a) for b in range(PIVOT)] for a in range(PIVOT)]
        r = []
        for a in range(PIVOT):
            row = spread_row(matrix, begin + a)
            inside = (row_place >= begin) & (row_place < begin + PIVOT)
            unit = jnp.where(row_place == begin + a, 1.0, 0.0)
            r.append(jnp.where(inside, unit, row))
        det = 1.0 / (p[0][0] * p[1][1] - p[0][1] * p[1][0])
        e = [[p[1][1] * det, -p[0][1] * det], [-p[1][0] * det, p[0][0] * det]]
        u = [[e[a][0] * p[0][b] + e[a][1] * p[1][b] for b in (2, 3)] for a in (0, 1)]
        s = [[p[a][b + 2] - (p[a][0] * u[0][b] + p[a][1] * u[1][b]) for b in (0, 1)] for a in (2, 3)]
        det = 1.0 / (s[0][0] * s[1][1] - s[0][1] * s[1][0])
        f = [[s[1][1] * det, -s[0][1] * det], [-s[1][0] * det, s[0][0] * det]]
        w = [e[a][0] * r[0] + e[a][1] * r[1] for a in (0, 1)]
        t = [r[a] - (p[a][0] * w[0] + p[a][1] * w[1]) for a in (2, 3)]
        last = [f[a][0] * t[0] + f[a][1] * t[1] for a in (0, 1)]
        first = [w[a] - (u[a][0] * last[0] + u[a][1] * last[1]) for a in (0, 1)]
        solved = first + last
        inside = (place >= begin) & (place < begin + PIVOT)
        rest = jnp.where(inside, 0.0, matrix)
        tall = [jnp.concatenate([row] * (size // 8), axis=0) for row in solved]
        for a in range(PIVOT):
            rest = rest - columns[a] * tall[a]
        for a in range(PIVOT):
            rest = jnp.where(rows == begin + a, tall[a], rest)
        matrix = rest
    return matrix


def score_kernel(total_count, route_ref, cov_ref, turned_ref, train_ref, out_ref, left, right, solved, ready):
    blocks = K_OUT // 2
    half = CHUNK // 2
    step = pl.program_id(0)

    @pl.when(step == 0)
    def _():
        inverse = inverses(damped(cov_ref[...], total_count))
        turned = pltpu.roll(inverse, LANES // 2, 1)
        low = low_half(K_OUT)
        left[...] = jnp.concatenate(split(turned[:, :K_OUT], 3), axis=1)
        double = jnp.concatenate([jnp.where(low, inverse, 0.0), jnp.where(low, 0.0, turned)], axis=0)
        high, small = split(double, 2)
        right[:LANES, :LANES] = high
        right[:LANES, LANES:] = small
        right[LANES:, :LANES] = high
        right[LANES:, LANES:] = jnp.zeros_like(small)

    group = 4
    for g in range(half // group):
        block = turned_ref[:, g * group * LANES:(g + 1) * group * LANES]
        tall = jnp.concatenate([block, block, block], axis=0)
        once = jnp.dot(left[...], tall, preferred_element_type=F32)
        once = jnp.concatenate([once[:, k * LANES:(k + 1) * LANES] for k in range(group)], axis=0)
        wide = jnp.concatenate(split(once, 2), axis=1)
        twice = jnp.dot(wide, right[...], preferred_element_type=F32)
        solved[g * group * K_OUT:(g + 1) * group * K_OUT, :] = twice[:, :LANES] + twice[:, LANES:]
    for c in range(blocks):
        first = solved[pl.ds(c, half, stride=K_OUT), :]
        second = solved[pl.ds(c + blocks, half, stride=K_OUT), :]
        even, odd = swap_pair(first, second)
        ready[:half, c * LANES:(c + 1) * LANES] = even.astype(BF16)
        ready[half:, c * LANES:(c + 1) * LANES] = odd.astype(BF16)
    scores = lax.dot_general(ready[...], train_ref[...], NT, preferred_element_type=F32)
    per_query = out_ref.shape[2]
    parts = out_ref.shape[1]
    for s in range(CHUNK // per_query):
        owner = route_ref[step * (CHUNK // per_query) + s]
        for part in range(parts):
            piece = scores[s * per_query:(s + 1) * per_query, part * LANES:(part + 1) * LANES]
            out_ref[owner, part, :, :] = piece


def all_scores(route, cov, turned, train, per_query, total_count):
    shard_count = route.shape[0]
    examples, width = train.shape
    steps = shard_count * per_query // CHUNK
    parts = examples // LANES
    return pl.pallas_call(
        functools.partial(score_kernel, total_count),
        out_shape=jax.ShapeDtypeStruct((shard_count, parts, per_query, LANES), F32),
        grid=(steps,),
        in_specs=[
            pl.BlockSpec(memory_space=pltpu.SMEM),
            pl.BlockSpec((K_OUT, 2 * K_IN), lambda step: (0, 0)),
            pl.BlockSpec((K_OUT, CHUNK * K_IN), lambda step: (0, step)),
            pl.BlockSpec((examples, width), lambda step: (0, 0)),
        ],
        out_specs=pl.BlockSpec((shard_count, parts, per_query, LANES), lambda step: (0, 0, 0, 0)),
        scratch_shapes=[
            pltpu.VMEM((K_OUT, 3 * K_OUT), BF16),
            pltpu.VMEM((2 * LANES, 2 * LANES), BF16),
            pltpu.VMEM((CHUNK // 2 * K_OUT, LANES), F32),
            pltpu.VMEM((CHUNK, width), BF16),
        ],
        compiler_params=pltpu.CompilerParams(vmem_limit_bytes=VMEM_LIMIT),
        cost_estimate=pl.CostEstimate(
            flops=2 * shard_count * per_query * width * (examples + 128), bytes_accessed=2 * examples * width, transcendentals=0
        ),
        name="solve_and_score",
    )(route, cov, turned, train)


def pick_kernel(listed_ref, received_ref, out_ref):
    for r in range(out_ref.shape[0]):
        shard = listed_ref[0, r]
        total = received_ref[shard, 0]
        for layer in range(1, received_ref.shape[1]):
            total = total + received_ref[shard, layer]
        out_ref[r] = total


def picked(listed, received):
    return pl.pallas_call(
        pick_kernel,
        out_shape=jax.ShapeDtypeStruct((listed.shape[1],) + received.shape[2:], F32),
        in_specs=[pl.BlockSpec(memory_space=pltpu.SMEM), pl.BlockSpec(memory_space=pltpu.VMEM)],
        out_specs=pl.BlockSpec(memory_space=pltpu.VMEM),
        compiler_params=pltpu.CompilerParams(vmem_limit_bytes=VMEM_LIMIT),
        name="pick_tiles",
    )(listed, received)


def exchange(values, distance, count):
    return lax.ppermute(values, "dp", [(k, k ^ distance) for k in range(count)])


def shards(train_grads, query_grads, listed):
    shard_count = lax.axis_size("dp")
    layers = lax.axis_size("layer")
    own_index = lax.axis_index("dp").astype(jnp.int32)
    examples = train_grads.shape[0]
    per_query = query_grads.shape[0]
    train = train_grads.reshape(examples, train_grads.shape[2])
    own_queries = query_grads.reshape(per_query, query_grads.shape[2])
    total_count = float(examples * shard_count)
    order = jnp.arange(shard_count, dtype=jnp.int32)
    if shard_count == 8:
        far = exchange(own_queries, 4, shard_count)
        cov = covariance_sums(*staged_rows(train))
        far, cov = lax.optimization_barrier((far, cov))
        column = jnp.concatenate([own_queries, far], axis=0)
        cov = cov + exchange(cov, 1, shard_count)
        near = exchange(column, 2, shard_count)
        near, cov = lax.optimization_barrier((near, cov))
        cov = cov + exchange(cov, 4, shard_count)
        column = jnp.concatenate([column, near], axis=0)
        queries = [column, exchange(column, 1, shard_count)]
        last = exchange(cov, 2, shard_count)
        turned, cov = lax.optimization_barrier((turned_queries(queries), cov))
        cov = cov + last
        order = jnp.array([0, 4, 2, 6, 1, 5, 3, 7], jnp.int32)
        route = own_index ^ order
    else:
        turned = turned_queries([lax.all_gather(own_queries, "dp", axis=0, tiled=True)])
        cov = lax.psum(covariance_sums(*staged_rows(train)), "dp")
        route = order
    scores = all_scores(route, cov, turned, train, per_query, total_count)
    outgoing = scores.reshape(shard_count * layers, per_query, examples // layers)
    received = lax.all_to_all(outgoing, ("dp", "layer"), split_axis=0, concat_axis=0, tiled=True)
    received = received.reshape(shard_count, layers, per_query, examples // layers)
    return picked(listed, received)


def solution(mesh):
    in_specs = (
        P(("groups", "dp"), "layer", None),
        P(("groups", "dp"), "layer", None),
        P(("groups", "dp"), None),
    )
    out_specs = P(("groups", "dp"), None, "layer")
    return jax.shard_map(shards, mesh=mesh, in_specs=in_specs, out_specs=out_specs, check_vma=False)
```

```python
import functools
import jax
import jax.numpy as jnp
from jax import lax
from jax.experimental import pallas as pl
from jax.experimental.pallas import tpu as pltpu
from jax.sharding import PartitionSpec as P

K_OUT = 64
K_IN = 64
LANES = 128
CHUNK = 64
PIVOT = 4
F32 = jnp.float32
BF16 = jnp.bfloat16
VMEM_LIMIT = 48 * 1024 * 1024
STAGE_VMEM_LIMIT = 50 * 1024 * 1024

NT = (((1,), (1,)), ((), ()))


def low_half(rows):
    return lax.broadcasted_iota(jnp.int32, (rows, LANES), 1) < LANES // 2


def swap_pair(first, second):
    low = low_half(first.shape[0])
    even = jnp.where(low, first, pltpu.roll(second, LANES // 2, 1))
    odd = jnp.where(low, pltpu.roll(first, LANES // 2, 1), second)
    return even, odd


def split(values, terms):
    parts = []
    for _ in range(terms):
        part = values.astype(BF16)
        parts.append(part)
        values = values - part.astype(F32)
    return parts


def stage_kernel(train_ref, in_ref, rows_ref, held, by_in, arrived):
    examples, width = train_ref.shape
    pair = 2 * LANES
    chunks, _, chunk = held.shape
    copies = []
    for g in range(chunks):
        source = train_ref.at[:, pl.ds(g * chunk, chunk)]
        copies.append(pltpu.make_async_copy(source, held.at[g], arrived.at[g]))
        copies[-1].start()
    row = lax.broadcasted_iota(jnp.int32, (pair, pair), 0)
    lane = lax.broadcasted_iota(jnp.int32, (pair, pair), 1)
    unit = jnp.where(row == lane, 1.0, 0.0).astype(BF16)
    for m in range(width // pair):
        if m * pair % chunk == 0:
            copies[m * pair // chunk].wait()
        begin = m * pair % chunk
        block = lax.dot_general(
            unit, held[m * pair // chunk, :, begin:begin + pair], NT, preferred_element_type=F32
        )
        for k in range(4):
            start = (4 * m + k) * examples
            by_in[:, start:start + examples] = block[k * K_IN:(k + 1) * K_IN, :].astype(BF16)
        for half in range(2):
            for j in range(K_IN // 8):
                first = half * K_IN + j * 8
                both = jnp.concatenate([block[first:first + 8, :], block[first + LANES:first + LANES + 8, :]], axis=0)
                at = half * K_OUT // 2 * 8 + m * 16
                rows_ref[at:at + 16, j * examples:(j + 1) * examples] = both.astype(BF16)
    in_ref[...] = lax.dot_general(by_in[...], by_in[...], NT, preferred_element_type=F32)


def gram_kernel(in_ref, rows_ref, cov_ref):
    count = rows_ref.shape[0] // 2
    row = lax.broadcasted_iota(jnp.int32, (count, count), 0)
    lane = lax.broadcasted_iota(jnp.int32, (count, count), 1)
    same = (row & 7) == (lane & 7)
    lane = lax.broadcasted_iota(jnp.int32, (count, count // 8), 0)
    column = lax.broadcasted_iota(jnp.int32, (count, count // 8), 1)
    merge = jnp.where(lane // 8 == column, 1.0, 0.0).astype(BF16)
    blocks = []
    for a, b in ((0, 0), (0, 1), (1, 1)):
        left = rows_ref[a * count:(a + 1) * count, :]
        right = rows_ref[b * count:(b + 1) * count, :]
        every = jnp.where(same, lax.dot_general(left, right, NT, preferred_element_type=F32), 0.0)
        summed = jnp.sum(every.reshape(count // 8, 8, count), axis=1)
        parts = split(summed, 3)
        blocks.append(sum(jnp.dot(part, merge, preferred_element_type=F32) for part in reversed(parts)))
    top = jnp.concatenate([blocks[0], blocks[1]], axis=1)
    bottom = jnp.concatenate([blocks[1].T, blocks[2]], axis=1)
    cov_ref[...] = jnp.concatenate([in_ref[...], jnp.concatenate([top, bottom], axis=0)], axis=1)


def staged_rows(train):
    examples, width = train.shape
    chunks = 8 if width % (8 * 2 * LANES) == 0 else 1
    return pl.pallas_call(
        stage_kernel,
        out_shape=(
            jax.ShapeDtypeStruct((K_IN, K_IN), F32),
            jax.ShapeDtypeStruct((8 * K_OUT, K_IN // 8 * examples), BF16),
        ),
        in_specs=[pl.BlockSpec(memory_space=pltpu.HBM)],
        out_specs=(pl.BlockSpec(memory_space=pltpu.VMEM), pl.BlockSpec(memory_space=pltpu.VMEM)),
        scratch_shapes=[
            pltpu.VMEM((chunks, examples, width // chunks), BF16),
            pltpu.VMEM((K_IN, K_OUT * examples), BF16),
            pltpu.SemaphoreType.DMA((chunks,)),
        ],
        compiler_params=pltpu.CompilerParams(vmem_limit_bytes=STAGE_VMEM_LIMIT),
        cost_estimate=pl.CostEstimate(flops=32 * examples * 64**3, bytes_accessed=2 * examples * width, transcendentals=0),
        name="stage_rows",
    )(train)


def covariance_sums(in_sum, rows):
    return pl.pallas_call(
        gram_kernel,
        out_shape=jax.ShapeDtypeStruct((K_OUT, 2 * K_IN), F32),
        in_specs=[pl.BlockSpec(memory_space=pltpu.VMEM), pl.BlockSpec(memory_space=pltpu.VMEM)],
        out_specs=pl.BlockSpec(memory_space=pltpu.VMEM),
        compiler_params=pltpu.CompilerParams(vmem_limit_bytes=VMEM_LIMIT),
        cost_estimate=pl.CostEstimate(flops=2 * rows.shape[0] * rows.size, bytes_accessed=2 * rows.size, transcendentals=0),
        name="covariance",
    )(in_sum, rows)


def turn_kernel(*refs):
    query_refs, out_ref, spread = refs[:-2], refs[-2], refs[-1]
    blocks = out_ref.shape[0] // 2
    half = CHUNK // 2
    for c in range(blocks):
        at = c * CHUNK
        for ref in query_refs:
            count = ref.shape[0]
            spread[at:at + count, :] = ref[:, c * LANES:(c + 1) * LANES].astype(F32)
            at = at + count
    for p in range(half):
        first = spread[pl.ds(p, blocks, stride=CHUNK), :]
        second = spread[pl.ds(p + half, blocks, stride=CHUNK), :]
        even, odd = swap_pair(first, second)
        out_ref[:blocks, p * LANES:(p + 1) * LANES] = even.astype(BF16)
        out_ref[blocks:, p * LANES:(p + 1) * LANES] = odd.astype(BF16)


def turned_queries(queries):
    width = queries[0].shape[1]
    total = sum(part.shape[0] for part in queries)
    steps = total // CHUNK
    if steps == 1:
        in_specs = [pl.BlockSpec(part.shape, lambda step: (0, 0)) for part in queries]
    else:
        in_specs = [pl.BlockSpec((CHUNK, width), lambda step: (step, 0))]
    return pl.pallas_call(
        turn_kernel,
        out_shape=jax.ShapeDtypeStruct((K_OUT, total * K_IN), BF16),
        grid=(steps,),
        in_specs=in_specs,
        out_specs=pl.BlockSpec((K_OUT, CHUNK * K_IN), lambda step: (0, step)),
        scratch_shapes=[pltpu.VMEM((width // LANES * CHUNK, LANES), F32)],
        compiler_params=pltpu.CompilerParams(vmem_limit_bytes=VMEM_LIMIT),
        cost_estimate=pl.CostEstimate(flops=4096 * total * width, bytes_accessed=4 * total * width, transcendentals=0),
        name="turn_queries",
    )(*queries)


def damped(cov, total_count):
    rows = lax.broadcasted_iota(jnp.int32, (K_OUT, LANES), 0)
    lanes = lax.broadcasted_iota(jnp.int32, (K_OUT, LANES), 1)
    low = lanes < K_IN
    diagonal = rows == jnp.where(low, lanes, lanes - K_IN)
    cov = cov * (1.0 / total_count)
    on_diagonal = jnp.sum(jnp.where(diagonal, cov, 0.0), axis=0, keepdims=True)
    low_row = low_half(1)
    in_mean = jnp.sum(jnp.where(low_row, on_diagonal, 0.0), axis=1, keepdims=True) / K_IN
    out_mean = jnp.sum(jnp.where(low_row, 0.0, on_diagonal), axis=1, keepdims=True) / K_OUT
    scale = jnp.where(low_row, 1.0 / in_mean, 1.0)
    added = jnp.where(low_row, 0.1, 0.1 * out_mean)
    return cov * scale + jnp.where(diagonal, added, 0.0)


def inverses(matrix):
    size = matrix.shape[0]
    lanes = lax.broadcasted_iota(jnp.int32, (size, LANES), 1)
    offset = jnp.where(lanes < size, 0, size)
    rows = lax.broadcasted_iota(jnp.int32, (size, LANES), 0)
    row_lanes = lax.broadcasted_iota(jnp.int32, (8, LANES), 1)
    row_place = jnp.where(row_lanes < size, row_lanes, row_lanes - size)
    place = lanes - offset

    def spread_row(values, row):
        return jnp.broadcast_to(values[row:row + 1, :], (8, LANES))

    for begin in range(0, size, PIVOT):
        columns = [jnp.take_along_axis(matrix, offset + begin + a, axis=1) for a in range(PIVOT)]
        p = [[spread_row(columns[b], begin + a) for b in range(PIVOT)] for a in range(PIVOT)]
        r = []
        for a in range(PIVOT):
            row = spread_row(matrix, begin + a)
            inside = (row_place >= begin) & (row_place < begin + PIVOT)
            unit = jnp.where(row_place == begin + a, 1.0, 0.0)
            r.append(jnp.where(inside, unit, row))
        det = 1.0 / (p[0][0] * p[1][1] - p[0][1] * p[1][0])
        e = [[p[1][1] * det, -p[0][1] * det], [-p[1][0] * det, p[0][0] * det]]
        u = [[e[a][0] * p[0][b] + e[a][1] * p[1][b] for b in (2, 3)] for a in (0, 1)]
        s = [[p[a][b + 2] - (p[a][0] * u[0][b] + p[a][1] * u[1][b]) for b in (0, 1)] for a in (2, 3)]
        det = 1.0 / (s[0][0] * s[1][1] - s[0][1] * s[1][0])
        f = [[s[1][1] * det, -s[0][1] * det], [-s[1][0] * det, s[0][0] * det]]
        w = [e[a][0] * r[0] + e[a][1] * r[1] for a in (0, 1)]
        t = [r[a] - (p[a][0] * w[0] + p[a][1] * w[1]) for a in (2, 3)]
        last = [f[a][0] * t[0] + f[a][1] * t[1] for a in (0, 1)]
        first = [w[a] - (u[a][0] * last[0] + u[a][1] * last[1]) for a in (0, 1)]
        solved = first + last
        inside = (place >= begin) & (place < begin + PIVOT)
        rest = jnp.where(inside, 0.0, matrix)
        tall = [jnp.concatenate([row] * (size // 8), axis=0) for row in solved]
        for a in range(PIVOT):
            rest = rest - columns[a] * tall[a]
        for a in range(PIVOT):
            rest = jnp.where(rows == begin + a, tall[a], rest)
        matrix = rest
    return matrix


def score_kernel(total_count, route_ref, cov_ref, turned_ref, train_ref, out_ref, left, right, solved, ready):
    blocks = K_OUT // 2
    half = CHUNK // 2
    step = pl.program_id(0)

    @pl.when(step == 0)
    def _():
        inverse = inverses(damped(cov_ref[...], total_count))
        turned = pltpu.roll(inverse, LANES // 2, 1)
        low = low_half(K_OUT)
        left[...] = jnp.concatenate(split(turned[:, :K_OUT], 3), axis=1)
        double = jnp.concatenate([jnp.where(low, inverse, 0.0), jnp.where(low, 0.0, turned)], axis=0)
        high, small = split(double, 2)
        right[:LANES, :LANES] = high
        right[:LANES, LANES:] = small
        right[LANES:, :LANES] = high
        right[LANES:, LANES:] = jnp.zeros_like(small)

    group = 4
    for g in range(half // group):
        block = turned_ref[:, g * group * LANES:(g + 1) * group * LANES]
        tall = jnp.concatenate([block, block, block], axis=0)
        once = jnp.dot(left[...], tall, preferred_element_type=F32)
        once = jnp.concatenate([once[:, k * LANES:(k + 1) * LANES] for k in range(group)], axis=0)
        wide = jnp.concatenate(split(once, 2), axis=1)
        twice = jnp.dot(wide, right[...], preferred_element_type=F32)
        solved[g * group:(g + 1) * group, :, :] = (twice[:, :LANES] + twice[:, LANES:]).reshape(group, K_OUT, LANES)
    by_row = [jnp.swapaxes(solved[:, 8 * k:8 * (k + 1), :], 0, 1) for k in range(K_OUT // 8)]
    for c in range(blocks):
        first = by_row[c // 8][c % 8]
        second = by_row[(c + blocks) // 8][c % 8]
        even, odd = swap_pair(first, second)
        ready[:half, c * LANES:(c + 1) * LANES] = even.astype(BF16)
        ready[half:, c * LANES:(c + 1) * LANES] = odd.astype(BF16)
    scores = lax.dot_general(ready[...], train_ref[...], NT, preferred_element_type=F32)
    per_query = out_ref.shape[2]
    parts = out_ref.shape[1]
    for s in range(CHUNK // per_query):
        owner = route_ref[step * (CHUNK // per_query) + s]
        for part in range(parts):
            piece = scores[s * per_query:(s + 1) * per_query, part * LANES:(part + 1) * LANES]
            out_ref[owner, part, :, :] = piece


def all_scores(route, cov, turned, train, per_query, total_count):
    shard_count = route.shape[0]
    examples, width = train.shape
    steps = shard_count * per_query // CHUNK
    parts = examples // LANES
    return pl.pallas_call(
        functools.partial(score_kernel, total_count),
        out_shape=jax.ShapeDtypeStruct((shard_count, parts, per_query, LANES), F32),
        grid=(steps,),
        in_specs=[
            pl.BlockSpec(memory_space=pltpu.SMEM),
            pl.BlockSpec((K_OUT, 2 * K_IN), lambda step: (0, 0)),
            pl.BlockSpec((K_OUT, CHUNK * K_IN), lambda step: (0, step)),
            pl.BlockSpec((examples, width), lambda step: (0, 0)),
        ],
        out_specs=pl.BlockSpec((shard_count, parts, per_query, LANES), lambda step: (0, 0, 0, 0)),
        scratch_shapes=[
            pltpu.VMEM((K_OUT, 3 * K_OUT), BF16),
            pltpu.VMEM((2 * LANES, 2 * LANES), BF16),
            pltpu.VMEM((CHUNK // 2, K_OUT, LANES), F32),
            pltpu.VMEM((CHUNK, width), BF16),
        ],
        compiler_params=pltpu.CompilerParams(vmem_limit_bytes=VMEM_LIMIT),
        cost_estimate=pl.CostEstimate(
            flops=2 * shard_count * per_query * width * (examples + 128), bytes_accessed=2 * examples * width, transcendentals=0
        ),
        name="solve_and_score",
    )(route, cov, turned, train)


def picked(listed, received):
    shard = jnp.arange(received.shape[0], dtype=jnp.int32)
    wanted = (listed[0][:, None] == shard[None, :])[:, :, None, None, None]
    return jnp.sum(jnp.where(wanted, received[None], 0.0), axis=(1, 2))


def exchange(values, distance, count):
    return lax.ppermute(values, "dp", [(k, k ^ distance) for k in range(count)])


def shards(train_grads, query_grads, listed):
    shard_count = lax.axis_size("dp")
    layers = lax.axis_size("layer")
    own_index = lax.axis_index("dp").astype(jnp.int32)
    examples = train_grads.shape[0]
    per_query = query_grads.shape[0]
    train = train_grads.reshape(examples, train_grads.shape[2])
    own_queries = query_grads.reshape(per_query, query_grads.shape[2])
    total_count = float(examples * shard_count)
    order = jnp.arange(shard_count, dtype=jnp.int32)
    if shard_count == 8:
        far = exchange(own_queries, 4, shard_count)
        cov = covariance_sums(*staged_rows(train))
        far, _ = lax.optimization_barrier((far, cov))
        column = jnp.concatenate([own_queries, far], axis=0)
        cov = cov + exchange(cov, 1, shard_count)
        near = exchange(column, 2, shard_count)
        near, cov = lax.optimization_barrier((near, cov))
        cov = cov + exchange(cov, 4, shard_count)
        column = jnp.concatenate([column, near], axis=0)
        queries = [column, exchange(column, 1, shard_count)]
        last = exchange(cov, 2, shard_count)
        turned, cov = lax.optimization_barrier((turned_queries(queries), cov))
        cov = cov + last
        order = jnp.array([0, 4, 2, 6, 1, 5, 3, 7], jnp.int32)
        route = own_index ^ order
    else:
        turned = turned_queries([lax.all_gather(own_queries, "dp", axis=0, tiled=True)])
        cov = lax.psum(covariance_sums(*staged_rows(train)), "dp")
        route = order
    scores = all_scores(route, cov, turned, train, per_query, total_count)
    outgoing = scores.reshape(shard_count * layers, per_query, examples // layers)
    received = lax.all_to_all(outgoing, ("dp", "layer"), split_axis=0, concat_axis=0, tiled=True)
    received = received.reshape(shard_count, layers, per_query, examples // layers)
    return picked(listed, received)


def solution(mesh):
    in_specs = (
        P(("groups", "dp"), "layer", None),
        P(("groups", "dp"), "layer", None),
        P(("groups", "dp"), None),
    )
    out_specs = P(("groups", "dp"), None, "layer")
    return jax.shard_map(shards, mesh=mesh, in_specs=in_specs, out_specs=out_specs, check_vma=False)
```

```python
import functools
import jax
import jax.numpy as jnp
from jax import lax
from jax.experimental import pallas as pl
from jax.experimental.pallas import tpu as pltpu
from jax.sharding import PartitionSpec as P

K_OUT = 64
K_IN = 64
LANES = 128
CHUNK = 64
PIVOT = 4
F32 = jnp.float32
BF16 = jnp.bfloat16
VMEM_LIMIT = 48 * 1024 * 1024
STAGE_VMEM_LIMIT = 50 * 1024 * 1024

NT = (((1,), (1,)), ((), ()))


def low_half(rows):
    return lax.broadcasted_iota(jnp.int32, (rows, LANES), 1) < LANES // 2


def swap_pair(first, second):
    low = low_half(first.shape[0])
    even = jnp.where(low, first, pltpu.roll(second, LANES // 2, 1))
    odd = jnp.where(low, pltpu.roll(first, LANES // 2, 1), second)
    return even, odd


def split(values, terms):
    parts = []
    for _ in range(terms):
        part = values.astype(BF16)
        parts.append(part)
        values = values - part.astype(F32)
    return parts


def stage_kernel(train_ref, in_ref, rows_ref, held, by_in, arrived):
    examples, width = train_ref.shape
    pair = 2 * LANES
    chunks, _, chunk = held.shape
    copies = []
    for g in range(chunks):
        source = train_ref.at[:, pl.ds(g * chunk, chunk)]
        copies.append(pltpu.make_async_copy(source, held.at[g], arrived.at[g]))
        copies[-1].start()
    for m in range(width // pair):
        if m * pair % chunk == 0:
            copies[m * pair // chunk].wait()
        begin = m * pair % chunk
        block = held[m * pair // chunk, :, begin:begin + pair].astype(F32).T
        for k in range(4):
            start = (4 * m + k) * examples
            by_in[:, start:start + examples] = block[k * K_IN:(k + 1) * K_IN, :].astype(BF16)
        for half in range(2):
            for j in range(K_IN // 8):
                first = half * K_IN + j * 8
                both = jnp.concatenate([block[first:first + 8, :], block[first + LANES:first + LANES + 8, :]], axis=0)
                at = half * K_OUT // 2 * 8 + m * 16
                rows_ref[at:at + 16, j * examples:(j + 1) * examples] = both.astype(BF16)
    in_ref[...] = lax.dot_general(by_in[...], by_in[...], NT, preferred_element_type=F32)


def gram_kernel(in_ref, rows_ref, cov_ref):
    count = rows_ref.shape[0]
    every = lax.dot_general(rows_ref[...], rows_ref[...], NT, preferred_element_type=F32)
    row = lax.broadcasted_iota(jnp.int32, (count, count), 0)
    lane = lax.broadcasted_iota(jnp.int32, (count, count), 1)
    every = jnp.where((row & 7) == (lane & 7), every, 0.0)
    summed = jnp.sum(every.reshape(count // 8, 8, count), axis=1)
    lane = lax.broadcasted_iota(jnp.int32, (count, count // 8), 0)
    column = lax.broadcasted_iota(jnp.int32, (count, count // 8), 1)
    merge = jnp.where(lane // 8 == column, 1.0, 0.0).astype(BF16)
    out_sum = sum(jnp.dot(part, merge, preferred_element_type=F32) for part in reversed(split(summed, 3)))
    cov_ref[...] = jnp.concatenate([in_ref[...], out_sum], axis=1)


def staged_rows(train):
    examples, width = train.shape
    chunks = 8 if width % (8 * 2 * LANES) == 0 else 1
    return pl.pallas_call(
        stage_kernel,
        out_shape=(
            jax.ShapeDtypeStruct((K_IN, K_IN), F32),
            jax.ShapeDtypeStruct((8 * K_OUT, K_IN // 8 * examples), BF16),
        ),
        in_specs=[pl.BlockSpec(memory_space=pltpu.HBM)],
        out_specs=(pl.BlockSpec(memory_space=pltpu.VMEM), pl.BlockSpec(memory_space=pltpu.VMEM)),
        scratch_shapes=[
            pltpu.VMEM((chunks, examples, width // chunks), BF16),
            pltpu.VMEM((K_IN, K_OUT * examples), BF16),
            pltpu.SemaphoreType.DMA((chunks,)),
        ],
        compiler_params=pltpu.CompilerParams(vmem_limit_bytes=STAGE_VMEM_LIMIT),
        cost_estimate=pl.CostEstimate(flops=32 * examples * 64**3, bytes_accessed=2 * examples * width, transcendentals=0),
        name="stage_rows",
    )(train)


def covariance_sums(in_sum, rows):
    return pl.pallas_call(
        gram_kernel,
        out_shape=jax.ShapeDtypeStruct((K_OUT, 2 * K_IN), F32),
        in_specs=[pl.BlockSpec(memory_space=pltpu.VMEM), pl.BlockSpec(memory_space=pltpu.VMEM)],
        out_specs=pl.BlockSpec(memory_space=pltpu.VMEM),
        compiler_params=pltpu.CompilerParams(vmem_limit_bytes=VMEM_LIMIT),
        cost_estimate=pl.CostEstimate(flops=2 * rows.shape[0] * rows.size, bytes_accessed=2 * rows.size, transcendentals=0),
        name="covariance",
    )(in_sum, rows)


def turn_kernel(*refs):
    query_refs, out_ref, spread = refs[:-2], refs[-2], refs[-1]
    blocks = out_ref.shape[0] // 2
    half = CHUNK // 2
    for c in range(blocks):
        at = c * CHUNK
        for ref in query_refs:
            count = ref.shape[0]
            spread[at:at + count, :] = ref[:, c * LANES:(c + 1) * LANES].astype(F32)
            at = at + count
    for p in range(half):
        first = spread[pl.ds(p, blocks, stride=CHUNK), :]
        second = spread[pl.ds(p + half, blocks, stride=CHUNK), :]
        even, odd = swap_pair(first, second)
        out_ref[:blocks, p * LANES:(p + 1) * LANES] = even.astype(BF16)
        out_ref[blocks:, p * LANES:(p + 1) * LANES] = odd.astype(BF16)


def turned_queries(queries):
    width = queries[0].shape[1]
    total = sum(part.shape[0] for part in queries)
    steps = total // CHUNK
    if steps == 1:
        in_specs = [pl.BlockSpec(part.shape, lambda step: (0, 0)) for part in queries]
    else:
        in_specs = [pl.BlockSpec((CHUNK, width), lambda step: (step, 0))]
    return pl.pallas_call(
        turn_kernel,
        out_shape=jax.ShapeDtypeStruct((K_OUT, total * K_IN), BF16),
        grid=(steps,),
        in_specs=in_specs,
        out_specs=pl.BlockSpec((K_OUT, CHUNK * K_IN), lambda step: (0, step)),
        scratch_shapes=[pltpu.VMEM((width // LANES * CHUNK, LANES), F32)],
        compiler_params=pltpu.CompilerParams(vmem_limit_bytes=VMEM_LIMIT),
        cost_estimate=pl.CostEstimate(flops=4096 * total * width, bytes_accessed=4 * total * width, transcendentals=0),
        name="turn_queries",
    )(*queries)


def damped(cov, total_count):
    rows = lax.broadcasted_iota(jnp.int32, (K_OUT, LANES), 0)
    lanes = lax.broadcasted_iota(jnp.int32, (K_OUT, LANES), 1)
    low = lanes < K_IN
    diagonal = rows == jnp.where(low, lanes, lanes - K_IN)
    cov = cov * (1.0 / total_count)
    on_diagonal = jnp.sum(jnp.where(diagonal, cov, 0.0), axis=0, keepdims=True)
    low_row = low_half(1)
    in_mean = jnp.sum(jnp.where(low_row, on_diagonal, 0.0), axis=1, keepdims=True) / K_IN
    out_mean = jnp.sum(jnp.where(low_row, 0.0, on_diagonal), axis=1, keepdims=True) / K_OUT
    scale = jnp.where(low_row, 1.0 / in_mean, 1.0)
    added = jnp.where(low_row, 0.1, 0.1 * out_mean)
    return cov * scale + jnp.where(diagonal, added, 0.0)


def inverses(matrix):
    size = matrix.shape[0]
    sub = 8
    lanes = lax.broadcasted_iota(jnp.int32, (sub, LANES), 1)
    offset = jnp.where(lanes < size, 0, size)
    place = lanes - offset
    row = lax.broadcasted_iota(jnp.int32, (sub, LANES), 0)
    tiles = [matrix[k:k + sub, :] for k in range(0, size, sub)]

    def spread_row(values, at):
        return jnp.broadcast_to(values[at:at + 1, :], (sub, LANES))

    def column(values, lane):
        return jnp.take_along_axis(values, offset + lane, axis=1, mode="promise_in_bounds")

    for begin in range(0, size, PIVOT):
        owner, first_row = begin // sub, begin % sub
        inside = (place >= begin) & (place < begin + PIVOT)
        columns = [[column(tile, begin + a) for a in range(PIVOT)] for tile in tiles]
        p = [[spread_row(columns[owner][b], first_row + a) for b in range(PIVOT)] for a in range(PIVOT)]
        r = []
        for a in range(PIVOT):
            unit = jnp.where(place == begin + a, 1.0, 0.0)
            r.append(jnp.where(inside, unit, spread_row(tiles[owner], first_row + a)))
        det = 1.0 / (p[0][0] * p[1][1] - p[0][1] * p[1][0])
        e = [[p[1][1] * det, -p[0][1] * det], [-p[1][0] * det, p[0][0] * det]]
        u = [[e[a][0] * p[0][b] + e[a][1] * p[1][b] for b in (2, 3)] for a in (0, 1)]
        s = [[p[a][b + 2] - (p[a][0] * u[0][b] + p[a][1] * u[1][b]) for b in (0, 1)] for a in (2, 3)]
        det = 1.0 / (s[0][0] * s[1][1] - s[0][1] * s[1][0])
        f = [[s[1][1] * det, -s[0][1] * det], [-s[1][0] * det, s[0][0] * det]]
        w = [e[a][0] * r[0] + e[a][1] * r[1] for a in (0, 1)]
        t = [r[a] - (p[a][0] * w[0] + p[a][1] * w[1]) for a in (2, 3)]
        last = [f[a][0] * t[0] + f[a][1] * t[1] for a in (0, 1)]
        first = [w[a] - (u[a][0] * last[0] + u[a][1] * last[1]) for a in (0, 1)]
        solved = first + last
        for k in range(len(tiles)):
            rest = jnp.where(inside, 0.0, tiles[k])
            part = [columns[k][a] * solved[a] for a in range(PIVOT)]
            rest = (rest - (part[0] + part[1])) - (part[2] + part[3])
            if k == owner:
                for a in range(PIVOT):
                    rest = jnp.where(row == first_row + a, solved[a], rest)
            tiles[k] = rest
    return jnp.concatenate(tiles, axis=0)


def score_kernel(total_count, route_ref, cov_ref, turned_ref, train_ref, out_ref, left, right, solved, wide, ready):
    blocks = K_OUT // 2
    half = CHUNK // 2
    step = pl.program_id(0)

    @pl.when(step == 0)
    def _():
        inverse = inverses(damped(cov_ref[...], total_count))
        turned = pltpu.roll(inverse, LANES // 2, 1)
        low = low_half(K_OUT)
        left[...] = jnp.concatenate(split(turned[:, :K_OUT], 3), axis=1)
        double = jnp.concatenate([jnp.where(low, inverse, 0.0), jnp.where(low, 0.0, turned)], axis=0)
        high, small = split(double, 2)
        right[:LANES, :LANES] = high
        right[:LANES, LANES:] = small
        right[LANES:, :LANES] = high
        right[LANES:, LANES:] = jnp.zeros_like(small)

    group = 4
    for g in range(half // group):
        block = turned_ref[:, g * group * LANES:(g + 1) * group * LANES]
        tall = jnp.concatenate([block, block, block], axis=0)
        once = jnp.dot(left[...], tall, preferred_element_type=F32)
        for k in range(group):
            high, small = split(once[:, k * LANES:(k + 1) * LANES], 2)
            at = (g * group + k) * K_OUT
            wide[at:at + K_OUT, :LANES] = high
            wide[at:at + K_OUT, LANES:] = small
    twice = jnp.dot(wide[...], right[...], preferred_element_type=F32)
    solved[...] = twice[:, :LANES] + twice[:, LANES:]
    for c in range(blocks):
        first = solved[pl.ds(c, half, stride=K_OUT), :]
        second = solved[pl.ds(c + blocks, half, stride=K_OUT), :]
        even, odd = swap_pair(first, second)
        ready[:half, c * LANES:(c + 1) * LANES] = even.astype(BF16)
        ready[half:, c * LANES:(c + 1) * LANES] = odd.astype(BF16)
    scores = lax.dot_general(ready[...], train_ref[...], NT, preferred_element_type=F32)
    per_query = out_ref.shape[2]
    parts = out_ref.shape[1]
    for s in range(CHUNK // per_query):
        owner = route_ref[step * (CHUNK // per_query) + s]
        for part in range(parts):
            piece = scores[s * per_query:(s + 1) * per_query, part * LANES:(part + 1) * LANES]
            out_ref[owner, part, :, :] = piece


def all_scores(route, cov, turned, train, per_query, total_count):
    shard_count = route.shape[0]
    examples, width = train.shape
    steps = shard_count * per_query // CHUNK
    parts = examples // LANES
    return pl.pallas_call(
        functools.partial(score_kernel, total_count),
        out_shape=jax.ShapeDtypeStruct((shard_count, parts, per_query, LANES), F32),
        grid=(steps,),
        in_specs=[
            pl.BlockSpec(memory_space=pltpu.SMEM),
            pl.BlockSpec((K_OUT, 2 * K_IN), lambda step: (0, 0)),
            pl.BlockSpec((K_OUT, CHUNK * K_IN), lambda step: (0, step)),
            pl.BlockSpec((examples, width), lambda step: (0, 0)),
        ],
        out_specs=pl.BlockSpec((shard_count, parts, per_query, LANES), lambda step: (0, 0, 0, 0)),
        scratch_shapes=[
            pltpu.VMEM((K_OUT, 3 * K_OUT), BF16),
            pltpu.VMEM((2 * LANES, 2 * LANES), BF16),
            pltpu.VMEM((CHUNK // 2 * K_OUT, LANES), F32),
            pltpu.VMEM((CHUNK // 2 * K_OUT, 2 * LANES), BF16),
            pltpu.VMEM((CHUNK, width), BF16),
        ],
        compiler_params=pltpu.CompilerParams(vmem_limit_bytes=VMEM_LIMIT),
        cost_estimate=pl.CostEstimate(
            flops=2 * shard_count * per_query * width * (examples + 128), bytes_accessed=2 * examples * width, transcendentals=0
        ),
        name="solve_and_score",
    )(route, cov, turned, train)


def exchange(values, distance, count):
    return lax.ppermute(values, "dp", [(k, k ^ distance) for k in range(count)])


def shards(train_grads, query_grads, listed):
    shard_count = lax.axis_size("dp")
    layers = lax.axis_size("layer")
    own_index = lax.axis_index("dp").astype(jnp.int32)
    examples = train_grads.shape[0]
    per_query = query_grads.shape[0]
    train = train_grads.reshape(examples, train_grads.shape[2])
    own_queries = query_grads.reshape(per_query, query_grads.shape[2])
    total_count = float(examples * shard_count)
    order = jnp.arange(shard_count, dtype=jnp.int32)
    if shard_count == 8:
        far = exchange(own_queries, 4, shard_count)
        cov = covariance_sums(*staged_rows(train))
        far, _ = lax.optimization_barrier((far, cov))
        column = jnp.concatenate([own_queries, far], axis=0)
        cov = cov + exchange(cov, 1, shard_count)
        near = exchange(column, 2, shard_count)
        near, cov = lax.optimization_barrier((near, cov))
        cov = cov + exchange(cov, 4, shard_count)
        column = jnp.concatenate([column, near], axis=0)
        queries = [column, exchange(column, 1, shard_count)]
        last = exchange(cov, 2, shard_count)
        turned, cov = lax.optimization_barrier((turned_queries(queries), cov))
        cov = cov + last
        order = jnp.array([0, 4, 2, 6, 1, 5, 3, 7], jnp.int32)
        route = own_index ^ order
    else:
        turned = turned_queries([lax.all_gather(own_queries, "dp", axis=0, tiled=True)])
        cov = lax.psum(covariance_sums(*staged_rows(train)), "dp")
        route = order
    scores = all_scores(route, cov, turned, train, per_query, total_count)
    outgoing = scores.reshape(shard_count * layers, per_query, examples // layers)
    wanted = listed[0][:, None] == jnp.arange(shard_count, dtype=jnp.int32)[None, :]
    wanted, outgoing = lax.optimization_barrier((wanted, outgoing))
    received = lax.all_to_all(outgoing, ("dp", "layer"), split_axis=0, concat_axis=0, tiled=True)
    received = received.reshape(1, shard_count, layers, per_query, examples // layers)
    return jnp.sum(jnp.where(wanted[:, :, None, None, None], received, 0.0), axis=(1, 2))


def solution(mesh):
    in_specs = (
        P(("groups", "dp"), "layer", None),
        P(("groups", "dp"), "layer", None),
        P(("groups", "dp"), None),
    )
    out_specs = P(("groups", "dp"), None, "layer")
    return jax.shard_map(shards, mesh=mesh, in_specs=in_specs, out_specs=out_specs, check_vma=False)
```

```python
import functools
import jax
import jax.numpy as jnp
from jax import lax
from jax.experimental import pallas as pl
from jax.experimental.pallas import tpu as pltpu
from jax.sharding import PartitionSpec as P

K_OUT = 64
K_IN = 64
LANES = 128
CHUNK = 64
PIVOT = 4
F32 = jnp.float32
BF16 = jnp.bfloat16
VMEM_LIMIT = 48 * 1024 * 1024
STAGE_VMEM_LIMIT = 50 * 1024 * 1024

NT = (((1,), (1,)), ((), ()))


def low_half(rows):
    return lax.broadcasted_iota(jnp.int32, (rows, LANES), 1) < LANES // 2


def swap_pair(first, second):
    low = low_half(first.shape[0])
    even = jnp.where(low, first, pltpu.roll(second, LANES // 2, 1))
    odd = jnp.where(low, pltpu.roll(first, LANES // 2, 1), second)
    return even, odd


def split(values, terms):
    parts = []
    for _ in range(terms):
        part = values.astype(BF16)
        parts.append(part)
        values = values - part.astype(F32)
    return parts


def stage_kernel(train_ref, in_ref, rows_ref, held, by_in, arrived):
    examples, width = train_ref.shape
    pair = 2 * LANES
    chunks, _, chunk = held.shape
    copies = []
    for g in range(chunks):
        source = train_ref.at[:, pl.ds(g * chunk, chunk)]
        copies.append(pltpu.make_async_copy(source, held.at[g], arrived.at[g]))
        copies[-1].start()
    for m in range(width // pair):
        if m * pair % chunk == 0:
            copies[m * pair // chunk].wait()
        begin = m * pair % chunk
        block = held[m * pair // chunk, :, begin:begin + pair].astype(F32).T
        for k in range(4):
            start = (4 * m + k) * examples
            by_in[:, start:start + examples] = block[k * K_IN:(k + 1) * K_IN, :].astype(BF16)
        for half in range(2):
            for j in range(K_IN // 8):
                first = half * K_IN + j * 8
                both = jnp.concatenate([block[first:first + 8, :], block[first + LANES:first + LANES + 8, :]], axis=0)
                at = half * K_OUT // 2 * 8 + m * 16
                rows_ref[at:at + 16, j * examples:(j + 1) * examples] = both.astype(BF16)
    in_ref[...] = lax.dot_general(by_in[...], by_in[...], NT, preferred_element_type=F32)


def gram_kernel(in_ref, rows_ref, cov_ref):
    count = rows_ref.shape[0]
    every = lax.dot_general(rows_ref[...], rows_ref[...], NT, preferred_element_type=F32)
    row = lax.broadcasted_iota(jnp.int32, (count, count), 0)
    lane = lax.broadcasted_iota(jnp.int32, (count, count), 1)
    every = jnp.where((row & 7) == (lane & 7), every, 0.0)
    summed = jnp.sum(every.reshape(count // 8, 8, count), axis=1)
    lane = lax.broadcasted_iota(jnp.int32, (count, count // 8), 0)
    column = lax.broadcasted_iota(jnp.int32, (count, count // 8), 1)
    merge = jnp.where(lane // 8 == column, 1.0, 0.0).astype(BF16)
    out_sum = sum(jnp.dot(part, merge, preferred_element_type=F32) for part in reversed(split(summed, 3)))
    cov_ref[...] = jnp.concatenate([in_ref[...], out_sum], axis=1)


def staged_rows(train):
    examples, width = train.shape
    chunks = 8 if width % (8 * 2 * LANES) == 0 else 1
    return pl.pallas_call(
        stage_kernel,
        out_shape=(
            jax.ShapeDtypeStruct((K_IN, K_IN), F32),
            jax.ShapeDtypeStruct((8 * K_OUT, K_IN // 8 * examples), BF16),
        ),
        in_specs=[pl.BlockSpec(memory_space=pltpu.HBM)],
        out_specs=(pl.BlockSpec(memory_space=pltpu.VMEM), pl.BlockSpec(memory_space=pltpu.VMEM)),
        scratch_shapes=[
            pltpu.VMEM((chunks, examples, width // chunks), BF16),
            pltpu.VMEM((K_IN, K_OUT * examples), BF16),
            pltpu.SemaphoreType.DMA((chunks,)),
        ],
        compiler_params=pltpu.CompilerParams(vmem_limit_bytes=STAGE_VMEM_LIMIT),
        cost_estimate=pl.CostEstimate(flops=32 * examples * 64**3, bytes_accessed=2 * examples * width, transcendentals=0),
        name="stage_rows",
    )(train)


def covariance_sums(in_sum, rows):
    return pl.pallas_call(
        gram_kernel,
        out_shape=jax.ShapeDtypeStruct((K_OUT, 2 * K_IN), F32),
        in_specs=[pl.BlockSpec(memory_space=pltpu.VMEM), pl.BlockSpec(memory_space=pltpu.VMEM)],
        out_specs=pl.BlockSpec(memory_space=pltpu.VMEM),
        compiler_params=pltpu.CompilerParams(vmem_limit_bytes=VMEM_LIMIT),
        cost_estimate=pl.CostEstimate(flops=2 * rows.shape[0] * rows.size, bytes_accessed=2 * rows.size, transcendentals=0),
        name="covariance",
    )(in_sum, rows)


def turn_kernel(*refs):
    query_refs, out_ref, spread = refs[:-2], refs[-2], refs[-1]
    blocks = out_ref.shape[0] // 2
    half = CHUNK // 2
    for c in range(blocks):
        at = c * CHUNK
        for ref in query_refs:
            count = ref.shape[0]
            spread[at:at + count, :] = ref[:, c * LANES:(c + 1) * LANES].astype(F32)
            at = at + count
    for p in range(half):
        first = spread[pl.ds(p, blocks, stride=CHUNK), :]
        second = spread[pl.ds(p + half, blocks, stride=CHUNK), :]
        even, odd = swap_pair(first, second)
        out_ref[:blocks, p * LANES:(p + 1) * LANES] = even.astype(BF16)
        out_ref[blocks:, p * LANES:(p + 1) * LANES] = odd.astype(BF16)


def turned_queries(queries):
    width = queries[0].shape[1]
    total = sum(part.shape[0] for part in queries)
    steps = total // CHUNK
    if steps == 1:
        in_specs = [pl.BlockSpec(part.shape, lambda step: (0, 0)) for part in queries]
    else:
        in_specs = [pl.BlockSpec((CHUNK, width), lambda step: (step, 0))]
    return pl.pallas_call(
        turn_kernel,
        out_shape=jax.ShapeDtypeStruct((K_OUT, total * K_IN), BF16),
        grid=(steps,),
        in_specs=in_specs,
        out_specs=pl.BlockSpec((K_OUT, CHUNK * K_IN), lambda step: (0, step)),
        scratch_shapes=[pltpu.VMEM((width // LANES * CHUNK, LANES), F32)],
        compiler_params=pltpu.CompilerParams(vmem_limit_bytes=VMEM_LIMIT),
        cost_estimate=pl.CostEstimate(flops=4096 * total * width, bytes_accessed=4 * total * width, transcendentals=0),
        name="turn_queries",
    )(*queries)


def damped(cov, total_count):
    rows = lax.broadcasted_iota(jnp.int32, (K_OUT, LANES), 0)
    lanes = lax.broadcasted_iota(jnp.int32, (K_OUT, LANES), 1)
    low = lanes < K_IN
    diagonal = rows == jnp.where(low, lanes, lanes - K_IN)
    cov = cov * (1.0 / total_count)
    on_diagonal = jnp.sum(jnp.where(diagonal, cov, 0.0), axis=0, keepdims=True)
    low_row = low_half(1)
    in_mean = jnp.sum(jnp.where(low_row, on_diagonal, 0.0), axis=1, keepdims=True) / K_IN
    out_mean = jnp.sum(jnp.where(low_row, 0.0, on_diagonal), axis=1, keepdims=True) / K_OUT
    scale = jnp.where(low_row, 1.0 / in_mean, 1.0)
    added = jnp.where(low_row, 0.1, 0.1 * out_mean)
    return cov * scale + jnp.where(diagonal, added, 0.0)


def inverses(matrix):
    size = matrix.shape[0]
    sub = 8
    lanes = lax.broadcasted_iota(jnp.int32, (sub, LANES), 1)
    offset = jnp.where(lanes < size, 0, size)
    place = lanes - offset
    row = lax.broadcasted_iota(jnp.int32, (sub, LANES), 0)
    tiles = [matrix[k:k + sub, :] for k in range(0, size, sub)]

    def spread_row(values, at):
        return jnp.broadcast_to(values[at:at + 1, :], (sub, LANES))

    def column(values, lane):
        return jnp.take_along_axis(values, offset + lane, axis=1, mode="promise_in_bounds")

    for begin in range(0, size, PIVOT):
        owner, first_row = begin // sub, begin % sub
        inside = (place >= begin) & (place < begin + PIVOT)
        columns = [[column(tile, begin + a) for a in range(PIVOT)] for tile in tiles]
        p = [[spread_row(columns[owner][b], first_row + a) for b in range(PIVOT)] for a in range(PIVOT)]
        r = []
        for a in range(PIVOT):
            unit = jnp.where(place == begin + a, 1.0, 0.0)
            r.append(jnp.where(inside, unit, spread_row(tiles[owner], first_row + a)))
        det = 1.0 / (p[0][0] * p[1][1] - p[0][1] * p[1][0])
        e = [[p[1][1] * det, -p[0][1] * det], [-p[1][0] * det, p[0][0] * det]]
        u = [[e[a][0] * p[0][b] + e[a][1] * p[1][b] for b in (2, 3)] for a in (0, 1)]
        s = [[p[a][b + 2] - (p[a][0] * u[0][b] + p[a][1] * u[1][b]) for b in (0, 1)] for a in (2, 3)]
        det = 1.0 / (s[0][0] * s[1][1] - s[0][1] * s[1][0])
        f = [[s[1][1] * det, -s[0][1] * det], [-s[1][0] * det, s[0][0] * det]]
        w = [e[a][0] * r[0] + e[a][1] * r[1] for a in (0, 1)]
        t = [r[a] - (p[a][0] * w[0] + p[a][1] * w[1]) for a in (2, 3)]
        last = [f[a][0] * t[0] + f[a][1] * t[1] for a in (0, 1)]
        first = [w[a] - (u[a][0] * last[0] + u[a][1] * last[1]) for a in (0, 1)]
        solved = first + last
        for k in range(len(tiles)):
            rest = jnp.where(inside, 0.0, tiles[k])
            part = [columns[k][a] * solved[a] for a in range(PIVOT)]
            rest = (rest - (part[0] + part[1])) - (part[2] + part[3])
            if k == owner:
                for a in range(PIVOT):
                    rest = jnp.where(row == first_row + a, solved[a], rest)
            tiles[k] = rest
    return jnp.concatenate(tiles, axis=0)


def score_kernel(total_count, route_ref, cov_ref, turned_ref, train_ref, out_ref, left, right, solved, wide, ready):
    blocks = K_OUT // 2
    half = CHUNK // 2
    step = pl.program_id(0)

    @pl.when(step == 0)
    def _():
        inverse = inverses(damped(cov_ref[...], total_count))
        turned = pltpu.roll(inverse, LANES // 2, 1)
        low = low_half(K_OUT)
        left[...] = jnp.concatenate(split(turned[:, :K_OUT], 3), axis=1)
        double = jnp.concatenate([jnp.where(low, inverse, 0.0), jnp.where(low, 0.0, turned)], axis=0)
        high, small = split(double, 2)
        right[:LANES, :LANES] = high
        right[:LANES, LANES:] = small
        right[LANES:, :LANES] = high
        right[LANES:, LANES:] = jnp.zeros_like(small)

    group = 4
    for g in range(half // group):
        block = turned_ref[:, g * group * LANES:(g + 1) * group * LANES]
        tall = jnp.concatenate([block, block, block], axis=0)
        once = jnp.dot(left[...], tall, preferred_element_type=F32)
        for k in range(group):
            high, small = split(once[:, k * LANES:(k + 1) * LANES], 2)
            at = (g * group + k) * K_OUT
            wide[at:at + K_OUT, :LANES] = high
            wide[at:at + K_OUT, LANES:] = small
    twice = jnp.dot(wide[...], right[...], preferred_element_type=F32)
    solved[...] = twice[:, :LANES] + twice[:, LANES:]
    for c in range(blocks):
        first = solved[pl.ds(c, half, stride=K_OUT), :]
        second = solved[pl.ds(c + blocks, half, stride=K_OUT), :]
        even, odd = swap_pair(first, second)
        ready[:half, c * LANES:(c + 1) * LANES] = even.astype(BF16)
        ready[half:, c * LANES:(c + 1) * LANES] = odd.astype(BF16)
    scores = lax.dot_general(ready[...], train_ref[...], NT, preferred_element_type=F32)
    per_query = out_ref.shape[2]
    parts = out_ref.shape[1]
    for s in range(CHUNK // per_query):
        owner = route_ref[step * (CHUNK // per_query) + s]
        for part in range(parts):
            piece = scores[s * per_query:(s + 1) * per_query, part * LANES:(part + 1) * LANES]
            out_ref[owner, part, :, :] = piece.astype(BF16)


def all_scores(route, cov, turned, train, per_query, total_count):
    shard_count = route.shape[0]
    examples, width = train.shape
    steps = shard_count * per_query // CHUNK
    parts = examples // LANES
    return pl.pallas_call(
        functools.partial(score_kernel, total_count),
        out_shape=jax.ShapeDtypeStruct((shard_count, parts, per_query, LANES), BF16),
        grid=(steps,),
        in_specs=[
            pl.BlockSpec(memory_space=pltpu.SMEM),
            pl.BlockSpec((K_OUT, 2 * K_IN), lambda step: (0, 0)),
            pl.BlockSpec((K_OUT, CHUNK * K_IN), lambda step: (0, step)),
            pl.BlockSpec((examples, width), lambda step: (0, 0)),
        ],
        out_specs=pl.BlockSpec((shard_count, parts, per_query, LANES), lambda step: (0, 0, 0, 0)),
        scratch_shapes=[
            pltpu.VMEM((K_OUT, 3 * K_OUT), BF16),
            pltpu.VMEM((2 * LANES, 2 * LANES), BF16),
            pltpu.VMEM((CHUNK // 2 * K_OUT, LANES), F32),
            pltpu.VMEM((CHUNK // 2 * K_OUT, 2 * LANES), BF16),
            pltpu.VMEM((CHUNK, width), BF16),
        ],
        compiler_params=pltpu.CompilerParams(vmem_limit_bytes=VMEM_LIMIT),
        cost_estimate=pl.CostEstimate(
            flops=2 * shard_count * per_query * width * (examples + 128), bytes_accessed=2 * examples * width, transcendentals=0
        ),
        name="solve_and_score",
    )(route, cov, turned, train)


def exchange(values, distance, count):
    return lax.ppermute(values, "dp", [(k, k ^ distance) for k in range(count)])


def shards(train_grads, query_grads, listed):
    shard_count = lax.axis_size("dp")
    layers = lax.axis_size("layer")
    own_index = lax.axis_index("dp").astype(jnp.int32)
    examples = train_grads.shape[0]
    per_query = query_grads.shape[0]
    train = train_grads.reshape(examples, train_grads.shape[2])
    own_queries = query_grads.reshape(per_query, query_grads.shape[2])
    total_count = float(examples * shard_count)
    order = jnp.arange(shard_count, dtype=jnp.int32)
    if shard_count == 8:
        column = [exchange(own_queries, distance, shard_count) for distance in (4, 6, 2)]
        cov = covariance_sums(*staged_rows(train))
        column, cov = lax.optimization_barrier((column, cov))
        column = jnp.concatenate([own_queries] + column, axis=0)
        queries = [column, exchange(column, 1, shard_count)]
        for distance in (4, 2):
            cov = cov + exchange(cov, distance, shard_count)
        last = exchange(cov, 1, shard_count)
        turned, cov = lax.optimization_barrier((turned_queries(queries), cov))
        cov = cov + last
        order = jnp.array([0, 4, 6, 2, 1, 5, 7, 3], jnp.int32)
        route = own_index ^ order
    else:
        turned = turned_queries([lax.all_gather(own_queries, "dp", axis=0, tiled=True)])
        cov = lax.psum(covariance_sums(*staged_rows(train)), "dp")
        route = order
    scores = all_scores(route, cov, turned, train, per_query, total_count)
    outgoing = scores.reshape(shard_count * layers, per_query, examples // layers)
    wanted = listed[0][:, None] == jnp.arange(shard_count, dtype=jnp.int32)[None, :]
    wanted, outgoing = lax.optimization_barrier((wanted, outgoing))
    received = lax.all_to_all(outgoing, ("dp", "layer"), split_axis=0, concat_axis=0, tiled=True)
    received = received.reshape(1, shard_count, layers, per_query, examples // layers).astype(F32)
    return jnp.sum(jnp.where(wanted[:, :, None, None, None], received, 0.0), axis=(1, 2))


def solution(mesh):
    in_specs = (
        P(("groups", "dp"), "layer", None),
        P(("groups", "dp"), "layer", None),
        P(("groups", "dp"), None),
    )
    out_specs = P(("groups", "dp"), None, "layer")
    return jax.shard_map(shards, mesh=mesh, in_specs=in_specs, out_specs=out_specs, check_vma=False)
```

```python
import functools
import jax
import jax.numpy as jnp
from jax import lax
from jax.experimental import pallas as pl
from jax.experimental.pallas import tpu as pltpu
from jax.sharding import PartitionSpec as P

K_OUT = 64
K_IN = 64
LANES = 128
CHUNK = 64
HALF = CHUNK // 2
PIVOT = 4
F32 = jnp.float32
BF16 = jnp.bfloat16
VMEM_LIMIT = 48 * 1024 * 1024
INVERSE_COST = 2 * 10**9
STAGE_VMEM_LIMIT = 50 * 1024 * 1024

NT = (((1,), (1,)), ((), ()))


def low_half(rows):
    return lax.broadcasted_iota(jnp.int32, (rows, LANES), 1) < LANES // 2


def swap_pair(first, second):
    low = low_half(first.shape[0])
    even = jnp.where(low, first, pltpu.roll(second, LANES // 2, 1))
    odd = jnp.where(low, pltpu.roll(first, LANES // 2, 1), second)
    return even, odd


def split(values, terms):
    parts = []
    for _ in range(terms):
        part = values.astype(BF16)
        parts.append(part)
        values = values - part.astype(F32)
    return parts


def stage_kernel(train_ref, in_ref, rows_ref, held, by_in, arrived):
    examples, width = train_ref.shape
    pair = 2 * LANES
    chunks, _, chunk = held.shape
    copies = []
    for g in range(chunks):
        source = train_ref.at[:, pl.ds(g * chunk, chunk)]
        copies.append(pltpu.make_async_copy(source, held.at[g], arrived.at[g]))
        copies[-1].start()
    for m in range(width // pair):
        if m * pair % chunk == 0:
            copies[m * pair // chunk].wait()
        begin = m * pair % chunk
        block = held[m * pair // chunk, :, begin:begin + pair].astype(F32).T
        for k in range(4):
            start = (4 * m + k) * examples
            by_in[:, start:start + examples] = block[k * K_IN:(k + 1) * K_IN, :].astype(BF16)
        for half in range(2):
            for j in range(K_IN // 8):
                first = half * K_IN + j * 8
                both = jnp.concatenate([block[first:first + 8, :], block[first + LANES:first + LANES + 8, :]], axis=0)
                at = half * K_OUT // 2 * 8 + m * 16
                rows_ref[at:at + 16, j * examples:(j + 1) * examples] = both.astype(BF16)
    in_ref[...] = lax.dot_general(by_in[...], by_in[...], NT, preferred_element_type=F32)


def gram_kernel(in_ref, rows_ref, cov_ref):
    count = rows_ref.shape[0]
    every = lax.dot_general(rows_ref[...], rows_ref[...], NT, preferred_element_type=F32)
    row = lax.broadcasted_iota(jnp.int32, (count, count), 0)
    lane = lax.broadcasted_iota(jnp.int32, (count, count), 1)
    every = jnp.where((row & 7) == (lane & 7), every, 0.0)
    summed = jnp.sum(every.reshape(count // 8, 8, count), axis=1)
    lane = lax.broadcasted_iota(jnp.int32, (count, count // 8), 0)
    column = lax.broadcasted_iota(jnp.int32, (count, count // 8), 1)
    merge = jnp.where(lane // 8 == column, 1.0, 0.0).astype(BF16)
    out_sum = sum(jnp.dot(part, merge, preferred_element_type=F32) for part in reversed(split(summed, 3)))
    cov_ref[...] = jnp.concatenate([in_ref[...], out_sum], axis=1)


def staged_rows(train):
    examples, width = train.shape
    chunks = 8 if width % (8 * 2 * LANES) == 0 else 1
    return pl.pallas_call(
        stage_kernel,
        out_shape=(
            jax.ShapeDtypeStruct((K_IN, K_IN), F32),
            jax.ShapeDtypeStruct((8 * K_OUT, K_IN // 8 * examples), BF16),
        ),
        in_specs=[pl.BlockSpec(memory_space=pltpu.HBM)],
        out_specs=(pl.BlockSpec(memory_space=pltpu.VMEM), pl.BlockSpec(memory_space=pltpu.VMEM)),
        scratch_shapes=[
            pltpu.VMEM((chunks, examples, width // chunks), BF16),
            pltpu.VMEM((K_IN, K_OUT * examples), BF16),
            pltpu.SemaphoreType.DMA((chunks,)),
        ],
        compiler_params=pltpu.CompilerParams(vmem_limit_bytes=STAGE_VMEM_LIMIT),
        cost_estimate=pl.CostEstimate(flops=32 * examples * 64**3, bytes_accessed=2 * examples * width, transcendentals=0),
        name="stage_rows",
    )(train)


def covariance_sums(in_sum, rows):
    return pl.pallas_call(
        gram_kernel,
        out_shape=jax.ShapeDtypeStruct((K_OUT, 2 * K_IN), F32),
        in_specs=[pl.BlockSpec(memory_space=pltpu.VMEM), pl.BlockSpec(memory_space=pltpu.VMEM)],
        out_specs=pl.BlockSpec(memory_space=pltpu.VMEM),
        compiler_params=pltpu.CompilerParams(vmem_limit_bytes=VMEM_LIMIT),
        cost_estimate=pl.CostEstimate(flops=2 * rows.shape[0] * rows.size, bytes_accessed=2 * rows.size, transcendentals=0),
        name="covariance",
    )(in_sum, rows)


def turn_kernel(query_ref, out_ref, spread):
    count, width = query_ref.shape
    blocks = width // LANES
    pairs = count // 2
    for c in range(blocks):
        spread[c * count:(c + 1) * count, :] = query_ref[:, c * LANES:(c + 1) * LANES].astype(F32)
    for p in range(pairs):
        first = spread[pl.ds(p, blocks, stride=count), :]
        second = spread[pl.ds(p + pairs, blocks, stride=count), :]
        even, odd = swap_pair(first, second)
        out_ref[:blocks, p * LANES:(p + 1) * LANES] = even.astype(BF16)
        out_ref[blocks:, p * LANES:(p + 1) * LANES] = odd.astype(BF16)


def turned_queries(queries):
    total, width = queries.shape
    return pl.pallas_call(
        turn_kernel,
        out_shape=jax.ShapeDtypeStruct((K_OUT, total * K_IN), BF16),
        grid=(total // HALF,),
        in_specs=[pl.BlockSpec((HALF, width), lambda step: (step, 0))],
        out_specs=pl.BlockSpec((K_OUT, HALF * K_IN), lambda step: (0, step)),
        scratch_shapes=[pltpu.VMEM((width // LANES * HALF, LANES), F32)],
        compiler_params=pltpu.CompilerParams(vmem_limit_bytes=VMEM_LIMIT),
        cost_estimate=pl.CostEstimate(flops=4096 * total * width, bytes_accessed=4 * total * width, transcendentals=0),
        name="turn_queries",
    )(queries)


def damped(cov, total_count):
    rows = lax.broadcasted_iota(jnp.int32, (K_OUT, LANES), 0)
    lanes = lax.broadcasted_iota(jnp.int32, (K_OUT, LANES), 1)
    low = lanes < K_IN
    diagonal = rows == jnp.where(low, lanes, lanes - K_IN)
    cov = cov * (1.0 / total_count)
    on_diagonal = jnp.sum(jnp.where(diagonal, cov, 0.0), axis=0, keepdims=True)
    low_row = low_half(1)
    in_mean = jnp.sum(jnp.where(low_row, on_diagonal, 0.0), axis=1, keepdims=True) / K_IN
    out_mean = jnp.sum(jnp.where(low_row, 0.0, on_diagonal), axis=1, keepdims=True) / K_OUT
    scale = jnp.where(low_row, 1.0 / in_mean, 1.0)
    added = jnp.where(low_row, 0.1, 0.1 * out_mean)
    return cov * scale + jnp.where(diagonal, added, 0.0)


def inverses(matrix):
    size = matrix.shape[0]
    sub = 8
    lanes = lax.broadcasted_iota(jnp.int32, (sub, LANES), 1)
    offset = jnp.where(lanes < size, 0, size)
    place = lanes - offset
    row = lax.broadcasted_iota(jnp.int32, (sub, LANES), 0)
    tiles = [matrix[k:k + sub, :] for k in range(0, size, sub)]

    def spread_row(values, at):
        return jnp.broadcast_to(values[at:at + 1, :], (sub, LANES))

    def column(values, lane):
        return jnp.take_along_axis(values, offset + lane, axis=1, mode="promise_in_bounds")

    for begin in range(0, size, PIVOT):
        owner, first_row = begin // sub, begin % sub
        inside = (place >= begin) & (place < begin + PIVOT)
        columns = [[column(tile, begin + a) for a in range(PIVOT)] for tile in tiles]
        p = [[spread_row(columns[owner][b], first_row + a) for b in range(PIVOT)] for a in range(PIVOT)]
        r = []
        for a in range(PIVOT):
            unit = jnp.where(place == begin + a, 1.0, 0.0)
            r.append(jnp.where(inside, unit, spread_row(tiles[owner], first_row + a)))
        det = 1.0 / (p[0][0] * p[1][1] - p[0][1] * p[1][0])
        e = [[p[1][1] * det, -p[0][1] * det], [-p[1][0] * det, p[0][0] * det]]
        u = [[e[a][0] * p[0][b] + e[a][1] * p[1][b] for b in (2, 3)] for a in (0, 1)]
        s = [[p[a][b + 2] - (p[a][0] * u[0][b] + p[a][1] * u[1][b]) for b in (0, 1)] for a in (2, 3)]
        det = 1.0 / (s[0][0] * s[1][1] - s[0][1] * s[1][0])
        f = [[s[1][1] * det, -s[0][1] * det], [-s[1][0] * det, s[0][0] * det]]
        w = [e[a][0] * r[0] + e[a][1] * r[1] for a in (0, 1)]
        t = [r[a] - (p[a][0] * w[0] + p[a][1] * w[1]) for a in (2, 3)]
        last = [f[a][0] * t[0] + f[a][1] * t[1] for a in (0, 1)]
        first = [w[a] - (u[a][0] * last[0] + u[a][1] * last[1]) for a in (0, 1)]
        solved = first + last
        for k in range(len(tiles)):
            rest = jnp.where(inside, 0.0, tiles[k])
            part = [columns[k][a] * solved[a] for a in range(PIVOT)]
            rest = (rest - (part[0] + part[1])) - (part[2] + part[3])
            if k == owner:
                for a in range(PIVOT):
                    rest = jnp.where(row == first_row + a, solved[a], rest)
            tiles[k] = rest
    return jnp.concatenate(tiles, axis=0)


def inverse_kernel(total_count, cov_ref, left_ref, right_ref):
    inverse = inverses(damped(cov_ref[...], total_count))
    turned = pltpu.roll(inverse, LANES // 2, 1)
    low = low_half(K_OUT)
    left_ref[...] = jnp.concatenate(split(turned[:, :K_OUT], 3), axis=1)
    double = jnp.concatenate([jnp.where(low, inverse, 0.0), jnp.where(low, 0.0, turned)], axis=0)
    high, small = split(double, 2)
    right_ref[:LANES, :LANES] = high
    right_ref[:LANES, LANES:] = small
    right_ref[LANES:, :LANES] = high
    right_ref[LANES:, LANES:] = jnp.zeros_like(small)


def inverse_factors(cov, total_count):
    return pl.pallas_call(
        functools.partial(inverse_kernel, total_count),
        out_shape=(
            jax.ShapeDtypeStruct((K_OUT, 3 * K_OUT), BF16),
            jax.ShapeDtypeStruct((2 * LANES, 2 * LANES), BF16),
        ),
        in_specs=[pl.BlockSpec(memory_space=pltpu.VMEM)],
        out_specs=(pl.BlockSpec(memory_space=pltpu.VMEM), pl.BlockSpec(memory_space=pltpu.VMEM)),
        compiler_params=pltpu.CompilerParams(vmem_limit_bytes=VMEM_LIMIT),
        cost_estimate=pl.CostEstimate(flops=INVERSE_COST, bytes_accessed=0, transcendentals=0),
        name="inverses",
    )(cov)


def score_kernel(route_ref, left_ref, right_ref, first_ref, second_ref, train_ref, out_ref, solved, wide, ready):
    blocks = K_OUT // 2
    pairs = HALF // 2
    step = pl.program_id(0)
    group = 4
    for side, turned_ref in enumerate((first_ref, second_ref)):
        for g in range(pairs // group):
            block = turned_ref[:, g * group * LANES:(g + 1) * group * LANES]
            tall = jnp.concatenate([block, block, block], axis=0)
            once = jnp.dot(left_ref[...], tall, preferred_element_type=F32)
            for k in range(group):
                high, small = split(once[:, k * LANES:(k + 1) * LANES], 2)
                at = (side * pairs + g * group + k) * K_OUT
                wide[at:at + K_OUT, :LANES] = high
                wide[at:at + K_OUT, LANES:] = small
    twice = jnp.dot(wide[...], right_ref[...], preferred_element_type=F32)
    solved[...] = twice[:, :LANES] + twice[:, LANES:]
    for c in range(blocks):
        first = solved[pl.ds(c, 2 * pairs, stride=K_OUT), :]
        second = solved[pl.ds(c + blocks, 2 * pairs, stride=K_OUT), :]
        even, odd = swap_pair(first, second)
        columns = slice(c * LANES, (c + 1) * LANES)
        for side in range(2):
            at = side * HALF
            ready[at:at + pairs, columns] = even[side * pairs:(side + 1) * pairs, :].astype(BF16)
            ready[at + pairs:at + HALF, columns] = odd[side * pairs:(side + 1) * pairs, :].astype(BF16)
    scores = lax.dot_general(ready[...], train_ref[...], NT, preferred_element_type=F32)
    per_query = out_ref.shape[2]
    parts = out_ref.shape[1]
    for s in range(CHUNK // per_query):
        owner = route_ref[step * (CHUNK // per_query) + s]
        for part in range(parts):
            piece = scores[s * per_query:(s + 1) * per_query, part * LANES:(part + 1) * LANES]
            out_ref[owner, part, :, :] = piece


def all_scores(route, factors, turned, train, per_query):
    shard_count = route.shape[0]
    examples, width = train.shape
    steps = shard_count * per_query // CHUNK
    parts = examples // LANES
    if len(turned) == 2:
        places = [lambda step: (0, 0), lambda step: (0, 0)]
    else:
        turned = turned * 2
        places = [lambda step: (0, 2 * step), lambda step: (0, 2 * step + 1)]
    return pl.pallas_call(
        score_kernel,
        out_shape=jax.ShapeDtypeStruct((shard_count, parts, per_query, LANES), F32),
        grid=(steps,),
        in_specs=[
            pl.BlockSpec(memory_space=pltpu.SMEM),
            pl.BlockSpec((K_OUT, 3 * K_OUT), lambda step: (0, 0)),
            pl.BlockSpec((2 * LANES, 2 * LANES), lambda step: (0, 0)),
            pl.BlockSpec((K_OUT, HALF * K_IN), places[0]),
            pl.BlockSpec((K_OUT, HALF * K_IN), places[1]),
            pl.BlockSpec((examples, width), lambda step: (0, 0)),
        ],
        out_specs=pl.BlockSpec((shard_count, parts, per_query, LANES), lambda step: (0, 0, 0, 0)),
        scratch_shapes=[
            pltpu.VMEM((HALF * K_OUT, LANES), F32),
            pltpu.VMEM((HALF * K_OUT, 2 * LANES), BF16),
            pltpu.VMEM((CHUNK, width), BF16),
        ],
        compiler_params=pltpu.CompilerParams(vmem_limit_bytes=VMEM_LIMIT),
        cost_estimate=pl.CostEstimate(
            flops=2 * shard_count * per_query * width * (examples + 128), bytes_accessed=2 * examples * width, transcendentals=0
        ),
        name="products_and_scores",
    )(route, *factors, *turned, train)


def exchange(values, distance, count):
    return lax.ppermute(values, "dp", [(k, k ^ distance) for k in range(count)])


def shards(train_grads, query_grads, listed):
    shard_count = lax.axis_size("dp")
    layers = lax.axis_size("layer")
    own_index = lax.axis_index("dp").astype(jnp.int32)
    examples = train_grads.shape[0]
    per_query = query_grads.shape[0]
    train = train_grads.reshape(examples, train_grads.shape[2])
    own_queries = query_grads.reshape(per_query, query_grads.shape[2])
    total_count = float(examples * shard_count)
    order = jnp.arange(shard_count, dtype=jnp.int32)
    if shard_count == 8:
        far = exchange(own_queries, 4, shard_count)
        cov = covariance_sums(*staged_rows(train))
        far, _ = lax.optimization_barrier((far, cov))
        column = jnp.concatenate([own_queries, far], axis=0)
        cov = cov + exchange(cov, 1, shard_count)
        near = exchange(column, 2, shard_count)
        column = jnp.concatenate([column, near], axis=0)
        cov = cov + exchange(cov, 4, shard_count)
        beside = exchange(column, 1, shard_count)
        last = exchange(cov, 2, shard_count)
        here, cov = lax.optimization_barrier((turned_queries(column), cov))
        factors = inverse_factors(cov + last, total_count)
        beside, _ = lax.optimization_barrier((beside, factors[0]))
        turned = [here, turned_queries(beside)]
        order = jnp.array([0, 4, 2, 6, 1, 5, 3, 7], jnp.int32)
        route = own_index ^ order
    else:
        turned = [turned_queries(lax.all_gather(own_queries, "dp", axis=0, tiled=True))]
        cov = lax.psum(covariance_sums(*staged_rows(train)), "dp")
        factors = inverse_factors(cov, total_count)
        route = order
    scores = all_scores(route, factors, turned, train, per_query)
    outgoing = scores.reshape(shard_count * layers, per_query, examples // layers)
    wanted = listed[0][:, None] == jnp.arange(shard_count, dtype=jnp.int32)[None, :]
    wanted, outgoing = lax.optimization_barrier((wanted, outgoing))
    received = lax.all_to_all(outgoing, ("dp", "layer"), split_axis=0, concat_axis=0, tiled=True)
    received = received.reshape(1, shard_count, layers, per_query, examples // layers)
    return jnp.sum(jnp.where(wanted[:, :, None, None, None], received, 0.0), axis=(1, 2))


def solution(mesh):
    in_specs = (
        P(("groups", "dp"), "layer", None),
        P(("groups", "dp"), "layer", None),
        P(("groups", "dp"), None),
    )
    out_specs = P(("groups", "dp"), None, "layer")
    return jax.shard_map(shards, mesh=mesh, in_specs=in_specs, out_specs=out_specs, check_vma=False)
```

```python
import functools
import jax
import jax.numpy as jnp
from jax import lax
from jax.experimental import pallas as pl
from jax.experimental.pallas import tpu as pltpu
from jax.sharding import PartitionSpec as P

K_OUT = 64
K_IN = 64
LANES = 128
CHUNK = 64
HALF = CHUNK // 2
PIVOT = 4
F32 = jnp.float32
BF16 = jnp.bfloat16
VMEM_LIMIT = 48 * 1024 * 1024
INVERSE_COST = 2 * 10**9
STAGE_VMEM_LIMIT = 50 * 1024 * 1024

NT = (((1,), (1,)), ((), ()))


def low_half(rows):
    return lax.broadcasted_iota(jnp.int32, (rows, LANES), 1) < LANES // 2


def swap_pair(first, second):
    low = low_half(first.shape[0])
    even = jnp.where(low, first, pltpu.roll(second, LANES // 2, 1))
    odd = jnp.where(low, pltpu.roll(first, LANES // 2, 1), second)
    return even, odd


def split(values, terms):
    parts = []
    for _ in range(terms):
        part = values.astype(BF16)
        parts.append(part)
        values = values - part.astype(F32)
    return parts


def stage_kernel(train_ref, in_ref, rows_ref, held, by_in, arrived):
    examples, width = train_ref.shape
    pair = 2 * LANES
    chunks, _, chunk = held.shape
    copies = []
    for g in range(chunks):
        source = train_ref.at[:, pl.ds(g * chunk, chunk)]
        copies.append(pltpu.make_async_copy(source, held.at[g], arrived.at[g]))
        copies[-1].start()
    for m in range(width // pair):
        if m * pair % chunk == 0:
            copies[m * pair // chunk].wait()
        begin = m * pair % chunk
        block = held[m * pair // chunk, :, begin:begin + pair].astype(F32).T
        for k in range(4):
            start = (4 * m + k) * examples
            by_in[:, start:start + examples] = block[k * K_IN:(k + 1) * K_IN, :].astype(BF16)
        for half in range(2):
            for j in range(K_IN // 8):
                first = half * K_IN + j * 8
                both = jnp.concatenate([block[first:first + 8, :], block[first + LANES:first + LANES + 8, :]], axis=0)
                at = half * K_OUT // 2 * 8 + m * 16
                rows_ref[at:at + 16, j * examples:(j + 1) * examples] = both.astype(BF16)
    in_ref[...] = lax.dot_general(by_in[...], by_in[...], NT, preferred_element_type=F32)


def tile_sums(values):
    count, width = values.shape
    row = lax.broadcasted_iota(jnp.int32, (8, width), 0)
    result = []
    for begin in range(0, count, 64):
        tiles = [values[begin + 8 * k:begin + 8 * k + 8, :] for k in range(8)]
        for distance in (1, 2, 4):
            low = (row & distance) == 0
            pairs = zip(tiles[0::2], tiles[1::2])
            tiles = [jnp.where(low, x, y) + pltpu.roll(jnp.where(low, y, x), distance, 0) for x, y in pairs]
        result.append(tiles[0])
    return jnp.concatenate(result, axis=0)


def gram_kernel(in_ref, rows_ref, cov_ref):
    count = rows_ref.shape[0]
    every = lax.dot_general(rows_ref[...], rows_ref[...], NT, preferred_element_type=F32)
    row = lax.broadcasted_iota(jnp.int32, (count, count), 0)
    lane = lax.broadcasted_iota(jnp.int32, (count, count), 1)
    every = jnp.where((row & 7) == (lane & 7), every, 0.0)
    summed = tile_sums(every)
    lane = lax.broadcasted_iota(jnp.int32, (count, count // 8), 0)
    column = lax.broadcasted_iota(jnp.int32, (count, count // 8), 1)
    merge = jnp.where(lane // 8 == column, 1.0, 0.0).astype(BF16)
    out_sum = sum(jnp.dot(part, merge, preferred_element_type=F32) for part in reversed(split(summed, 3)))
    cov_ref[...] = jnp.concatenate([in_ref[...], out_sum], axis=1)


def staged_rows(train):
    examples, width = train.shape
    chunks = 16 if width % (16 * 2 * LANES) == 0 else 1
    return pl.pallas_call(
        stage_kernel,
        out_shape=(
            jax.ShapeDtypeStruct((K_IN, K_IN), F32),
            jax.ShapeDtypeStruct((8 * K_OUT, K_IN // 8 * examples), BF16),
        ),
        in_specs=[pl.BlockSpec(memory_space=pltpu.HBM)],
        out_specs=(pl.BlockSpec(memory_space=pltpu.VMEM), pl.BlockSpec(memory_space=pltpu.VMEM)),
        scratch_shapes=[
            pltpu.VMEM((chunks, examples, width // chunks), BF16),
            pltpu.VMEM((K_IN, K_OUT * examples), BF16),
            pltpu.SemaphoreType.DMA((chunks,)),
        ],
        compiler_params=pltpu.CompilerParams(vmem_limit_bytes=STAGE_VMEM_LIMIT),
        cost_estimate=pl.CostEstimate(flops=32 * examples * 64**3, bytes_accessed=2 * examples * width, transcendentals=0),
        name="stage_rows",
    )(train)


def covariance_sums(in_sum, rows):
    return pl.pallas_call(
        gram_kernel,
        out_shape=jax.ShapeDtypeStruct((K_OUT, 2 * K_IN), F32),
        in_specs=[pl.BlockSpec(memory_space=pltpu.VMEM), pl.BlockSpec(memory_space=pltpu.VMEM)],
        out_specs=pl.BlockSpec(memory_space=pltpu.VMEM),
        compiler_params=pltpu.CompilerParams(vmem_limit_bytes=VMEM_LIMIT),
        cost_estimate=pl.CostEstimate(flops=2 * rows.shape[0] * rows.size, bytes_accessed=2 * rows.size, transcendentals=0),
        name="covariance",
    )(in_sum, rows)


def turn_kernel(query_ref, out_ref, spread):
    count, width = query_ref.shape
    blocks = width // LANES
    pairs = count // 2
    for c in range(blocks):
        spread[c * count:(c + 1) * count, :] = query_ref[:, c * LANES:(c + 1) * LANES].astype(F32)
    for p in range(pairs):
        first = spread[pl.ds(p, blocks, stride=count), :]
        second = spread[pl.ds(p + pairs, blocks, stride=count), :]
        even, odd = swap_pair(first, second)
        out_ref[:blocks, p * LANES:(p + 1) * LANES] = even.astype(BF16)
        out_ref[blocks:, p * LANES:(p + 1) * LANES] = odd.astype(BF16)


def turned_queries(queries):
    total, width = queries.shape
    return pl.pallas_call(
        turn_kernel,
        out_shape=jax.ShapeDtypeStruct((K_OUT, total * K_IN), BF16),
        grid=(total // HALF,),
        in_specs=[pl.BlockSpec((HALF, width), lambda step: (step, 0))],
        out_specs=pl.BlockSpec((K_OUT, HALF * K_IN), lambda step: (0, step)),
        scratch_shapes=[pltpu.VMEM((width // LANES * HALF, LANES), F32)],
        compiler_params=pltpu.CompilerParams(vmem_limit_bytes=VMEM_LIMIT),
        cost_estimate=pl.CostEstimate(flops=4096 * total * width, bytes_accessed=4 * total * width, transcendentals=0),
        name="turn_queries",
    )(queries)


def damped(cov, total_count):
    rows = lax.broadcasted_iota(jnp.int32, (K_OUT, LANES), 0)
    lanes = lax.broadcasted_iota(jnp.int32, (K_OUT, LANES), 1)
    low = lanes < K_IN
    diagonal = rows == jnp.where(low, lanes, lanes - K_IN)
    cov = cov * (1.0 / total_count)
    on_diagonal = jnp.sum(jnp.where(diagonal, cov, 0.0), axis=0, keepdims=True)
    low_row = low_half(1)
    in_mean = jnp.sum(jnp.where(low_row, on_diagonal, 0.0), axis=1, keepdims=True) / K_IN
    out_mean = jnp.sum(jnp.where(low_row, 0.0, on_diagonal), axis=1, keepdims=True) / K_OUT
    scale = jnp.where(low_row, 1.0 / in_mean, 1.0)
    added = jnp.where(low_row, 0.1, 0.1 * out_mean)
    return cov * scale + jnp.where(diagonal, added, 0.0)


def inverses(matrix):
    size = matrix.shape[0]
    sub = 8
    lanes = lax.broadcasted_iota(jnp.int32, (sub, LANES), 1)
    offset = jnp.where(lanes < size, 0, size)
    place = lanes - offset
    row = lax.broadcasted_iota(jnp.int32, (sub, LANES), 0)
    tiles = [matrix[k:k + sub, :] for k in range(0, size, sub)]

    def spread_row(values, at):
        return jnp.broadcast_to(values[at:at + 1, :], (sub, LANES))

    def column(values, lane):
        return jnp.take_along_axis(values, offset + lane, axis=1, mode="promise_in_bounds")

    for begin in range(0, size, PIVOT):
        owner, first_row = begin // sub, begin % sub
        inside = (place >= begin) & (place < begin + PIVOT)
        columns = [[column(tile, begin + a) for a in range(PIVOT)] for tile in tiles]
        p = [[None] * PIVOT for _ in range(PIVOT)]
        for a in range(PIVOT):
            for b in range(a, PIVOT):
                p[a][b] = p[b][a] = spread_row(columns[owner][b], first_row + a)
        r = []
        for a in range(PIVOT):
            unit = jnp.where(place == begin + a, 1.0, 0.0)
            r.append(jnp.where(inside, unit, spread_row(tiles[owner], first_row + a)))
        det = 1.0 / (p[0][0] * p[1][1] - p[0][1] * p[1][0])
        across = -p[0][1] * det
        e = [[p[1][1] * det, across], [across, p[0][0] * det]]
        u = [[e[a][0] * p[0][b] + e[a][1] * p[1][b] for b in (2, 3)] for a in (0, 1)]
        s = [p[a][b + 2] - (p[a][0] * u[0][b] + p[a][1] * u[1][b]) for a, b in ((2, 0), (2, 1), (3, 1))]
        det = 1.0 / (s[0] * s[2] - s[1] * s[1])
        across = -s[1] * det
        f = [[s[2] * det, across], [across, s[0] * det]]
        w = [e[a][0] * r[0] + e[a][1] * r[1] for a in (0, 1)]
        t = [r[a] - (p[a][0] * w[0] + p[a][1] * w[1]) for a in (2, 3)]
        last = [f[a][0] * t[0] + f[a][1] * t[1] for a in (0, 1)]
        first = [w[a] - (u[a][0] * last[0] + u[a][1] * last[1]) for a in (0, 1)]
        solved = first + last
        for k in range(len(tiles)):
            rest = jnp.where(inside, 0.0, tiles[k])
            part = [columns[k][a] * solved[a] for a in range(PIVOT)]
            rest = (rest - (part[0] + part[1])) - (part[2] + part[3])
            if k == owner:
                for a in range(PIVOT):
                    rest = jnp.where(row == first_row + a, solved[a], rest)
            tiles[k] = rest
    return jnp.concatenate(tiles, axis=0)


def inverse_kernel(total_count, cov_ref, left_ref, right_ref):
    inverse = inverses(damped(cov_ref[...], total_count))
    turned = pltpu.roll(inverse, LANES // 2, 1)
    low = low_half(K_OUT)
    left_ref[...] = jnp.concatenate(split(turned[:, :K_OUT], 3), axis=1)
    double = jnp.concatenate([jnp.where(low, inverse, 0.0), jnp.where(low, 0.0, turned)], axis=0)
    high, small = split(double, 2)
    right_ref[:LANES, :LANES] = high
    right_ref[:LANES, LANES:] = small
    right_ref[LANES:, :LANES] = high
    right_ref[LANES:, LANES:] = jnp.zeros_like(small)


def inverse_factors(cov, total_count):
    return pl.pallas_call(
        functools.partial(inverse_kernel, total_count),
        out_shape=(
            jax.ShapeDtypeStruct((K_OUT, 3 * K_OUT), BF16),
            jax.ShapeDtypeStruct((2 * LANES, 2 * LANES), BF16),
        ),
        in_specs=[pl.BlockSpec(memory_space=pltpu.VMEM)],
        out_specs=(pl.BlockSpec(memory_space=pltpu.VMEM), pl.BlockSpec(memory_space=pltpu.VMEM)),
        compiler_params=pltpu.CompilerParams(vmem_limit_bytes=VMEM_LIMIT),
        cost_estimate=pl.CostEstimate(flops=INVERSE_COST, bytes_accessed=0, transcendentals=0),
        name="inverses",
    )(cov)


def score_kernel(route_ref, left_ref, right_ref, first_ref, second_ref, train_ref, out_ref, solved, wide, ready):
    blocks = K_OUT // 2
    pairs = HALF // 2
    step = pl.program_id(0)
    group = 4
    for side, turned_ref in enumerate((first_ref, second_ref)):
        for g in range(pairs // group):
            block = turned_ref[:, g * group * LANES:(g + 1) * group * LANES]
            tall = jnp.concatenate([block, block, block], axis=0)
            once = jnp.dot(left_ref[...], tall, preferred_element_type=F32)
            for k in range(group):
                high, small = split(once[:, k * LANES:(k + 1) * LANES], 2)
                at = (side * pairs + g * group + k) * K_OUT
                wide[at:at + K_OUT, :LANES] = high
                wide[at:at + K_OUT, LANES:] = small
    twice = jnp.dot(wide[...], right_ref[...], preferred_element_type=F32)
    solved[...] = twice[:, :LANES] + twice[:, LANES:]
    for c in range(blocks):
        first = solved[pl.ds(c, 2 * pairs, stride=K_OUT), :]
        second = solved[pl.ds(c + blocks, 2 * pairs, stride=K_OUT), :]
        even, odd = swap_pair(first, second)
        columns = slice(c * LANES, (c + 1) * LANES)
        for side in range(2):
            at = side * HALF
            ready[at:at + pairs, columns] = even[side * pairs:(side + 1) * pairs, :].astype(BF16)
            ready[at + pairs:at + HALF, columns] = odd[side * pairs:(side + 1) * pairs, :].astype(BF16)
    scores = lax.dot_general(train_ref[...], ready[...], NT, preferred_element_type=F32).T
    per_query = out_ref.shape[2]
    parts = out_ref.shape[1]
    for s in range(CHUNK // per_query):
        owner = route_ref[step * (CHUNK // per_query) + s]
        for part in range(parts):
            piece = scores[s * per_query:(s + 1) * per_query, part * LANES:(part + 1) * LANES]
            out_ref[owner, part, :, :] = piece


def all_scores(route, factors, turned, train, per_query):
    shard_count = route.shape[0]
    examples, width = train.shape
    steps = shard_count * per_query // CHUNK
    parts = examples // LANES
    if len(turned) == 2:
        places = [lambda step: (0, 0), lambda step: (0, 0)]
    else:
        turned = turned * 2
        places = [lambda step: (0, 2 * step), lambda step: (0, 2 * step + 1)]
    return pl.pallas_call(
        score_kernel,
        out_shape=jax.ShapeDtypeStruct((shard_count, parts, per_query, LANES), F32),
        grid=(steps,),
        in_specs=[
            pl.BlockSpec(memory_space=pltpu.SMEM),
            pl.BlockSpec((K_OUT, 3 * K_OUT), lambda step: (0, 0)),
            pl.BlockSpec((2 * LANES, 2 * LANES), lambda step: (0, 0)),
            pl.BlockSpec((K_OUT, HALF * K_IN), places[0]),
            pl.BlockSpec((K_OUT, HALF * K_IN), places[1]),
            pl.BlockSpec((examples, width), lambda step: (0, 0)),
        ],
        out_specs=pl.BlockSpec((shard_count, parts, per_query, LANES), lambda step: (0, 0, 0, 0)),
        scratch_shapes=[
            pltpu.VMEM((HALF * K_OUT, LANES), F32),
            pltpu.VMEM((HALF * K_OUT, 2 * LANES), BF16),
            pltpu.VMEM((CHUNK, width), BF16),
        ],
        compiler_params=pltpu.CompilerParams(vmem_limit_bytes=VMEM_LIMIT),
        cost_estimate=pl.CostEstimate(
            flops=2 * shard_count * per_query * width * (examples + 128), bytes_accessed=2 * examples * width, transcendentals=0
        ),
        name="products_and_scores",
    )(route, *factors, *turned, train)


def exchange(values, distance, count):
    return lax.ppermute(values, "dp", [(k, k ^ distance) for k in range(count)])


def shards(train_grads, query_grads, listed):
    shard_count = lax.axis_size("dp")
    layers = lax.axis_size("layer")
    own_index = lax.axis_index("dp").astype(jnp.int32)
    examples = train_grads.shape[0]
    per_query = query_grads.shape[0]
    train = train_grads.reshape(examples, train_grads.shape[2])
    own_queries = query_grads.reshape(per_query, query_grads.shape[2])
    total_count = float(examples * shard_count)
    order = jnp.arange(shard_count, dtype=jnp.int32)
    if shard_count == 8:
        far = exchange(own_queries, 4, shard_count)
        cov = covariance_sums(*staged_rows(train))
        far, _ = lax.optimization_barrier((far, cov))
        column = jnp.concatenate([own_queries, far], axis=0)
        cov = cov + exchange(cov, 1, shard_count)
        near = exchange(column, 2, shard_count)
        column = jnp.concatenate([column, near], axis=0)
        cov = cov + exchange(cov, 4, shard_count)
        beside = exchange(column, 1, shard_count)
        last = exchange(cov, 2, shard_count)
        here, cov = lax.optimization_barrier((turned_queries(column), cov))
        factors = inverse_factors(cov + last, total_count)
        beside, _ = lax.optimization_barrier((beside, factors[0]))
        turned = [here, turned_queries(beside)]
        order = jnp.array([0, 4, 2, 6, 1, 5, 3, 7], jnp.int32)
        route = own_index ^ order
    else:
        turned = [turned_queries(lax.all_gather(own_queries, "dp", axis=0, tiled=True))]
        cov = lax.psum(covariance_sums(*staged_rows(train)), "dp")
        factors = inverse_factors(cov, total_count)
        route = order
    scores = all_scores(route, factors, turned, train, per_query)
    outgoing = scores.reshape(shard_count * layers, per_query, examples // layers)
    wanted = listed[0][:, None] == jnp.arange(shard_count, dtype=jnp.int32)[None, :]
    wanted, outgoing = lax.optimization_barrier((wanted, outgoing))
    received = lax.all_to_all(outgoing, ("dp", "layer"), split_axis=0, concat_axis=0, tiled=True)
    received = received.reshape(1, shard_count, layers, per_query, examples // layers)
    return jnp.sum(jnp.where(wanted[:, :, None, None, None], received, 0.0), axis=(1, 2))


def solution(mesh):
    in_specs = (
        P(("groups", "dp"), "layer", None),
        P(("groups", "dp"), "layer", None),
        P(("groups", "dp"), None),
    )
    out_specs = P(("groups", "dp"), None, "layer")
    return jax.shard_map(shards, mesh=mesh, in_specs=in_specs, out_specs=out_specs, check_vma=False)
```

```python
import functools
import jax
import jax.numpy as jnp
from jax import lax
from jax.experimental import pallas as pl
from jax.experimental.pallas import tpu as pltpu
from jax.sharding import PartitionSpec as P

K_OUT = 64
K_IN = 64
LANES = 128
CHUNK = 64
HALF = CHUNK // 2
PIVOT = 4
F32 = jnp.float32
BF16 = jnp.bfloat16
VMEM_LIMIT = 48 * 1024 * 1024
INVERSE_COST = 2 * 10**9
STAGE_VMEM_LIMIT = 50 * 1024 * 1024

NT = (((1,), (1,)), ((), ()))


def low_half(rows):
    return lax.broadcasted_iota(jnp.int32, (rows, LANES), 1) < LANES // 2


def swap_pair(first, second):
    low = low_half(first.shape[0])
    even = jnp.where(low, first, pltpu.roll(second, LANES // 2, 1))
    odd = jnp.where(low, pltpu.roll(first, LANES // 2, 1), second)
    return even, odd


def split(values, terms):
    parts = []
    for _ in range(terms):
        part = values.astype(BF16)
        parts.append(part)
        values = values - part.astype(F32)
    return parts


def stage_kernel(train_ref, in_ref, rows_ref, held, by_in, arrived):
    examples, width = train_ref.shape
    pair = 2 * LANES
    chunks, _, chunk = held.shape
    copies = []
    for g in range(chunks):
        source = train_ref.at[:, pl.ds(g * chunk, chunk)]
        copies.append(pltpu.make_async_copy(source, held.at[g], arrived.at[g]))
        copies[-1].start()
    for m in range(width // pair):
        if m * pair % chunk == 0:
            copies[m * pair // chunk].wait()
        begin = m * pair % chunk
        block = held[m * pair // chunk, :, begin:begin + pair].astype(F32).T
        for k in range(4):
            start = (4 * m + k) * examples
            by_in[:, start:start + examples] = block[k * K_IN:(k + 1) * K_IN, :].astype(BF16)
        for half in range(2):
            for j in range(K_IN // 8):
                first = half * K_IN + j * 8
                both = jnp.concatenate([block[first:first + 8, :], block[first + LANES:first + LANES + 8, :]], axis=0)
                at = half * K_OUT // 2 * 8 + m * 16
                rows_ref[at:at + 16, j * examples:(j + 1) * examples] = both.astype(BF16)
    in_ref[...] = lax.dot_general(by_in[...], by_in[...], NT, preferred_element_type=F32)


def tile_sums(values):
    count, width = values.shape
    row = lax.broadcasted_iota(jnp.int32, (8, width), 0)
    result = []
    for begin in range(0, count, 64):
        tiles = [values[begin + 8 * k:begin + 8 * k + 8, :] for k in range(8)]
        for distance in (1, 2, 4):
            low = (row & distance) == 0
            pairs = zip(tiles[0::2], tiles[1::2])
            tiles = [jnp.where(low, x, y) + pltpu.roll(jnp.where(low, y, x), distance, 0) for x, y in pairs]
        result.append(tiles[0])
    return jnp.concatenate(result, axis=0)


def gram_kernel(in_ref, rows_ref, cov_ref):
    count = rows_ref.shape[0]
    every = lax.dot_general(rows_ref[...], rows_ref[...], NT, preferred_element_type=F32)
    row = lax.broadcasted_iota(jnp.int32, (count, count), 0)
    lane = lax.broadcasted_iota(jnp.int32, (count, count), 1)
    every = jnp.where((row & 7) == (lane & 7), every, 0.0)
    summed = tile_sums(every)
    lane = lax.broadcasted_iota(jnp.int32, (count, count // 8), 0)
    column = lax.broadcasted_iota(jnp.int32, (count, count // 8), 1)
    merge = jnp.where(lane // 8 == column, 1.0, 0.0).astype(BF16)
    out_sum = sum(jnp.dot(part, merge, preferred_element_type=F32) for part in reversed(split(summed, 3)))
    cov_ref[...] = packed(jnp.concatenate([in_ref[...], out_sum], axis=1))


def packed(sums):
    rows = K_OUT // 2
    odd = (lax.broadcasted_iota(jnp.int32, (rows // 2, LANES), 1) // rows) % 2 == 1
    corner = jnp.where(odd, sums[rows:rows + rows // 2, :], pltpu.roll(sums[rows + rows // 2:, :], LANES - rows, 1))
    return jnp.concatenate([sums[:rows, :], corner], axis=0)


def unpacked(sums):
    rows = K_OUT // 2
    top, corner = sums[:rows, :], sums[rows:, :]
    right = jnp.concatenate([corner, pltpu.roll(corner, rows, 1)], axis=0)
    turned = top.T
    empty = jnp.zeros((rows, rows), F32)
    left = jnp.concatenate([turned[rows:2 * rows, :], empty, turned[3 * rows:, :], empty], axis=1)
    odd = (lax.broadcasted_iota(jnp.int32, (rows, LANES), 1) // rows) % 2 == 1
    return jnp.concatenate([top, jnp.where(odd, right, left)], axis=0)


def staged_rows(train):
    examples, width = train.shape
    chunks = 4 if width % (4 * 2 * LANES) == 0 else 1
    return pl.pallas_call(
        stage_kernel,
        out_shape=(
            jax.ShapeDtypeStruct((K_IN, K_IN), F32),
            jax.ShapeDtypeStruct((8 * K_OUT, K_IN // 8 * examples), BF16),
        ),
        in_specs=[pl.BlockSpec(memory_space=pltpu.HBM)],
        out_specs=(pl.BlockSpec(memory_space=pltpu.VMEM), pl.BlockSpec(memory_space=pltpu.VMEM)),
        scratch_shapes=[
            pltpu.VMEM((chunks, examples, width // chunks), BF16),
            pltpu.VMEM((K_IN, K_OUT * examples), BF16),
            pltpu.SemaphoreType.DMA((chunks,)),
        ],
        compiler_params=pltpu.CompilerParams(vmem_limit_bytes=STAGE_VMEM_LIMIT),
        cost_estimate=pl.CostEstimate(flops=32 * examples * 64**3, bytes_accessed=2 * examples * width, transcendentals=0),
        name="stage_rows",
    )(train)


def covariance_sums(in_sum, rows):
    return pl.pallas_call(
        gram_kernel,
        out_shape=jax.ShapeDtypeStruct((K_OUT * 3 // 4, 2 * K_IN), F32),
        in_specs=[pl.BlockSpec(memory_space=pltpu.VMEM), pl.BlockSpec(memory_space=pltpu.VMEM)],
        out_specs=pl.BlockSpec(memory_space=pltpu.VMEM),
        compiler_params=pltpu.CompilerParams(vmem_limit_bytes=VMEM_LIMIT),
        cost_estimate=pl.CostEstimate(flops=2 * rows.shape[0] * rows.size, bytes_accessed=2 * rows.size, transcendentals=0),
        name="covariance",
    )(in_sum, rows)


def turn_kernel(query_ref, out_ref, spread):
    count, width = query_ref.shape
    blocks = width // LANES
    pairs = count // 2
    for c in range(blocks):
        spread[c * count:(c + 1) * count, :] = query_ref[:, c * LANES:(c + 1) * LANES].astype(F32)
    for p in range(pairs):
        first = spread[pl.ds(p, blocks, stride=count), :]
        second = spread[pl.ds(p + pairs, blocks, stride=count), :]
        even, odd = swap_pair(first, second)
        out_ref[:blocks, p * LANES:(p + 1) * LANES] = even.astype(BF16)
        out_ref[blocks:, p * LANES:(p + 1) * LANES] = odd.astype(BF16)


def turned_queries(queries):
    total, width = queries.shape
    return pl.pallas_call(
        turn_kernel,
        out_shape=jax.ShapeDtypeStruct((K_OUT, total * K_IN), BF16),
        grid=(total // HALF,),
        in_specs=[pl.BlockSpec((HALF, width), lambda step: (step, 0))],
        out_specs=pl.BlockSpec((K_OUT, HALF * K_IN), lambda step: (0, step)),
        scratch_shapes=[pltpu.VMEM((width // LANES * HALF, LANES), F32)],
        compiler_params=pltpu.CompilerParams(vmem_limit_bytes=VMEM_LIMIT),
        cost_estimate=pl.CostEstimate(flops=4096 * total * width, bytes_accessed=4 * total * width, transcendentals=0),
        name="turn_queries",
    )(queries)


def damped(cov, total_count):
    rows = lax.broadcasted_iota(jnp.int32, (K_OUT, LANES), 0)
    lanes = lax.broadcasted_iota(jnp.int32, (K_OUT, LANES), 1)
    low = lanes < K_IN
    diagonal = rows == jnp.where(low, lanes, lanes - K_IN)
    cov = cov * (1.0 / total_count)
    on_diagonal = jnp.sum(jnp.where(diagonal, cov, 0.0), axis=0, keepdims=True)
    low_row = low_half(1)
    in_mean = jnp.sum(jnp.where(low_row, on_diagonal, 0.0), axis=1, keepdims=True) / K_IN
    out_mean = jnp.sum(jnp.where(low_row, 0.0, on_diagonal), axis=1, keepdims=True) / K_OUT
    scale = jnp.where(low_row, 1.0 / in_mean, 1.0)
    added = jnp.where(low_row, 0.1, 0.1 * out_mean)
    return cov * scale + jnp.where(diagonal, added, 0.0)


def reciprocal(values):
    estimate = pl.reciprocal(values, approx=True)
    for _ in range(2):
        estimate = estimate * (2.0 - values * estimate)
    return estimate


def inverses(matrix):
    size = matrix.shape[0]
    sub = 8
    lanes = lax.broadcasted_iota(jnp.int32, (sub, LANES), 1)
    offset = jnp.where(lanes < size, 0, size)
    place = lanes - offset
    row = lax.broadcasted_iota(jnp.int32, (sub, LANES), 0)
    tiles = [matrix[k:k + sub, :] for k in range(0, size, sub)]

    def spread_row(values, at):
        return jnp.broadcast_to(values[at:at + 1, :], (sub, LANES))

    def column(values, lane):
        return jnp.take_along_axis(values, offset + lane, axis=1, mode="promise_in_bounds")

    for begin in range(0, size, PIVOT):
        owner, first_row = begin // sub, begin % sub
        inside = (place >= begin) & (place < begin + PIVOT)
        columns = [[column(tile, begin + a) for a in range(PIVOT)] for tile in tiles]
        p = [[None] * PIVOT for _ in range(PIVOT)]
        for a in range(PIVOT):
            for b in range(a, PIVOT):
                p[a][b] = p[b][a] = spread_row(columns[owner][b], first_row + a)
        r = []
        for a in range(PIVOT):
            unit = jnp.where(place == begin + a, 1.0, 0.0)
            r.append(jnp.where(inside, unit, spread_row(tiles[owner], first_row + a)))
        det = reciprocal(p[0][0] * p[1][1] - p[0][1] * p[1][0])
        across = -p[0][1] * det
        e = [[p[1][1] * det, across], [across, p[0][0] * det]]
        u = [[e[a][0] * p[0][b] + e[a][1] * p[1][b] for b in (2, 3)] for a in (0, 1)]
        s = [p[a][b + 2] - (p[a][0] * u[0][b] + p[a][1] * u[1][b]) for a, b in ((2, 0), (2, 1), (3, 1))]
        det = reciprocal(s[0] * s[2] - s[1] * s[1])
        across = -s[1] * det
        f = [[s[2] * det, across], [across, s[0] * det]]
        w = [e[a][0] * r[0] + e[a][1] * r[1] for a in (0, 1)]
        t = [r[a] - (p[a][0] * w[0] + p[a][1] * w[1]) for a in (2, 3)]
        last = [f[a][0] * t[0] + f[a][1] * t[1] for a in (0, 1)]
        first = [w[a] - (u[a][0] * last[0] + u[a][1] * last[1]) for a in (0, 1)]
        solved = first + last
        for k in range(len(tiles)):
            rest = jnp.where(inside, 0.0, tiles[k])
            part = [columns[k][a] * solved[a] for a in range(PIVOT)]
            rest = (rest - (part[0] + part[1])) - (part[2] + part[3])
            if k == owner:
                for a in range(PIVOT):
                    rest = jnp.where(row == first_row + a, solved[a], rest)
            tiles[k] = rest
    return jnp.concatenate(tiles, axis=0)


def inverse_kernel(total_count, cov_ref, left_ref, right_ref):
    inverse = inverses(damped(unpacked(cov_ref[...]), total_count))
    turned = pltpu.roll(inverse, LANES // 2, 1)
    low = low_half(K_OUT)
    left_ref[...] = jnp.concatenate(split(turned[:, :K_OUT], 3), axis=1)
    double = jnp.concatenate([jnp.where(low, inverse, 0.0), jnp.where(low, 0.0, turned)], axis=0)
    high, small = split(double, 2)
    right_ref[:LANES, :LANES] = high
    right_ref[:LANES, LANES:] = small
    right_ref[LANES:, :LANES] = high
    right_ref[LANES:, LANES:] = jnp.zeros_like(small)


def inverse_factors(cov, total_count):
    return pl.pallas_call(
        functools.partial(inverse_kernel, total_count),
        out_shape=(
            jax.ShapeDtypeStruct((K_OUT, 3 * K_OUT), BF16),
            jax.ShapeDtypeStruct((2 * LANES, 2 * LANES), BF16),
        ),
        in_specs=[pl.BlockSpec(memory_space=pltpu.VMEM)],
        out_specs=(pl.BlockSpec(memory_space=pltpu.VMEM), pl.BlockSpec(memory_space=pltpu.VMEM)),
        compiler_params=pltpu.CompilerParams(vmem_limit_bytes=VMEM_LIMIT),
        cost_estimate=pl.CostEstimate(flops=INVERSE_COST, bytes_accessed=0, transcendentals=0),
        name="inverses",
    )(cov)


def score_kernel(route_ref, left_ref, right_ref, first_ref, second_ref, train_ref, out_ref, solved, wide, ready):
    blocks = K_OUT // 2
    pairs = HALF // 2
    step = pl.program_id(0)
    group = 4
    for side, turned_ref in enumerate((first_ref, second_ref)):
        for g in range(pairs // group):
            block = turned_ref[:, g * group * LANES:(g + 1) * group * LANES]
            tall = jnp.concatenate([block, block, block], axis=0)
            once = jnp.dot(left_ref[...], tall, preferred_element_type=F32)
            for k in range(group):
                high, small = split(once[:, k * LANES:(k + 1) * LANES], 2)
                at = (side * pairs + g * group + k) * K_OUT
                wide[at:at + K_OUT, :LANES] = high
                wide[at:at + K_OUT, LANES:] = small
    twice = jnp.dot(wide[...], right_ref[...], preferred_element_type=F32)
    solved[...] = twice[:, :LANES] + twice[:, LANES:]
    for c in range(blocks):
        first = solved[pl.ds(c, 2 * pairs, stride=K_OUT), :]
        second = solved[pl.ds(c + blocks, 2 * pairs, stride=K_OUT), :]
        even, odd = swap_pair(first, second)
        columns = slice(c * LANES, (c + 1) * LANES)
        for side in range(2):
            at = side * HALF
            ready[at:at + pairs, columns] = even[side * pairs:(side + 1) * pairs, :].astype(BF16)
            ready[at + pairs:at + HALF, columns] = odd[side * pairs:(side + 1) * pairs, :].astype(BF16)
    scores = lax.dot_general(ready[...], train_ref[...], NT, preferred_element_type=F32)
    per_query = out_ref.shape[2]
    parts = out_ref.shape[1]
    for s in range(CHUNK // per_query):
        owner = route_ref[step * (CHUNK // per_query) + s]
        for part in range(parts):
            piece = scores[s * per_query:(s + 1) * per_query, part * LANES:(part + 1) * LANES]
            out_ref[owner, part, :, :] = piece


def all_scores(route, factors, turned, train, per_query):
    shard_count = route.shape[0]
    examples, width = train.shape
    steps = shard_count * per_query // CHUNK
    parts = examples // LANES
    if len(turned) == 2:
        places = [lambda step: (0, 0), lambda step: (0, 0)]
    else:
        turned = turned * 2
        places = [lambda step: (0, 2 * step), lambda step: (0, 2 * step + 1)]
    return pl.pallas_call(
        score_kernel,
        out_shape=jax.ShapeDtypeStruct((shard_count, parts, per_query, LANES), F32),
        grid=(steps,),
        in_specs=[
            pl.BlockSpec(memory_space=pltpu.SMEM),
            pl.BlockSpec((K_OUT, 3 * K_OUT), lambda step: (0, 0)),
            pl.BlockSpec((2 * LANES, 2 * LANES), lambda step: (0, 0)),
            pl.BlockSpec((K_OUT, HALF * K_IN), places[0]),
            pl.BlockSpec((K_OUT, HALF * K_IN), places[1]),
            pl.BlockSpec((examples, width), lambda step: (0, 0)),
        ],
        out_specs=pl.BlockSpec((shard_count, parts, per_query, LANES), lambda step: (0, 0, 0, 0)),
        scratch_shapes=[
            pltpu.VMEM((HALF * K_OUT, LANES), F32),
            pltpu.VMEM((HALF * K_OUT, 2 * LANES), BF16),
            pltpu.VMEM((CHUNK, width), BF16),
        ],
        compiler_params=pltpu.CompilerParams(vmem_limit_bytes=VMEM_LIMIT),
        cost_estimate=pl.CostEstimate(
            flops=2 * shard_count * per_query * width * (examples + 128), bytes_accessed=2 * examples * width, transcendentals=0
        ),
        name="products_and_scores",
    )(route, *factors, *turned, train)


def exchange(values, distance, count):
    return lax.ppermute(values, "dp", [(k, k ^ distance) for k in range(count)])


def shards(train_grads, query_grads, listed):
    shard_count = lax.axis_size("dp")
    layers = lax.axis_size("layer")
    own_index = lax.axis_index("dp").astype(jnp.int32)
    examples = train_grads.shape[0]
    per_query = query_grads.shape[0]
    train = train_grads.reshape(examples, train_grads.shape[2])
    own_queries = query_grads.reshape(per_query, query_grads.shape[2])
    total_count = float(examples * shard_count)
    order = jnp.arange(shard_count, dtype=jnp.int32)
    if shard_count == 8:
        far = exchange(own_queries, 4, shard_count)
        cov = covariance_sums(*staged_rows(train))
        far, _ = lax.optimization_barrier((far, cov))
        column = jnp.concatenate([own_queries, far], axis=0)
        cov = cov + exchange(cov, 1, shard_count)
        near = exchange(column, 2, shard_count)
        column = jnp.concatenate([column, near], axis=0)
        cov = cov + exchange(cov, 4, shard_count)
        beside = exchange(column, 1, shard_count)
        last = exchange(cov, 2, shard_count)
        here, cov = lax.optimization_barrier((turned_queries(column), cov))
        factors = inverse_factors(cov + last, total_count)
        beside, _ = lax.optimization_barrier((beside, factors[0]))
        turned = [here, turned_queries(beside)]
        order = jnp.array([0, 4, 2, 6, 1, 5, 3, 7], jnp.int32)
        route = own_index ^ order
    else:
        turned = [turned_queries(lax.all_gather(own_queries, "dp", axis=0, tiled=True))]
        cov = lax.psum(covariance_sums(*staged_rows(train)), "dp")
        factors = inverse_factors(cov, total_count)
        route = order
    scores = all_scores(route, factors, turned, train, per_query)
    outgoing = scores.reshape(shard_count * layers, per_query, examples // layers)
    wanted = listed[0][:, None] == jnp.arange(shard_count, dtype=jnp.int32)[None, :]
    wanted, outgoing = lax.optimization_barrier((wanted, outgoing))
    received = lax.all_to_all(outgoing, ("dp", "layer"), split_axis=0, concat_axis=0, tiled=True)
    received = received.reshape(1, shard_count, layers, per_query, examples // layers)
    return jnp.sum(jnp.where(wanted[:, :, None, None, None], received, 0.0), axis=(1, 2))


def solution(mesh):
    in_specs = (
        P(("groups", "dp"), "layer", None),
        P(("groups", "dp"), "layer", None),
        P(("groups", "dp"), None),
    )
    out_specs = P(("groups", "dp"), None, "layer")
    return jax.shard_map(shards, mesh=mesh, in_specs=in_specs, out_specs=out_specs, check_vma=False)
```

```python
import functools
import jax
import jax.numpy as jnp
from jax import lax
from jax.experimental import pallas as pl
from jax.experimental.pallas import tpu as pltpu
from jax.sharding import PartitionSpec as P

K_OUT = 64
K_IN = 64
LANES = 128
CHUNK = 64
HALF = CHUNK // 2
PIVOT = 4
F32 = jnp.float32
BF16 = jnp.bfloat16
VMEM_LIMIT = 48 * 1024 * 1024
INVERSE_COST = 2 * 10**9
STAGE_VMEM_LIMIT = 50 * 1024 * 1024

NT = (((1,), (1,)), ((), ()))


def low_half(rows):
    return lax.broadcasted_iota(jnp.int32, (rows, LANES), 1) < LANES // 2


def swap_pair(first, second):
    low = low_half(first.shape[0])
    even = jnp.where(low, first, pltpu.roll(second, LANES // 2, 1))
    odd = jnp.where(low, pltpu.roll(first, LANES // 2, 1), second)
    return even, odd


def split(values, terms):
    parts = []
    for _ in range(terms):
        part = values.astype(BF16)
        parts.append(part)
        values = values - part.astype(F32)
    return parts


def stage_kernel(train_ref, in_ref, rows_ref, held, by_in, arrived):
    examples, width = train_ref.shape
    pair = 2 * LANES
    chunks, _, chunk = held.shape
    copies = []
    for g in range(chunks):
        source = train_ref.at[:, pl.ds(g * chunk, chunk)]
        copies.append(pltpu.make_async_copy(source, held.at[g], arrived.at[g]))
        copies[-1].start()
    for m in range(width // pair):
        if m * pair % chunk == 0:
            copies[m * pair // chunk].wait()
        begin = m * pair % chunk
        block = held[m * pair // chunk, :, begin:begin + pair].astype(F32).T
        for k in range(4):
            start = (4 * m + k) * examples
            by_in[:, start:start + examples] = block[k * K_IN:(k + 1) * K_IN, :].astype(BF16)
        for half in range(2):
            for j in range(K_IN // 8):
                first = half * K_IN + j * 8
                both = jnp.concatenate([block[first:first + 8, :], block[first + LANES:first + LANES + 8, :]], axis=0)
                at = half * K_OUT // 2 * 8 + m * 16
                rows_ref[at:at + 16, j * examples:(j + 1) * examples] = both.astype(BF16)
    in_ref[...] = lax.dot_general(by_in[...], by_in[...], NT, preferred_element_type=F32)


def tile_sums(values):
    count, width = values.shape
    row = lax.broadcasted_iota(jnp.int32, (8, width), 0)
    result = []
    for begin in range(0, count, 64):
        tiles = [values[begin + 8 * k:begin + 8 * k + 8, :] for k in range(8)]
        for distance in (1, 2, 4):
            low = (row & distance) == 0
            pairs = zip(tiles[0::2], tiles[1::2])
            tiles = [jnp.where(low, x, y) + pltpu.roll(jnp.where(low, y, x), distance, 0) for x, y in pairs]
        result.append(tiles[0])
    return jnp.concatenate(result, axis=0)


def gram_kernel(in_ref, rows_ref, cov_ref):
    count = rows_ref.shape[0]
    every = lax.dot_general(rows_ref[...], rows_ref[...], NT, preferred_element_type=F32)
    row = lax.broadcasted_iota(jnp.int32, (count, count), 0)
    lane = lax.broadcasted_iota(jnp.int32, (count, count), 1)
    every = jnp.where((row & 7) == (lane & 7), every, 0.0)
    summed = tile_sums(every)
    lane = lax.broadcasted_iota(jnp.int32, (count, count // 8), 0)
    column = lax.broadcasted_iota(jnp.int32, (count, count // 8), 1)
    merge = jnp.where(lane // 8 == column, 1.0, 0.0).astype(BF16)
    out_sum = sum(jnp.dot(part, merge, preferred_element_type=F32) for part in reversed(split(summed, 3)))
    cov_ref[...] = jnp.concatenate([in_ref[...], out_sum], axis=1)


def staged_rows(train):
    examples, width = train.shape
    chunks = 4 if width % (4 * 2 * LANES) == 0 else 1
    return pl.pallas_call(
        stage_kernel,
        out_shape=(
            jax.ShapeDtypeStruct((K_IN, K_IN), F32),
            jax.ShapeDtypeStruct((8 * K_OUT, K_IN // 8 * examples), BF16),
        ),
        in_specs=[pl.BlockSpec(memory_space=pltpu.HBM)],
        out_specs=(pl.BlockSpec(memory_space=pltpu.VMEM), pl.BlockSpec(memory_space=pltpu.VMEM)),
        scratch_shapes=[
            pltpu.VMEM((chunks, examples, width // chunks), BF16),
            pltpu.VMEM((K_IN, K_OUT * examples), BF16),
            pltpu.SemaphoreType.DMA((chunks,)),
        ],
        compiler_params=pltpu.CompilerParams(vmem_limit_bytes=STAGE_VMEM_LIMIT),
        cost_estimate=pl.CostEstimate(flops=32 * examples * 64**3, bytes_accessed=2 * examples * width, transcendentals=0),
        name="stage_rows",
    )(train)


def covariance_sums(in_sum, rows):
    return pl.pallas_call(
        gram_kernel,
        out_shape=jax.ShapeDtypeStruct((K_OUT, 2 * K_IN), F32),
        in_specs=[pl.BlockSpec(memory_space=pltpu.VMEM), pl.BlockSpec(memory_space=pltpu.VMEM)],
        out_specs=pl.BlockSpec(memory_space=pltpu.VMEM),
        compiler_params=pltpu.CompilerParams(vmem_limit_bytes=VMEM_LIMIT),
        cost_estimate=pl.CostEstimate(flops=2 * rows.shape[0] * rows.size, bytes_accessed=2 * rows.size, transcendentals=0),
        name="covariance",
    )(in_sum, rows)


def turn_kernel(query_ref, out_ref, spread):
    count, width = query_ref.shape
    blocks = width // LANES
    pairs = count // 2
    pitch = spread.shape[0] // blocks
    for c in range(blocks):
        spread[c * pitch:c * pitch + count, :] = query_ref[:, c * LANES:(c + 1) * LANES].astype(F32)
    for p in range(pairs):
        first = spread[pl.ds(p, blocks, stride=pitch), :]
        second = spread[pl.ds(p + pairs, blocks, stride=pitch), :]
        even, odd = swap_pair(first, second)
        out_ref[:blocks, p * LANES:(p + 1) * LANES] = even.astype(BF16)
        out_ref[blocks:, p * LANES:(p + 1) * LANES] = odd.astype(BF16)


def turned_queries(queries):
    total, width = queries.shape
    return pl.pallas_call(
        turn_kernel,
        out_shape=jax.ShapeDtypeStruct((K_OUT, total * K_IN), BF16),
        grid=(total // HALF,),
        in_specs=[pl.BlockSpec((HALF, width), lambda step: (step, 0))],
        out_specs=pl.BlockSpec((K_OUT, HALF * K_IN), lambda step: (0, step)),
        scratch_shapes=[pltpu.VMEM((width // LANES * (HALF + 8), LANES), F32)],
        compiler_params=pltpu.CompilerParams(vmem_limit_bytes=VMEM_LIMIT),
        cost_estimate=pl.CostEstimate(flops=4096 * total * width, bytes_accessed=4 * total * width, transcendentals=0),
        name="turn_queries",
    )(queries)


def damped(cov, total_count):
    rows = lax.broadcasted_iota(jnp.int32, (K_OUT, LANES), 0)
    lanes = lax.broadcasted_iota(jnp.int32, (K_OUT, LANES), 1)
    low = lanes < K_IN
    diagonal = rows == jnp.where(low, lanes, lanes - K_IN)
    cov = cov * (1.0 / total_count)
    on_diagonal = jnp.sum(jnp.where(diagonal, cov, 0.0), axis=0, keepdims=True)
    low_row = low_half(1)
    in_mean = jnp.sum(jnp.where(low_row, on_diagonal, 0.0), axis=1, keepdims=True) / K_IN
    out_mean = jnp.sum(jnp.where(low_row, 0.0, on_diagonal), axis=1, keepdims=True) / K_OUT
    scale = jnp.where(low_row, 1.0 / in_mean, 1.0)
    added = jnp.where(low_row, 0.1, 0.1 * out_mean)
    return cov * scale + jnp.where(diagonal, added, 0.0)


def inverses(matrix):
    size = matrix.shape[0]
    sub = 8
    lanes = lax.broadcasted_iota(jnp.int32, (sub, LANES), 1)
    offset = jnp.where(lanes < size, 0, size)
    place = lanes - offset
    row = lax.broadcasted_iota(jnp.int32, (sub, LANES), 0)
    tiles = [matrix[k:k + sub, :] for k in range(0, size, sub)]

    def spread_row(values, at):
        return jnp.broadcast_to(values[at:at + 1, :], (sub, LANES))

    def column(values, lane):
        return jnp.take_along_axis(values, offset + lane, axis=1, mode="promise_in_bounds")

    for begin in range(0, size, PIVOT):
        owner, first_row = begin // sub, begin % sub
        inside = (place >= begin) & (place < begin + PIVOT)
        columns = [[column(tile, begin + a) for a in range(PIVOT)] for tile in tiles]
        p = [[None] * PIVOT for _ in range(PIVOT)]
        for a in range(PIVOT):
            for b in range(a, PIVOT):
                p[a][b] = p[b][a] = spread_row(columns[owner][b], first_row + a)
        r = []
        for a in range(PIVOT):
            unit = jnp.where(place == begin + a, 1.0, 0.0)
            r.append(jnp.where(inside, unit, spread_row(tiles[owner], first_row + a)))
        det = 1.0 / (p[0][0] * p[1][1] - p[0][1] * p[1][0])
        across = -p[0][1] * det
        e = [[p[1][1] * det, across], [across, p[0][0] * det]]
        u = [[e[a][0] * p[0][b] + e[a][1] * p[1][b] for b in (2, 3)] for a in (0, 1)]
        s = [p[a][b + 2] - (p[a][0] * u[0][b] + p[a][1] * u[1][b]) for a, b in ((2, 0), (2, 1), (3, 1))]
        det = 1.0 / (s[0] * s[2] - s[1] * s[1])
        across = -s[1] * det
        f = [[s[2] * det, across], [across, s[0] * det]]
        w = [e[a][0] * r[0] + e[a][1] * r[1] for a in (0, 1)]
        t = [r[a] - (p[a][0] * w[0] + p[a][1] * w[1]) for a in (2, 3)]
        last = [f[a][0] * t[0] + f[a][1] * t[1] for a in (0, 1)]
        first = [w[a] - (u[a][0] * last[0] + u[a][1] * last[1]) for a in (0, 1)]
        solved = first + last
        for k in range(len(tiles)):
            rest = jnp.where(inside, 0.0, tiles[k])
            part = [columns[k][a] * solved[a] for a in range(PIVOT)]
            rest = (rest - (part[0] + part[1])) - (part[2] + part[3])
            if k == owner:
                for a in range(PIVOT):
                    rest = jnp.where(row == first_row + a, solved[a], rest)
            tiles[k] = rest
    return jnp.concatenate(tiles, axis=0)


def inverse_kernel(total_count, cov_ref, left_ref, right_ref):
    inverse = inverses(damped(cov_ref[...], total_count))
    turned = pltpu.roll(inverse, LANES // 2, 1)
    low = low_half(K_OUT)
    left_ref[...] = jnp.concatenate(split(turned[:, :K_OUT], 3), axis=0)
    double = jnp.concatenate([jnp.where(low, inverse, 0.0), jnp.where(low, 0.0, turned)], axis=0)
    high, small = split(double, 2)
    right_ref[:LANES, :LANES] = high
    right_ref[:LANES, LANES:] = small
    right_ref[LANES:, :LANES] = high
    right_ref[LANES:, LANES:] = jnp.zeros_like(small)


def inverse_factors(cov, total_count):
    return pl.pallas_call(
        functools.partial(inverse_kernel, total_count),
        out_shape=(
            jax.ShapeDtypeStruct((3 * K_OUT, K_OUT), BF16),
            jax.ShapeDtypeStruct((2 * LANES, 2 * LANES), BF16),
        ),
        in_specs=[pl.BlockSpec(memory_space=pltpu.VMEM)],
        out_specs=(pl.BlockSpec(memory_space=pltpu.VMEM), pl.BlockSpec(memory_space=pltpu.VMEM)),
        compiler_params=pltpu.CompilerParams(vmem_limit_bytes=VMEM_LIMIT),
        cost_estimate=pl.CostEstimate(flops=INVERSE_COST, bytes_accessed=0, transcendentals=0),
        name="inverses",
    )(cov)


def score_kernel(route_ref, left_ref, right_ref, first_ref, second_ref, train_ref, out_ref, solved, wide, ready):
    blocks = K_OUT // 2
    pairs = HALF // 2
    pitch = solved.shape[0] // (2 * pairs)
    step = pl.program_id(0)
    group = 4
    for side, turned_ref in enumerate((first_ref, second_ref)):
        for g in range(pairs // group):
            block = turned_ref[:, g * group * LANES:(g + 1) * group * LANES]
            terms = jnp.dot(left_ref[...], block, preferred_element_type=F32)
            once = terms[:K_OUT, :] + (terms[K_OUT:2 * K_OUT, :] + terms[2 * K_OUT:, :])
            for k in range(group):
                high, small = split(once[:, k * LANES:(k + 1) * LANES], 2)
                at = (side * pairs + g * group + k) * K_OUT
                wide[at:at + K_OUT, :LANES] = high
                wide[at:at + K_OUT, LANES:] = small
    twice = jnp.dot(wide[...], right_ref[...], preferred_element_type=F32)
    for p in range(2 * pairs):
        part = twice[p * K_OUT:(p + 1) * K_OUT, :]
        solved[p * pitch:p * pitch + K_OUT, :] = part[:, :LANES] + part[:, LANES:]
    for c in range(blocks):
        first = solved[pl.ds(c, 2 * pairs, stride=pitch), :]
        second = solved[pl.ds(c + blocks, 2 * pairs, stride=pitch), :]
        even, odd = swap_pair(first, second)
        columns = slice(c * LANES, (c + 1) * LANES)
        for side in range(2):
            at = side * HALF
            ready[at:at + pairs, columns] = even[side * pairs:(side + 1) * pairs, :].astype(BF16)
            ready[at + pairs:at + HALF, columns] = odd[side * pairs:(side + 1) * pairs, :].astype(BF16)
    scores = lax.dot_general(ready[...], train_ref[...], NT, preferred_element_type=F32)
    per_query = out_ref.shape[2]
    parts = out_ref.shape[1]
    for s in range(CHUNK // per_query):
        owner = route_ref[step * (CHUNK // per_query) + s]
        for part in range(parts):
            piece = scores[s * per_query:(s + 1) * per_query, part * LANES:(part + 1) * LANES]
            out_ref[owner, part, :, :] = piece


def all_scores(route, factors, turned, train, per_query):
    shard_count = route.shape[0]
    examples, width = train.shape
    steps = shard_count * per_query // CHUNK
    parts = examples // LANES
    if len(turned) == 2:
        places = [lambda step: (0, 0), lambda step: (0, 0)]
    else:
        turned = turned * 2
        places = [lambda step: (0, 2 * step), lambda step: (0, 2 * step + 1)]
    return pl.pallas_call(
        score_kernel,
        out_shape=jax.ShapeDtypeStruct((shard_count, parts, per_query, LANES), F32),
        grid=(steps,),
        in_specs=[
            pl.BlockSpec(memory_space=pltpu.SMEM),
            pl.BlockSpec((3 * K_OUT, K_OUT), lambda step: (0, 0)),
            pl.BlockSpec((2 * LANES, 2 * LANES), lambda step: (0, 0)),
            pl.BlockSpec((K_OUT, HALF * K_IN), places[0]),
            pl.BlockSpec((K_OUT, HALF * K_IN), places[1]),
            pl.BlockSpec((examples, width), lambda step: (0, 0)),
        ],
        out_specs=pl.BlockSpec((shard_count, parts, per_query, LANES), lambda step: (0, 0, 0, 0)),
        scratch_shapes=[
            pltpu.VMEM((HALF * (K_OUT + 8), LANES), F32),
            pltpu.VMEM((HALF * K_OUT, 2 * LANES), BF16),
            pltpu.VMEM((CHUNK, width), BF16),
        ],
        compiler_params=pltpu.CompilerParams(vmem_limit_bytes=VMEM_LIMIT),
        cost_estimate=pl.CostEstimate(
            flops=2 * shard_count * per_query * width * (examples + 128), bytes_accessed=2 * examples * width, transcendentals=0
        ),
        name="products_and_scores",
    )(route, *factors, *turned, train)


def exchange(values, distance, count):
    return lax.ppermute(values, "dp", [(k, k ^ distance) for k in range(count)])


def shards(train_grads, query_grads, listed):
    shard_count = lax.axis_size("dp")
    layers = lax.axis_size("layer")
    own_index = lax.axis_index("dp").astype(jnp.int32)
    examples = train_grads.shape[0]
    per_query = query_grads.shape[0]
    train = train_grads.reshape(examples, train_grads.shape[2])
    own_queries = query_grads.reshape(per_query, query_grads.shape[2])
    total_count = float(examples * shard_count)
    order = jnp.arange(shard_count, dtype=jnp.int32)
    if shard_count == 8:
        far = exchange(own_queries, 4, shard_count)
        cov = covariance_sums(*staged_rows(train))
        far, _ = lax.optimization_barrier((far, cov))
        column = jnp.concatenate([own_queries, far], axis=0)
        cov = cov + exchange(cov, 1, shard_count)
        near = exchange(column, 2, shard_count)
        column = jnp.concatenate([column, near], axis=0)
        cov = cov + exchange(cov, 4, shard_count)
        beside = exchange(column, 1, shard_count)
        last = exchange(cov, 2, shard_count)
        here, cov = lax.optimization_barrier((turned_queries(column), cov))
        factors = inverse_factors(cov + last, total_count)
        beside, _ = lax.optimization_barrier((beside, factors[0]))
        turned = [here, turned_queries(beside)]
        order = jnp.array([0, 4, 2, 6, 1, 5, 3, 7], jnp.int32)
        route = own_index ^ order
    else:
        turned = [turned_queries(lax.all_gather(own_queries, "dp", axis=0, tiled=True))]
        cov = lax.psum(covariance_sums(*staged_rows(train)), "dp")
        factors = inverse_factors(cov, total_count)
        route = order
    scores = all_scores(route, factors, turned, train, per_query)
    outgoing = scores.reshape(shard_count * layers, per_query, examples // layers)
    wanted = listed[0][:, None] == jnp.arange(shard_count, dtype=jnp.int32)[None, :]
    wanted, outgoing = lax.optimization_barrier((wanted, outgoing))
    received = lax.all_to_all(outgoing, ("dp", "layer"), split_axis=0, concat_axis=0, tiled=True)
    received = received.reshape(1, shard_count, layers, per_query, examples // layers)
    return jnp.sum(jnp.where(wanted[:, :, None, None, None], received, 0.0), axis=(1, 2))


def solution(mesh):
    in_specs = (
        P(("groups", "dp"), "layer", None),
        P(("groups", "dp"), "layer", None),
        P(("groups", "dp"), None),
    )
    out_specs = P(("groups", "dp"), None, "layer")
    return jax.shard_map(shards, mesh=mesh, in_specs=in_specs, out_specs=out_specs, check_vma=False)
```

```python
import functools
import jax
import jax.numpy as jnp
from jax import lax
from jax.experimental import pallas as pl
from jax.experimental.pallas import tpu as pltpu
from jax.sharding import PartitionSpec as P

K_OUT = 64
K_IN = 64
LANES = 128
CHUNK = 64
HALF = CHUNK // 2
PIVOT = 4
F32 = jnp.float32
BF16 = jnp.bfloat16
VMEM_LIMIT = 48 * 1024 * 1024
INVERSE_COST = 2 * 10**9
STAGE_VMEM_LIMIT = 50 * 1024 * 1024

NT = (((1,), (1,)), ((), ()))


def low_half(rows):
    return lax.broadcasted_iota(jnp.int32, (rows, LANES), 1) < LANES // 2


def swap_pair(first, second):
    low = low_half(first.shape[0])
    even = jnp.where(low, first, pltpu.roll(second, LANES // 2, 1))
    odd = jnp.where(low, pltpu.roll(first, LANES // 2, 1), second)
    return even, odd


def split(values, terms):
    parts = []
    for _ in range(terms):
        part = values.astype(BF16)
        parts.append(part)
        values = values - part.astype(F32)
    return parts


def covariance_kernel(train_ref, cov_ref, held, turned, by_in, by_out, arrived):
    examples, width = train_ref.shape
    blocks = width // LANES
    parts = examples // LANES
    pitch = turned.shape[1] // blocks
    chunks, _, chunk = held.shape
    copies = []
    for g in range(chunks):
        source = train_ref.at[:, pl.ds(g * chunk, chunk)]
        copies.append(pltpu.make_async_copy(source, held.at[g], arrived.at[g]))
        copies[-1].start()
    for c in range(blocks):
        if c * LANES % chunk == 0:
            copies[c * LANES // chunk].wait()
        begin = c * LANES % chunk
        block = held[c * LANES // chunk, :, begin:begin + LANES].astype(F32).T
        for part in range(parts):
            turned[part, c * pitch:c * pitch + LANES, :] = block[:, part * LANES:(part + 1) * LANES]
        for half in range(2):
            start = (2 * c + half) * examples
            by_in[:, start:start + examples] = block[half * K_IN:(half + 1) * K_IN, :].astype(BF16)
    for j in range(K_IN):
        for part in range(parts):
            start = j * examples + part * LANES
            for half in range(2):
                rows = turned[part, pl.ds(half * K_IN + j, blocks, stride=pitch), :]
                by_out[half * blocks:(half + 1) * blocks, start:start + LANES] = rows.astype(BF16)
    in_sum = lax.dot_general(by_in[...], by_in[...], NT, preferred_element_type=F32)
    out_sum = lax.dot_general(by_out[...], by_out[...], NT, preferred_element_type=F32)
    cov_ref[...] = jnp.concatenate([in_sum, out_sum], axis=1)


def covariance_sums(train):
    examples, width = train.shape
    chunks = 4 if width % (4 * LANES) == 0 else 1
    return pl.pallas_call(
        covariance_kernel,
        out_shape=jax.ShapeDtypeStruct((K_OUT, 2 * K_IN), F32),
        in_specs=[pl.BlockSpec(memory_space=pltpu.HBM)],
        out_specs=pl.BlockSpec(memory_space=pltpu.VMEM),
        scratch_shapes=[
            pltpu.VMEM((chunks, examples, width // chunks), BF16),
            pltpu.VMEM((examples // LANES, width // LANES * (LANES + 8), LANES), F32),
            pltpu.VMEM((K_IN, K_OUT * examples), BF16),
            pltpu.VMEM((K_OUT, K_IN * examples), BF16),
            pltpu.SemaphoreType.DMA((chunks,)),
        ],
        compiler_params=pltpu.CompilerParams(vmem_limit_bytes=STAGE_VMEM_LIMIT),
        cost_estimate=pl.CostEstimate(flops=64 * examples * 64**3, bytes_accessed=2 * examples * width, transcendentals=0),
        name="covariance",
    )(train)


def turn_kernel(query_ref, out_ref, spread):
    count, width = query_ref.shape
    blocks = width // LANES
    pairs = count // 2
    pitch = spread.shape[0] // blocks
    for c in range(blocks):
        spread[c * pitch:c * pitch + count, :] = query_ref[:, c * LANES:(c + 1) * LANES].astype(F32)
    for p in range(pairs):
        first = spread[pl.ds(p, blocks, stride=pitch), :]
        second = spread[pl.ds(p + pairs, blocks, stride=pitch), :]
        even, odd = swap_pair(first, second)
        out_ref[:blocks, p * LANES:(p + 1) * LANES] = even.astype(BF16)
        out_ref[blocks:, p * LANES:(p + 1) * LANES] = odd.astype(BF16)


def turned_queries(queries):
    total, width = queries.shape
    return pl.pallas_call(
        turn_kernel,
        out_shape=jax.ShapeDtypeStruct((K_OUT, total * K_IN), BF16),
        grid=(total // HALF,),
        in_specs=[pl.BlockSpec((HALF, width), lambda step: (step, 0))],
        out_specs=pl.BlockSpec((K_OUT, HALF * K_IN), lambda step: (0, step)),
        scratch_shapes=[pltpu.VMEM((width // LANES * (HALF + 8), LANES), F32)],
        compiler_params=pltpu.CompilerParams(vmem_limit_bytes=VMEM_LIMIT),
        cost_estimate=pl.CostEstimate(flops=4096 * total * width, bytes_accessed=4 * total * width, transcendentals=0),
        name="turn_queries",
    )(queries)


def damped(cov, total_count):
    rows = lax.broadcasted_iota(jnp.int32, (K_OUT, LANES), 0)
    lanes = lax.broadcasted_iota(jnp.int32, (K_OUT, LANES), 1)
    low = lanes < K_IN
    diagonal = rows == jnp.where(low, lanes, lanes - K_IN)
    cov = cov * (1.0 / total_count)
    on_diagonal = jnp.sum(jnp.where(diagonal, cov, 0.0), axis=0, keepdims=True)
    low_row = low_half(1)
    in_mean = jnp.sum(jnp.where(low_row, on_diagonal, 0.0), axis=1, keepdims=True) / K_IN
    out_mean = jnp.sum(jnp.where(low_row, 0.0, on_diagonal), axis=1, keepdims=True) / K_OUT
    scale = jnp.where(low_row, 1.0 / in_mean, 1.0)
    added = jnp.where(low_row, 0.1, 0.1 * out_mean)
    return cov * scale + jnp.where(diagonal, added, 0.0)


def inverses(matrix):
    size = matrix.shape[0]
    sub = 8
    lanes = lax.broadcasted_iota(jnp.int32, (sub, LANES), 1)
    offset = jnp.where(lanes < size, 0, size)
    place = lanes - offset
    row = lax.broadcasted_iota(jnp.int32, (sub, LANES), 0)
    tiles = [matrix[k:k + sub, :] for k in range(0, size, sub)]

    def spread_row(values, at):
        return jnp.broadcast_to(values[at:at + 1, :], (sub, LANES))

    def column(values, lane):
        return jnp.take_along_axis(values, offset + lane, axis=1, mode="promise_in_bounds")

    for begin in range(0, size, PIVOT):
        owner, first_row = begin // sub, begin % sub
        inside = (place >= begin) & (place < begin + PIVOT)
        columns = [[column(tile, begin + a) for a in range(PIVOT)] for tile in tiles]
        p = [[None] * PIVOT for _ in range(PIVOT)]
        for a in range(PIVOT):
            for b in range(a, PIVOT):
                p[a][b] = p[b][a] = spread_row(columns[owner][b], first_row + a)
        r = []
        for a in range(PIVOT):
            unit = jnp.where(place == begin + a, 1.0, 0.0)
            r.append(jnp.where(inside, unit, spread_row(tiles[owner], first_row + a)))
        det = 1.0 / (p[0][0] * p[1][1] - p[0][1] * p[1][0])
        across = -p[0][1] * det
        e = [[p[1][1] * det, across], [across, p[0][0] * det]]
        u = [[e[a][0] * p[0][b] + e[a][1] * p[1][b] for b in (2, 3)] for a in (0, 1)]
        s = [p[a][b + 2] - (p[a][0] * u[0][b] + p[a][1] * u[1][b]) for a, b in ((2, 0), (2, 1), (3, 1))]
        det = 1.0 / (s[0] * s[2] - s[1] * s[1])
        across = -s[1] * det
        f = [[s[2] * det, across], [across, s[0] * det]]
        w = [e[a][0] * r[0] + e[a][1] * r[1] for a in (0, 1)]
        t = [r[a] - (p[a][0] * w[0] + p[a][1] * w[1]) for a in (2, 3)]
        last = [f[a][0] * t[0] + f[a][1] * t[1] for a in (0, 1)]
        first = [w[a] - (u[a][0] * last[0] + u[a][1] * last[1]) for a in (0, 1)]
        solved = first + last
        for k in range(len(tiles)):
            rest = jnp.where(inside, 0.0, tiles[k])
            part = [columns[k][a] * solved[a] for a in range(PIVOT)]
            rest = (rest - (part[0] + part[1])) - (part[2] + part[3])
            if k == owner:
                for a in range(PIVOT):
                    rest = jnp.where(row == first_row + a, solved[a], rest)
            tiles[k] = rest
    return jnp.concatenate(tiles, axis=0)


def inverse_kernel(total_count, cov_ref, left_ref, right_ref):
    inverse = inverses(damped(cov_ref[...], total_count))
    turned = pltpu.roll(inverse, LANES // 2, 1)
    low = low_half(K_OUT)
    left_ref[...] = jnp.concatenate(split(turned[:, :K_OUT], 3), axis=0)
    double = jnp.concatenate([jnp.where(low, inverse, 0.0), jnp.where(low, 0.0, turned)], axis=0)
    high, small = split(double, 2)
    right_ref[:LANES, :LANES] = high
    right_ref[:LANES, LANES:] = small
    right_ref[LANES:, :LANES] = high
    right_ref[LANES:, LANES:] = jnp.zeros_like(small)


def inverse_factors(cov, total_count):
    return pl.pallas_call(
        functools.partial(inverse_kernel, total_count),
        out_shape=(
            jax.ShapeDtypeStruct((3 * K_OUT, K_OUT), BF16),
            jax.ShapeDtypeStruct((2 * LANES, 2 * LANES), BF16),
        ),
        in_specs=[pl.BlockSpec(memory_space=pltpu.VMEM)],
        out_specs=(pl.BlockSpec(memory_space=pltpu.VMEM), pl.BlockSpec(memory_space=pltpu.VMEM)),
        compiler_params=pltpu.CompilerParams(vmem_limit_bytes=VMEM_LIMIT),
        cost_estimate=pl.CostEstimate(flops=INVERSE_COST, bytes_accessed=0, transcendentals=0),
        name="inverses",
    )(cov)


def score_kernel(route_ref, left_ref, right_ref, first_ref, second_ref, train_ref, out_ref, solved, wide, ready):
    blocks = K_OUT // 2
    pairs = HALF // 2
    pitch = solved.shape[0] // (2 * pairs)
    step = pl.program_id(0)
    group = 4
    for side, turned_ref in enumerate((first_ref, second_ref)):
        for g in range(pairs // group):
            block = turned_ref[:, g * group * LANES:(g + 1) * group * LANES]
            terms = jnp.dot(left_ref[...], block, preferred_element_type=F32)
            once = terms[:K_OUT, :] + (terms[K_OUT:2 * K_OUT, :] + terms[2 * K_OUT:, :])
            for k in range(group):
                high, small = split(once[:, k * LANES:(k + 1) * LANES], 2)
                at = (side * pairs + g * group + k) * K_OUT
                wide[at:at + K_OUT, :LANES] = high
                wide[at:at + K_OUT, LANES:] = small
    twice = jnp.dot(wide[...], right_ref[...], preferred_element_type=F32)
    for p in range(2 * pairs):
        part = twice[p * K_OUT:(p + 1) * K_OUT, :]
        solved[p * pitch:p * pitch + K_OUT, :] = part[:, :LANES] + part[:, LANES:]
    for c in range(blocks):
        first = solved[pl.ds(c, 2 * pairs, stride=pitch), :]
        second = solved[pl.ds(c + blocks, 2 * pairs, stride=pitch), :]
        even, odd = swap_pair(first, second)
        columns = slice(c * LANES, (c + 1) * LANES)
        for side in range(2):
            at = side * HALF
            ready[at:at + pairs, columns] = even[side * pairs:(side + 1) * pairs, :].astype(BF16)
            ready[at + pairs:at + HALF, columns] = odd[side * pairs:(side + 1) * pairs, :].astype(BF16)
    scores = lax.dot_general(ready[...], train_ref[...], NT, preferred_element_type=F32)
    per_query = out_ref.shape[2]
    parts = out_ref.shape[1]
    for s in range(CHUNK // per_query):
        owner = route_ref[step * (CHUNK // per_query) + s]
        for part in range(parts):
            piece = scores[s * per_query:(s + 1) * per_query, part * LANES:(part + 1) * LANES]
            out_ref[owner, part, :, :] = piece


def all_scores(route, factors, turned, train, per_query):
    shard_count = route.shape[0]
    examples, width = train.shape
    steps = shard_count * per_query // CHUNK
    parts = examples // LANES
    if len(turned) == 2:
        places = [lambda step: (0, 0), lambda step: (0, 0)]
    else:
        turned = turned * 2
        places = [lambda step: (0, 2 * step), lambda step: (0, 2 * step + 1)]
    return pl.pallas_call(
        score_kernel,
        out_shape=jax.ShapeDtypeStruct((shard_count, parts, per_query, LANES), F32),
        grid=(steps,),
        in_specs=[
            pl.BlockSpec(memory_space=pltpu.SMEM),
            pl.BlockSpec((3 * K_OUT, K_OUT), lambda step: (0, 0)),
            pl.BlockSpec((2 * LANES, 2 * LANES), lambda step: (0, 0)),
            pl.BlockSpec((K_OUT, HALF * K_IN), places[0]),
            pl.BlockSpec((K_OUT, HALF * K_IN), places[1]),
            pl.BlockSpec((examples, width), lambda step: (0, 0)),
        ],
        out_specs=pl.BlockSpec((shard_count, parts, per_query, LANES), lambda step: (0, 0, 0, 0)),
        scratch_shapes=[
            pltpu.VMEM((HALF * (K_OUT + 8), LANES), F32),
            pltpu.VMEM((HALF * K_OUT, 2 * LANES), BF16),
            pltpu.VMEM((CHUNK, width), BF16),
        ],
        compiler_params=pltpu.CompilerParams(vmem_limit_bytes=VMEM_LIMIT),
        cost_estimate=pl.CostEstimate(
            flops=2 * shard_count * per_query * width * (examples + 128), bytes_accessed=2 * examples * width, transcendentals=0
        ),
        name="products_and_scores",
    )(route, *factors, *turned, train)


def exchange(values, distance, count):
    return lax.ppermute(values, "dp", [(k, k ^ distance) for k in range(count)])


def shards(train_grads, query_grads, listed):
    shard_count = lax.axis_size("dp")
    layers = lax.axis_size("layer")
    own_index = lax.axis_index("dp").astype(jnp.int32)
    examples = train_grads.shape[0]
    per_query = query_grads.shape[0]
    train = train_grads.reshape(examples, train_grads.shape[2])
    own_queries = query_grads.reshape(per_query, query_grads.shape[2])
    total_count = float(examples * shard_count)
    order = jnp.arange(shard_count, dtype=jnp.int32)
    if shard_count == 8:
        far = exchange(own_queries, 4, shard_count)
        cov = covariance_sums(train)
        far, _ = lax.optimization_barrier((far, cov))
        column = jnp.concatenate([own_queries, far], axis=0)
        cov = cov + exchange(cov, 1, shard_count)
        near = exchange(column, 2, shard_count)
        column = jnp.concatenate([column, near], axis=0)
        cov = cov + exchange(cov, 4, shard_count)
        beside = exchange(column, 1, shard_count)
        last = exchange(cov, 2, shard_count)
        here, cov = lax.optimization_barrier((turned_queries(column), cov))
        factors = inverse_factors(cov + last, total_count)
        beside, _ = lax.optimization_barrier((beside, factors[0]))
        turned = [here, turned_queries(beside)]
        order = jnp.array([0, 4, 2, 6, 1, 5, 3, 7], jnp.int32)
        route = own_index ^ order
    else:
        turned = [turned_queries(lax.all_gather(own_queries, "dp", axis=0, tiled=True))]
        cov = lax.psum(covariance_sums(train), "dp")
        factors = inverse_factors(cov, total_count)
        route = order
    scores = all_scores(route, factors, turned, train, per_query)
    outgoing = scores.reshape(shard_count * layers, per_query, examples // layers)
    wanted = listed[0][:, None] == jnp.arange(shard_count, dtype=jnp.int32)[None, :]
    wanted, outgoing = lax.optimization_barrier((wanted, outgoing))
    received = lax.all_to_all(outgoing, ("dp", "layer"), split_axis=0, concat_axis=0, tiled=True)
    received = received.reshape(1, shard_count, layers, per_query, examples // layers)
    return jnp.sum(jnp.where(wanted[:, :, None, None, None], received, 0.0), axis=(1, 2))


def solution(mesh):
    in_specs = (
        P(("groups", "dp"), "layer", None),
        P(("groups", "dp"), "layer", None),
        P(("groups", "dp"), None),
    )
    out_specs = P(("groups", "dp"), None, "layer")
    return jax.shard_map(shards, mesh=mesh, in_specs=in_specs, out_specs=out_specs, check_vma=False)
```

```python
import functools
import jax
import jax.numpy as jnp
from jax import lax
from jax.experimental import pallas as pl
from jax.experimental.pallas import tpu as pltpu
from jax.sharding import PartitionSpec as P

K_OUT = 64
K_IN = 64
LANES = 128
CHUNK = 64
HALF = CHUNK // 2
PIVOT = 4
F32 = jnp.float32
BF16 = jnp.bfloat16
VMEM_LIMIT = 48 * 1024 * 1024
INVERSE_COST = 2 * 10**9
STAGE_VMEM_LIMIT = 105 * 512 * 1024

NT = (((1,), (1,)), ((), ()))


def low_half(rows):
    return lax.broadcasted_iota(jnp.int32, (rows, LANES), 1) < LANES // 2


def swap_pair(first, second):
    low = low_half(first.shape[0])
    even = jnp.where(low, first, pltpu.roll(second, LANES // 2, 1))
    odd = jnp.where(low, pltpu.roll(first, LANES // 2, 1), second)
    return even, odd


def split(values, terms):
    parts = []
    for _ in range(terms):
        part = values.astype(BF16)
        parts.append(part)
        values = values - part.astype(F32)
    return parts


def covariance_kernel(train_ref, cov_ref, held, turned, by_in, by_out, arrived):
    examples, width = train_ref.shape
    blocks = width // LANES
    parts = examples // LANES
    pitch = turned.shape[1] // blocks
    chunks, _, chunk = held.shape
    copies = []
    for g in range(chunks):
        source = train_ref.at[:, pl.ds(g * chunk, chunk)]
        copies.append(pltpu.make_async_copy(source, held.at[g], arrived.at[g]))
        copies[-1].start()
    for c in range(blocks):
        if c * LANES % chunk == 0:
            copies[c * LANES // chunk].wait()
        begin = c * LANES % chunk
        block = held[c * LANES // chunk, :, begin:begin + LANES].astype(F32).T
        for part in range(parts):
            turned[part, c * pitch:c * pitch + LANES, :] = block[:, part * LANES:(part + 1) * LANES]
        for half in range(2):
            start = (2 * c + half) * examples
            by_in[:, start:start + examples] = block[half * K_IN:(half + 1) * K_IN, :].astype(BF16)
    for j in range(K_IN):
        for part in range(parts):
            start = j * examples + part * LANES
            for half in range(2):
                rows = turned[part, pl.ds(half * K_IN + j, blocks, stride=pitch), :]
                by_out[half * blocks:(half + 1) * blocks, start:start + LANES] = rows.astype(BF16)
    in_sum = lax.dot_general(by_in[...], by_in[...], NT, preferred_element_type=F32)
    out_sum = lax.dot_general(by_out[...], by_out[...], NT, preferred_element_type=F32)
    cov_ref[...] = jnp.concatenate([in_sum, out_sum], axis=1)


def covariance_sums(train):
    examples, width = train.shape
    chunks = 4 if width % (4 * LANES) == 0 else 1
    return pl.pallas_call(
        covariance_kernel,
        out_shape=jax.ShapeDtypeStruct((K_OUT, 2 * K_IN), F32),
        in_specs=[pl.BlockSpec(memory_space=pltpu.HBM)],
        out_specs=pl.BlockSpec(memory_space=pltpu.VMEM),
        scratch_shapes=[
            pltpu.VMEM((chunks, examples, width // chunks), BF16),
            pltpu.VMEM((examples // LANES, width // LANES * (LANES + 8), LANES), F32),
            pltpu.VMEM((K_IN, K_OUT * examples), BF16),
            pltpu.VMEM((K_OUT, K_IN * examples), BF16),
            pltpu.SemaphoreType.DMA((chunks,)),
        ],
        compiler_params=pltpu.CompilerParams(vmem_limit_bytes=STAGE_VMEM_LIMIT),
        cost_estimate=pl.CostEstimate(flops=64 * examples * 64**3, bytes_accessed=2 * examples * width, transcendentals=0),
        name="covariance",
    )(train)


def turn_kernel(query_ref, out_ref, spread):
    count, width = query_ref.shape
    blocks = width // LANES
    pairs = count // 2
    pitch = spread.shape[0] // blocks
    for c in range(blocks):
        spread[c * pitch:c * pitch + count, :] = query_ref[:, c * LANES:(c + 1) * LANES].astype(F32)
    for p in range(pairs):
        first = spread[pl.ds(p, blocks, stride=pitch), :]
        second = spread[pl.ds(p + pairs, blocks, stride=pitch), :]
        even, odd = swap_pair(first, second)
        out_ref[:blocks, p * LANES:(p + 1) * LANES] = even.astype(BF16)
        out_ref[blocks:, p * LANES:(p + 1) * LANES] = odd.astype(BF16)


def turned_queries(queries):
    total, width = queries.shape
    return pl.pallas_call(
        turn_kernel,
        out_shape=jax.ShapeDtypeStruct((K_OUT, total * K_IN), BF16),
        grid=(total // HALF,),
        in_specs=[pl.BlockSpec((HALF, width), lambda step: (step, 0))],
        out_specs=pl.BlockSpec((K_OUT, HALF * K_IN), lambda step: (0, step)),
        scratch_shapes=[pltpu.VMEM((width // LANES * (HALF + 8), LANES), F32)],
        compiler_params=pltpu.CompilerParams(vmem_limit_bytes=VMEM_LIMIT),
        cost_estimate=pl.CostEstimate(flops=4096 * total * width, bytes_accessed=4 * total * width, transcendentals=0),
        name="turn_queries",
    )(queries)


def damped(cov, total_count):
    rows = lax.broadcasted_iota(jnp.int32, (K_OUT, LANES), 0)
    lanes = lax.broadcasted_iota(jnp.int32, (K_OUT, LANES), 1)
    low = lanes < K_IN
    diagonal = rows == jnp.where(low, lanes, lanes - K_IN)
    cov = cov * (1.0 / total_count)
    on_diagonal = jnp.sum(jnp.where(diagonal, cov, 0.0), axis=0, keepdims=True)
    low_row = low_half(1)
    in_mean = jnp.sum(jnp.where(low_row, on_diagonal, 0.0), axis=1, keepdims=True) / K_IN
    out_mean = jnp.sum(jnp.where(low_row, 0.0, on_diagonal), axis=1, keepdims=True) / K_OUT
    scale = jnp.where(low_row, 1.0 / in_mean, 1.0)
    added = jnp.where(low_row, 0.1, 0.1 * out_mean)
    return cov * scale + jnp.where(diagonal, added, 0.0)


def inverses(matrix):
    size = matrix.shape[0]
    sub = 8
    lanes = lax.broadcasted_iota(jnp.int32, (sub, LANES), 1)
    offset = jnp.where(lanes < size, 0, size)
    place = lanes - offset
    row = lax.broadcasted_iota(jnp.int32, (sub, LANES), 0)
    tiles = [matrix[k:k + sub, :] for k in range(0, size, sub)]

    def spread_row(values, at):
        return jnp.broadcast_to(values[at:at + 1, :], (sub, LANES))

    def column(values, lane):
        return jnp.take_along_axis(values, offset + lane, axis=1, mode="promise_in_bounds")

    for begin in range(0, size, PIVOT):
        owner, first_row = begin // sub, begin % sub
        inside = (place >= begin) & (place < begin + PIVOT)
        columns = [[column(tile, begin + a) for a in range(PIVOT)] for tile in tiles]
        p = [[None] * PIVOT for _ in range(PIVOT)]
        for a in range(PIVOT):
            for b in range(a, PIVOT):
                p[a][b] = p[b][a] = spread_row(columns[owner][b], first_row + a)
        r = []
        for a in range(PIVOT):
            unit = jnp.where(place == begin + a, 1.0, 0.0)
            r.append(jnp.where(inside, unit, spread_row(tiles[owner], first_row + a)))
        det = 1.0 / (p[0][0] * p[1][1] - p[0][1] * p[1][0])
        across = -p[0][1] * det
        e = [[p[1][1] * det, across], [across, p[0][0] * det]]
        u = [[e[a][0] * p[0][b] + e[a][1] * p[1][b] for b in (2, 3)] for a in (0, 1)]
        s = [p[a][b + 2] - (p[a][0] * u[0][b] + p[a][1] * u[1][b]) for a, b in ((2, 0), (2, 1), (3, 1))]
        det = 1.0 / (s[0] * s[2] - s[1] * s[1])
        across = -s[1] * det
        f = [[s[2] * det, across], [across, s[0] * det]]
        w = [e[a][0] * r[0] + e[a][1] * r[1] for a in (0, 1)]
        t = [r[a] - (p[a][0] * w[0] + p[a][1] * w[1]) for a in (2, 3)]
        last = [f[a][0] * t[0] + f[a][1] * t[1] for a in (0, 1)]
        first = [w[a] - (u[a][0] * last[0] + u[a][1] * last[1]) for a in (0, 1)]
        solved = first + last
        for k in range(len(tiles)):
            rest = jnp.where(inside, 0.0, tiles[k])
            part = [columns[k][a] * solved[a] for a in range(PIVOT)]
            rest = (rest - (part[0] + part[1])) - (part[2] + part[3])
            if k == owner:
                for a in range(PIVOT):
                    rest = jnp.where(row == first_row + a, solved[a], rest)
            tiles[k] = rest
    return jnp.concatenate(tiles, axis=0)


def inverse_kernel(total_count, cov_ref, left_ref, right_ref):
    inverse = inverses(damped(cov_ref[...], total_count))
    turned = pltpu.roll(inverse, LANES // 2, 1)
    low = low_half(K_OUT)
    left_ref[...] = jnp.concatenate(split(turned[:, :K_OUT], 3), axis=0)
    double = jnp.concatenate([jnp.where(low, inverse, 0.0), jnp.where(low, 0.0, turned)], axis=0)
    high, small = split(double, 2)
    right_ref[:LANES, :] = high
    right_ref[LANES:2 * LANES, :] = high
    right_ref[2 * LANES:, :] = small


def inverse_factors(cov, total_count):
    return pl.pallas_call(
        functools.partial(inverse_kernel, total_count),
        out_shape=(
            jax.ShapeDtypeStruct((3 * K_OUT, K_OUT), BF16),
            jax.ShapeDtypeStruct((3 * LANES, LANES), BF16),
        ),
        in_specs=[pl.BlockSpec(memory_space=pltpu.VMEM)],
        out_specs=(pl.BlockSpec(memory_space=pltpu.VMEM), pl.BlockSpec(memory_space=pltpu.VMEM)),
        compiler_params=pltpu.CompilerParams(vmem_limit_bytes=VMEM_LIMIT),
        cost_estimate=pl.CostEstimate(flops=INVERSE_COST, bytes_accessed=0, transcendentals=0),
        name="inverses",
    )(cov)


def score_kernel(route_ref, left_ref, right_ref, first_ref, second_ref, train_ref, out_ref, solved, wide, ready):
    blocks = K_OUT // 2
    pairs = HALF // 2
    pitch = solved.shape[0] // (2 * pairs)
    step = pl.program_id(0)
    group = 4
    for side, turned_ref in enumerate((first_ref, second_ref)):
        for g in range(pairs // group):
            block = turned_ref[:, g * group * LANES:(g + 1) * group * LANES]
            terms = jnp.dot(left_ref[...], block, preferred_element_type=F32)
            once = terms[:K_OUT, :] + (terms[K_OUT:2 * K_OUT, :] + terms[2 * K_OUT:, :])
            for k in range(group):
                high, small = split(once[:, k * LANES:(k + 1) * LANES], 2)
                at = (side * pairs + g * group + k) * K_OUT
                wide[at:at + K_OUT, :LANES] = high
                wide[at:at + K_OUT, LANES:2 * LANES] = small
                wide[at:at + K_OUT, 2 * LANES:] = high
    twice = jnp.dot(wide[...], right_ref[...], preferred_element_type=F32)
    for p in range(2 * pairs):
        solved[p * pitch:p * pitch + K_OUT, :] = twice[p * K_OUT:(p + 1) * K_OUT, :]
    for c in range(blocks):
        first = solved[pl.ds(c, 2 * pairs, stride=pitch), :]
        second = solved[pl.ds(c + blocks, 2 * pairs, stride=pitch), :]
        even, odd = swap_pair(first, second)
        columns = slice(c * LANES, (c + 1) * LANES)
        for side in range(2):
            at = side * HALF
            ready[at:at + pairs, columns] = even[side * pairs:(side + 1) * pairs, :].astype(BF16)
            ready[at + pairs:at + HALF, columns] = odd[side * pairs:(side + 1) * pairs, :].astype(BF16)
    scores = lax.dot_general(ready[...], train_ref[...], NT, preferred_element_type=F32)
    per_query = out_ref.shape[2]
    parts = out_ref.shape[1]
    for s in range(CHUNK // per_query):
        owner = route_ref[step * (CHUNK // per_query) + s]
        for part in range(parts):
            piece = scores[s * per_query:(s + 1) * per_query, part * LANES:(part + 1) * LANES]
            out_ref[owner, part, :, :] = piece


def all_scores(route, factors, turned, train, per_query):
    shard_count = route.shape[0]
    examples, width = train.shape
    steps = shard_count * per_query // CHUNK
    parts = examples // LANES
    if len(turned) == 2:
        places = [lambda step: (0, 0), lambda step: (0, 0)]
    else:
        turned = turned * 2
        places = [lambda step: (0, 2 * step), lambda step: (0, 2 * step + 1)]
    return pl.pallas_call(
        score_kernel,
        out_shape=jax.ShapeDtypeStruct((shard_count, parts, per_query, LANES), F32),
        grid=(steps,),
        in_specs=[
            pl.BlockSpec(memory_space=pltpu.SMEM),
            pl.BlockSpec((3 * K_OUT, K_OUT), lambda step: (0, 0)),
            pl.BlockSpec((3 * LANES, LANES), lambda step: (0, 0)),
            pl.BlockSpec((K_OUT, HALF * K_IN), places[0]),
            pl.BlockSpec((K_OUT, HALF * K_IN), places[1]),
            pl.BlockSpec((examples, width), lambda step: (0, 0)),
        ],
        out_specs=pl.BlockSpec((shard_count, parts, per_query, LANES), lambda step: (0, 0, 0, 0)),
        scratch_shapes=[
            pltpu.VMEM((HALF * (K_OUT + 8), LANES), F32),
            pltpu.VMEM((HALF * K_OUT, 3 * LANES), BF16),
            pltpu.VMEM((CHUNK, width), BF16),
        ],
        compiler_params=pltpu.CompilerParams(vmem_limit_bytes=VMEM_LIMIT),
        cost_estimate=pl.CostEstimate(
            flops=2 * shard_count * per_query * width * (examples + 128), bytes_accessed=2 * examples * width, transcendentals=0
        ),
        name="products_and_scores",
    )(route, *factors, *turned, train)


def exchange(values, distance, count):
    return lax.ppermute(values, "dp", [(k, k ^ distance) for k in range(count)])


def shards(train_grads, query_grads, listed):
    shard_count = lax.axis_size("dp")
    layers = lax.axis_size("layer")
    own_index = lax.axis_index("dp").astype(jnp.int32)
    examples = train_grads.shape[0]
    per_query = query_grads.shape[0]
    train = train_grads.reshape(examples, train_grads.shape[2])
    own_queries = query_grads.reshape(per_query, query_grads.shape[2])
    total_count = float(examples * shard_count)
    order = jnp.arange(shard_count, dtype=jnp.int32)
    if shard_count == 8:
        far = exchange(own_queries, 4, shard_count)
        cov = covariance_sums(train)
        far, _ = lax.optimization_barrier((far, cov))
        column = jnp.concatenate([own_queries, far], axis=0)
        cov = cov + exchange(cov, 1, shard_count)
        near = exchange(column, 2, shard_count)
        column = jnp.concatenate([column, near], axis=0)
        cov = cov + exchange(cov, 4, shard_count)
        beside = exchange(column, 1, shard_count)
        last = exchange(cov, 2, shard_count)
        here, cov = lax.optimization_barrier((turned_queries(column), cov))
        factors = inverse_factors(cov + last, total_count)
        beside, _ = lax.optimization_barrier((beside, factors[0]))
        turned = [here, turned_queries(beside)]
        order = jnp.array([0, 4, 2, 6, 1, 5, 3, 7], jnp.int32)
        route = own_index ^ order
    else:
        turned = [turned_queries(lax.all_gather(own_queries, "dp", axis=0, tiled=True))]
        cov = lax.psum(covariance_sums(train), "dp")
        factors = inverse_factors(cov, total_count)
        route = order
    scores = all_scores(route, factors, turned, train, per_query)
    outgoing = scores.reshape(shard_count * layers, per_query, examples // layers)
    wanted = listed[0][:, None] == jnp.arange(shard_count, dtype=jnp.int32)[None, :]
    wanted, outgoing = lax.optimization_barrier((wanted, outgoing))
    received = lax.all_to_all(outgoing, ("dp", "layer"), split_axis=0, concat_axis=0, tiled=True)
    received = received.reshape(1, shard_count, layers, per_query, examples // layers)
    return jnp.sum(jnp.where(wanted[:, :, None, None, None], received, 0.0), axis=(1, 2))


def solution(mesh):
    in_specs = (
        P(("groups", "dp"), "layer", None),
        P(("groups", "dp"), "layer", None),
        P(("groups", "dp"), None),
    )
    out_specs = P(("groups", "dp"), None, "layer")
    return jax.shard_map(shards, mesh=mesh, in_specs=in_specs, out_specs=out_specs, check_vma=False)
```

```python
import functools
import jax
import jax.numpy as jnp
from jax import lax
from jax.experimental import pallas as pl
from jax.experimental.pallas import tpu as pltpu
from jax.sharding import PartitionSpec as P

K_OUT = 64
K_IN = 64
LANES = 128
CHUNK = 64
HALF = CHUNK // 2
PIVOT = 4
F32 = jnp.float32
BF16 = jnp.bfloat16
VMEM_LIMIT = 48 * 1024 * 1024
INVERSE_COST = 2 * 10**9
STAGE_VMEM_LIMIT = 105 * 512 * 1024

NT = (((1,), (1,)), ((), ()))


def low_half(rows):
    return lax.broadcasted_iota(jnp.int32, (rows, LANES), 1) < LANES // 2


def swap_pair(first, second):
    low = low_half(first.shape[0])
    even = jnp.where(low, first, pltpu.roll(second, LANES // 2, 1))
    odd = jnp.where(low, pltpu.roll(first, LANES // 2, 1), second)
    return even, odd


def split(values, terms):
    parts = []
    for _ in range(terms):
        part = values.astype(BF16)
        parts.append(part)
        values = values - part.astype(F32)
    return parts


def covariance_kernel(train_ref, cov_ref, held, turned, by_in, by_out, arrived):
    examples, width = train_ref.shape
    blocks = width // LANES
    parts = examples // LANES
    pitch = turned.shape[1] // blocks
    chunks, _, chunk = held.shape
    copies = []
    for g in range(chunks):
        source = train_ref.at[:, pl.ds(g * chunk, chunk)]
        copies.append(pltpu.make_async_copy(source, held.at[g], arrived.at[g]))
        copies[-1].start()
    for c in range(blocks):
        if c * LANES % chunk == 0:
            copies[c * LANES // chunk].wait()
        begin = c * LANES % chunk
        block = held[c * LANES // chunk, :, begin:begin + LANES].astype(F32).T
        for part in range(parts):
            turned[part, c * pitch:c * pitch + LANES, :] = block[:, part * LANES:(part + 1) * LANES]
        for half in range(2):
            start = (2 * c + half) * examples
            by_in[:, start:start + examples] = block[half * K_IN:(half + 1) * K_IN, :].astype(BF16)
    for j in range(K_IN):
        for part in range(parts):
            start = j * examples + part * LANES
            for half in range(2):
                rows = turned[part, pl.ds(half * K_IN + j, blocks, stride=pitch), :]
                by_out[half * blocks:(half + 1) * blocks, start:start + LANES] = rows.astype(BF16)
    in_sum = lax.dot_general(by_in[...], by_in[...], NT, preferred_element_type=F32)
    out_sum = lax.dot_general(by_out[...], by_out[...], NT, preferred_element_type=F32)
    cov_ref[...] = jnp.concatenate([in_sum, out_sum], axis=1)


def covariance_sums(train):
    examples, width = train.shape
    chunks = 4 if width % (4 * LANES) == 0 else 1
    return pl.pallas_call(
        covariance_kernel,
        out_shape=jax.ShapeDtypeStruct((K_OUT, 2 * K_IN), F32),
        in_specs=[pl.BlockSpec(memory_space=pltpu.HBM)],
        out_specs=pl.BlockSpec(memory_space=pltpu.VMEM),
        scratch_shapes=[
            pltpu.VMEM((chunks, examples, width // chunks), BF16),
            pltpu.VMEM((examples // LANES, width // LANES * (LANES + 8), LANES), F32),
            pltpu.VMEM((K_IN, K_OUT * examples), BF16),
            pltpu.VMEM((K_OUT, K_IN * examples), BF16),
            pltpu.SemaphoreType.DMA((chunks,)),
        ],
        compiler_params=pltpu.CompilerParams(vmem_limit_bytes=STAGE_VMEM_LIMIT),
        cost_estimate=pl.CostEstimate(flops=64 * examples * 64**3, bytes_accessed=2 * examples * width, transcendentals=0),
        name="covariance",
    )(train)


def turn_kernel(query_ref, out_ref, spread):
    count, width = query_ref.shape
    blocks = width // LANES
    pairs = count // 2
    pitch = spread.shape[0] // blocks
    for c in range(blocks):
        spread[c * pitch:c * pitch + count, :] = query_ref[:, c * LANES:(c + 1) * LANES].astype(F32)
    for p in range(pairs):
        first = spread[pl.ds(p, blocks, stride=pitch), :]
        second = spread[pl.ds(p + pairs, blocks, stride=pitch), :]
        even, odd = swap_pair(first, second)
        out_ref[:blocks, p * LANES:(p + 1) * LANES] = even.astype(BF16)
        out_ref[blocks:, p * LANES:(p + 1) * LANES] = odd.astype(BF16)


def turned_queries(queries):
    total, width = queries.shape
    return pl.pallas_call(
        turn_kernel,
        out_shape=jax.ShapeDtypeStruct((K_OUT, total * K_IN), BF16),
        grid=(total // HALF,),
        in_specs=[pl.BlockSpec((HALF, width), lambda step: (step, 0))],
        out_specs=pl.BlockSpec((K_OUT, HALF * K_IN), lambda step: (0, step)),
        scratch_shapes=[pltpu.VMEM((width // LANES * (HALF + 8), LANES), F32)],
        compiler_params=pltpu.CompilerParams(vmem_limit_bytes=VMEM_LIMIT),
        cost_estimate=pl.CostEstimate(flops=4096 * total * width, bytes_accessed=4 * total * width, transcendentals=0),
        name="turn_queries",
    )(queries)


def damped(cov, total_count):
    rows = lax.broadcasted_iota(jnp.int32, (K_OUT, LANES), 0)
    lanes = lax.broadcasted_iota(jnp.int32, (K_OUT, LANES), 1)
    low = lanes < K_IN
    diagonal = rows == jnp.where(low, lanes, lanes - K_IN)
    cov = cov * (1.0 / total_count)
    on_diagonal = jnp.sum(jnp.where(diagonal, cov, 0.0), axis=0, keepdims=True)
    low_row = low_half(1)
    in_mean = jnp.sum(jnp.where(low_row, on_diagonal, 0.0), axis=1, keepdims=True) / K_IN
    out_mean = jnp.sum(jnp.where(low_row, 0.0, on_diagonal), axis=1, keepdims=True) / K_OUT
    scale = jnp.where(low_row, 1.0 / in_mean, 1.0)
    added = jnp.where(low_row, 0.1, 0.1 * out_mean)
    return cov * scale + jnp.where(diagonal, added, 0.0)


def inverses(matrix):
    size = matrix.shape[0]
    sub = 8
    lanes = lax.broadcasted_iota(jnp.int32, (sub, LANES), 1)
    offset = jnp.where(lanes < size, 0, size)
    place = lanes - offset
    row = lax.broadcasted_iota(jnp.int32, (sub, LANES), 0)
    tiles = [matrix[k:k + sub, :] for k in range(0, size, sub)]

    def spread_row(values, at):
        return jnp.broadcast_to(values[at:at + 1, :], (sub, LANES))

    def column(values, lane):
        return jnp.take_along_axis(values, offset + lane, axis=1, mode="promise_in_bounds")

    for begin in range(0, size, PIVOT):
        owner, first_row = begin // sub, begin % sub
        inside = (place >= begin) & (place < begin + PIVOT)
        columns = [[column(tile, begin + a) for a in range(PIVOT)] for tile in tiles]
        p = [[None] * PIVOT for _ in range(PIVOT)]
        for a in range(PIVOT):
            for b in range(a, PIVOT):
                p[a][b] = p[b][a] = spread_row(columns[owner][b], first_row + a)
        r = []
        for a in range(PIVOT):
            unit = jnp.where(place == begin + a, 1.0, 0.0)
            r.append(jnp.where(inside, unit, spread_row(tiles[owner], first_row + a)))
        det = 1.0 / (p[0][0] * p[1][1] - p[0][1] * p[1][0])
        across = -p[0][1] * det
        e = [[p[1][1] * det, across], [across, p[0][0] * det]]
        u = [[e[a][0] * p[0][b] + e[a][1] * p[1][b] for b in (2, 3)] for a in (0, 1)]
        s = [p[a][b + 2] - (p[a][0] * u[0][b] + p[a][1] * u[1][b]) for a, b in ((2, 0), (2, 1), (3, 1))]
        det = 1.0 / (s[0] * s[2] - s[1] * s[1])
        across = -s[1] * det
        f = [[s[2] * det, across], [across, s[0] * det]]
        w = [e[a][0] * r[0] + e[a][1] * r[1] for a in (0, 1)]
        t = [r[a] - (p[a][0] * w[0] + p[a][1] * w[1]) for a in (2, 3)]
        last = [f[a][0] * t[0] + f[a][1] * t[1] for a in (0, 1)]
        first = [w[a] - (u[a][0] * last[0] + u[a][1] * last[1]) for a in (0, 1)]
        solved = first + last
        for k in range(len(tiles)):
            rest = jnp.where(inside, 0.0, tiles[k])
            part = [columns[k][a] * solved[a] for a in range(PIVOT)]
            rest = (rest - (part[0] + part[1])) - (part[2] + part[3])
            if k == owner:
                for a in range(PIVOT):
                    rest = jnp.where(row == first_row + a, solved[a], rest)
            tiles[k] = rest
    return jnp.concatenate(tiles, axis=0)


def inverse_kernel(total_count, cov_ref, left_ref, right_ref):
    inverse = inverses(damped(cov_ref[...], total_count))
    turned = pltpu.roll(inverse, LANES // 2, 1)
    low = low_half(K_OUT)
    left_ref[...] = jnp.concatenate(split(turned[:, :K_OUT], 3), axis=0)
    double = jnp.concatenate([jnp.where(low, inverse, 0.0), jnp.where(low, 0.0, turned)], axis=0)
    high, small = split(double, 2)
    right_ref[:LANES, :LANES] = high
    right_ref[:LANES, LANES:] = small
    right_ref[LANES:, :LANES] = high
    right_ref[LANES:, LANES:] = jnp.zeros_like(small)


def inverse_factors(cov, total_count):
    return pl.pallas_call(
        functools.partial(inverse_kernel, total_count),
        out_shape=(
            jax.ShapeDtypeStruct((3 * K_OUT, K_OUT), BF16),
            jax.ShapeDtypeStruct((2 * LANES, 2 * LANES), BF16),
        ),
        in_specs=[pl.BlockSpec(memory_space=pltpu.VMEM)],
        out_specs=(pl.BlockSpec(memory_space=pltpu.VMEM), pl.BlockSpec(memory_space=pltpu.VMEM)),
        compiler_params=pltpu.CompilerParams(vmem_limit_bytes=VMEM_LIMIT),
        cost_estimate=pl.CostEstimate(flops=INVERSE_COST, bytes_accessed=0, transcendentals=0),
        name="inverses",
    )(cov)


def score_kernel(route_ref, left_ref, right_ref, first_ref, second_ref, train_ref, out_ref, solved, wide, ready):
    blocks = K_OUT // 2
    pairs = HALF // 2
    pitch = solved.shape[0] // (2 * pairs)
    step = pl.program_id(0)
    group = 4
    for side, turned_ref in enumerate((first_ref, second_ref)):
        for g in range(pairs // group):
            block = turned_ref[:, g * group * LANES:(g + 1) * group * LANES]
            terms = jnp.dot(left_ref[...], block, preferred_element_type=F32)
            once = terms[:K_OUT, :] + (terms[K_OUT:2 * K_OUT, :] + terms[2 * K_OUT:, :])
            for k in range(group):
                high, small = split(once[:, k * LANES:(k + 1) * LANES], 2)
                at = (side * pairs + g * group + k) * K_OUT
                wide[at:at + K_OUT, :LANES] = high
                wide[at:at + K_OUT, LANES:] = small
    twice = jnp.dot(wide[...], right_ref[...], preferred_element_type=F32)
    for p in range(2 * pairs):
        part = twice[p * K_OUT:(p + 1) * K_OUT, :]
        solved[p * pitch:p * pitch + K_OUT, :] = part[:, :LANES] + part[:, LANES:]
    for c in range(blocks):
        first = solved[pl.ds(c, 2 * pairs, stride=pitch), :]
        second = solved[pl.ds(c + blocks, 2 * pairs, stride=pitch), :]
        even, odd = swap_pair(first, second)
        columns = slice(c * LANES, (c + 1) * LANES)
        for side in range(2):
            at = side * HALF
            ready[at:at + pairs, columns] = even[side * pairs:(side + 1) * pairs, :].astype(BF16)
            ready[at + pairs:at + HALF, columns] = odd[side * pairs:(side + 1) * pairs, :].astype(BF16)
    scores = lax.dot_general(ready[...], train_ref[...], NT, preferred_element_type=F32)
    per_query = out_ref.shape[2]
    parts = out_ref.shape[1]
    for s in range(CHUNK // per_query):
        owner = route_ref[step * (CHUNK // per_query) + s]
        for part in range(parts):
            piece = scores[s * per_query:(s + 1) * per_query, part * LANES:(part + 1) * LANES]
            out_ref[owner, part, :, :] = piece


def all_scores(route, factors, turned, train, per_query):
    shard_count = route.shape[0]
    examples, width = train.shape
    steps = shard_count * per_query // CHUNK
    parts = examples // LANES
    if len(turned) == 2:
        places = [lambda step: (0, 0), lambda step: (0, 0)]
    else:
        turned = turned * 2
        places = [lambda step: (0, 2 * step), lambda step: (0, 2 * step + 1)]
    return pl.pallas_call(
        score_kernel,
        out_shape=jax.ShapeDtypeStruct((shard_count, parts, per_query, LANES), F32),
        grid=(steps,),
        in_specs=[
            pl.BlockSpec(memory_space=pltpu.SMEM),
            pl.BlockSpec((3 * K_OUT, K_OUT), lambda step: (0, 0)),
            pl.BlockSpec((2 * LANES, 2 * LANES), lambda step: (0, 0)),
            pl.BlockSpec((K_OUT, HALF * K_IN), places[0]),
            pl.BlockSpec((K_OUT, HALF * K_IN), places[1]),
            pl.BlockSpec((examples, width), lambda step: (0, 0)),
        ],
        out_specs=pl.BlockSpec((shard_count, parts, per_query, LANES), lambda step: (0, 0, 0, 0)),
        scratch_shapes=[
            pltpu.VMEM((HALF * (K_OUT + 8), LANES), F32),
            pltpu.VMEM((HALF * K_OUT, 2 * LANES), BF16),
            pltpu.VMEM((CHUNK, width), BF16),
        ],
        compiler_params=pltpu.CompilerParams(vmem_limit_bytes=VMEM_LIMIT),
        cost_estimate=pl.CostEstimate(
            flops=2 * shard_count * per_query * width * (examples + 128), bytes_accessed=2 * examples * width, transcendentals=0
        ),
        name="products_and_scores",
    )(route, *factors, *turned, train)


def exchange(values, distance, count):
    return lax.ppermute(values, "dp", [(k, k ^ distance) for k in range(count)])


def shards(train_grads, query_grads, listed):
    shard_count = lax.axis_size("dp")
    layers = lax.axis_size("layer")
    own_index = lax.axis_index("dp").astype(jnp.int32)
    examples = train_grads.shape[0]
    per_query = query_grads.shape[0]
    train = train_grads.reshape(examples, train_grads.shape[2])
    own_queries = query_grads.reshape(per_query, query_grads.shape[2])
    total_count = float(examples * shard_count)
    order = jnp.arange(shard_count, dtype=jnp.int32)
    if shard_count == 8:
        far = exchange(own_queries, 4, shard_count)
        cov = covariance_sums(train)
        far, _ = lax.optimization_barrier((far, cov))
        column = jnp.concatenate([own_queries, far], axis=0)
        cov = cov + exchange(cov, 1, shard_count)
        near = exchange(column, 2, shard_count)
        column = jnp.concatenate([column, near], axis=0)
        cov = cov + exchange(cov, 4, shard_count)
        beside = exchange(column, 1, shard_count)
        last = exchange(cov, 2, shard_count)
        here, cov = lax.optimization_barrier((turned_queries(column), cov))
        factors = inverse_factors(cov + last, total_count)
        beside, _ = lax.optimization_barrier((beside, factors[0]))
        turned = [here, turned_queries(beside)]
        order = jnp.array([0, 4, 2, 6, 1, 5, 3, 7], jnp.int32)
        route = own_index ^ order
    else:
        turned = [turned_queries(lax.all_gather(own_queries, "dp", axis=0, tiled=True))]
        cov = lax.psum(covariance_sums(train), "dp")
        factors = inverse_factors(cov, total_count)
        route = order
    scores = all_scores(route, factors, turned, train, per_query)
    outgoing = scores.reshape(shard_count * layers, per_query, examples // layers)
    wanted = listed[0][:, None] == jnp.arange(shard_count, dtype=jnp.int32)[None, :]
    wanted, outgoing = lax.optimization_barrier((wanted, outgoing))
    received = lax.all_to_all(outgoing, ("dp", "layer"), split_axis=0, concat_axis=0, tiled=True)
    received = received.reshape(1, shard_count, layers, per_query, examples // layers)
    return jnp.sum(jnp.where(wanted[:, :, None, None, None], received, 0.0), axis=(1, 2))


def solution(mesh):
    in_specs = (
        P(("groups", "dp"), "layer", None),
        P(("groups", "dp"), "layer", None),
        P(("groups", "dp"), None),
    )
    out_specs = P(("groups", "dp"), None, "layer")
    return jax.shard_map(shards, mesh=mesh, in_specs=in_specs, out_specs=out_specs, check_vma=False)
```

```python
import functools
import jax
import jax.numpy as jnp
from jax import lax
from jax.experimental import pallas as pl
from jax.experimental.pallas import tpu as pltpu
from jax.sharding import PartitionSpec as P

K_OUT = 64
K_IN = 64
LANES = 128
CHUNK = 64
HALF = CHUNK // 2
PIVOT = 4
F32 = jnp.float32
BF16 = jnp.bfloat16
VMEM_LIMIT = 48 * 1024 * 1024
INVERSE_COST = 2 * 10**9
STAGE_VMEM_LIMIT = 105 * 512 * 1024

NT = (((1,), (1,)), ((), ()))


def low_half(rows):
    return lax.broadcasted_iota(jnp.int32, (rows, LANES), 1) < LANES // 2


def swap_pair(first, second):
    low = low_half(first.shape[0])
    even = jnp.where(low, first, pltpu.roll(second, LANES // 2, 1))
    odd = jnp.where(low, pltpu.roll(first, LANES // 2, 1), second)
    return even, odd


def split(values, terms):
    parts = []
    for _ in range(terms):
        part = values.astype(BF16)
        parts.append(part)
        values = values - part.astype(F32)
    return parts


def covariance_kernel(train_ref, cov_ref, held, turned, by_in, by_out, arrived):
    examples, width = train_ref.shape
    blocks = width // LANES
    parts = examples // LANES
    pitch = turned.shape[1] // blocks
    chunks, _, chunk = held.shape
    copies = []
    for g in range(chunks):
        source = train_ref.at[:, pl.ds(g * chunk, chunk)]
        copies.append(pltpu.make_async_copy(source, held.at[g], arrived.at[g]))
        copies[-1].start()
    for c in range(blocks):
        if c * LANES % chunk == 0:
            copies[c * LANES // chunk].wait()
        begin = c * LANES % chunk
        block = held[c * LANES // chunk, :, begin:begin + LANES].astype(F32).T
        for part in range(parts):
            turned[part, c * pitch:c * pitch + LANES, :] = block[:, part * LANES:(part + 1) * LANES]
        for half in range(2):
            start = (2 * c + half) * examples
            by_in[:, start:start + examples] = block[half * K_IN:(half + 1) * K_IN, :].astype(BF16)
    for j in range(K_IN):
        for part in range(parts):
            start = j * examples + part * LANES
            for half in range(2):
                rows = turned[part, pl.ds(half * K_IN + j, blocks, stride=pitch), :]
                by_out[half * blocks:(half + 1) * blocks, start:start + LANES] = rows.astype(BF16)
    in_sum = lax.dot_general(by_in[...], by_in[...], NT, preferred_element_type=F32)
    out_sum = lax.dot_general(by_out[...], by_out[...], NT, preferred_element_type=F32)
    cov_ref[...] = jnp.concatenate([in_sum, out_sum], axis=1)


def covariance_sums(train):
    examples, width = train.shape
    chunks = 2 if width % (2 * LANES) == 0 else 1
    return pl.pallas_call(
        covariance_kernel,
        out_shape=jax.ShapeDtypeStruct((K_OUT, 2 * K_IN), F32),
        in_specs=[pl.BlockSpec(memory_space=pltpu.HBM)],
        out_specs=pl.BlockSpec(memory_space=pltpu.VMEM),
        scratch_shapes=[
            pltpu.VMEM((chunks, examples, width // chunks), BF16),
            pltpu.VMEM((examples // LANES, width // LANES * (LANES + 8), LANES), F32),
            pltpu.VMEM((K_IN, K_OUT * examples), BF16),
            pltpu.VMEM((K_OUT, K_IN * examples), BF16),
            pltpu.SemaphoreType.DMA((chunks,)),
        ],
        compiler_params=pltpu.CompilerParams(vmem_limit_bytes=STAGE_VMEM_LIMIT),
        cost_estimate=pl.CostEstimate(flops=64 * examples * 64**3, bytes_accessed=2 * examples * width, transcendentals=0),
        name="covariance",
    )(train)


def turn_kernel(query_ref, out_ref, spread):
    count, width = query_ref.shape
    blocks = width // LANES
    pairs = count // 2
    pitch = spread.shape[0] // blocks
    for c in range(blocks):
        spread[c * pitch:c * pitch + count, :] = query_ref[:, c * LANES:(c + 1) * LANES].astype(F32)
    for p in range(pairs):
        first = spread[pl.ds(p, blocks, stride=pitch), :]
        second = spread[pl.ds(p + pairs, blocks, stride=pitch), :]
        even, odd = swap_pair(first, second)
        out_ref[:blocks, p * LANES:(p + 1) * LANES] = even.astype(BF16)
        out_ref[blocks:, p * LANES:(p + 1) * LANES] = odd.astype(BF16)


def turned_queries(queries):
    total, width = queries.shape
    return pl.pallas_call(
        turn_kernel,
        out_shape=jax.ShapeDtypeStruct((K_OUT, total * K_IN), BF16),
        grid=(total // HALF,),
        in_specs=[pl.BlockSpec((HALF, width), lambda step: (step, 0))],
        out_specs=pl.BlockSpec((K_OUT, HALF * K_IN), lambda step: (0, step)),
        scratch_shapes=[pltpu.VMEM((width // LANES * (HALF + 8), LANES), F32)],
        compiler_params=pltpu.CompilerParams(vmem_limit_bytes=VMEM_LIMIT),
        cost_estimate=pl.CostEstimate(flops=4096 * total * width, bytes_accessed=4 * total * width, transcendentals=0),
        name="turn_queries",
    )(queries)


def damped(cov, total_count):
    rows = lax.broadcasted_iota(jnp.int32, (K_OUT, LANES), 0)
    lanes = lax.broadcasted_iota(jnp.int32, (K_OUT, LANES), 1)
    low = lanes < K_IN
    diagonal = rows == jnp.where(low, lanes, lanes - K_IN)
    cov = cov * (1.0 / total_count)
    on_diagonal = jnp.sum(jnp.where(diagonal, cov, 0.0), axis=0, keepdims=True)
    low_row = low_half(1)
    in_mean = jnp.sum(jnp.where(low_row, on_diagonal, 0.0), axis=1, keepdims=True) / K_IN
    out_mean = jnp.sum(jnp.where(low_row, 0.0, on_diagonal), axis=1, keepdims=True) / K_OUT
    scale = jnp.where(low_row, 1.0 / in_mean, 1.0)
    added = jnp.where(low_row, 0.1, 0.1 * out_mean)
    return cov * scale + jnp.where(diagonal, added, 0.0)


def inverses(matrix):
    size = matrix.shape[0]
    sub = 8
    lanes = lax.broadcasted_iota(jnp.int32, (sub, LANES), 1)
    offset = jnp.where(lanes < size, 0, size)
    place = lanes - offset
    row = lax.broadcasted_iota(jnp.int32, (sub, LANES), 0)
    tiles = [matrix[k:k + sub, :] for k in range(0, size, sub)]

    def spread_row(values, at):
        return jnp.broadcast_to(values[at:at + 1, :], (sub, LANES))

    def column(values, lane):
        return jnp.take_along_axis(values, offset + lane, axis=1, mode="promise_in_bounds")

    for begin in range(0, size, PIVOT):
        owner, first_row = begin // sub, begin % sub
        inside = (place >= begin) & (place < begin + PIVOT)
        columns = [[column(tile, begin + a) for a in range(PIVOT)] for tile in tiles]
        p = [[None] * PIVOT for _ in range(PIVOT)]
        for a in range(PIVOT):
            for b in range(a, PIVOT):
                p[a][b] = p[b][a] = spread_row(columns[owner][b], first_row + a)
        r = []
        for a in range(PIVOT):
            unit = jnp.where(place == begin + a, 1.0, 0.0)
            r.append(jnp.where(inside, unit, spread_row(tiles[owner], first_row + a)))
        det = 1.0 / (p[0][0] * p[1][1] - p[0][1] * p[1][0])
        across = -p[0][1] * det
        e = [[p[1][1] * det, across], [across, p[0][0] * det]]
        u = [[e[a][0] * p[0][b] + e[a][1] * p[1][b] for b in (2, 3)] for a in (0, 1)]
        s = [p[a][b + 2] - (p[a][0] * u[0][b] + p[a][1] * u[1][b]) for a, b in ((2, 0), (2, 1), (3, 1))]
        det = 1.0 / (s[0] * s[2] - s[1] * s[1])
        across = -s[1] * det
        f = [[s[2] * det, across], [across, s[0] * det]]
        w = [e[a][0] * r[0] + e[a][1] * r[1] for a in (0, 1)]
        t = [r[a] - (p[a][0] * w[0] + p[a][1] * w[1]) for a in (2, 3)]
        last = [f[a][0] * t[0] + f[a][1] * t[1] for a in (0, 1)]
        first = [w[a] - (u[a][0] * last[0] + u[a][1] * last[1]) for a in (0, 1)]
        solved = first + last
        for k in range(len(tiles)):
            rest = jnp.where(inside, 0.0, tiles[k])
            part = [columns[k][a] * solved[a] for a in range(PIVOT)]
            rest = (rest - (part[0] + part[1])) - (part[2] + part[3])
            if k == owner:
                for a in range(PIVOT):
                    rest = jnp.where(row == first_row + a, solved[a], rest)
            tiles[k] = rest
    return jnp.concatenate(tiles, axis=0)


def inverse_kernel(total_count, cov_ref, left_ref, right_ref):
    inverse = inverses(damped(cov_ref[...], total_count))
    turned = pltpu.roll(inverse, LANES // 2, 1)
    low = low_half(K_OUT)
    left_ref[...] = jnp.concatenate(split(turned[:, :K_OUT], 3), axis=0)
    double = jnp.concatenate([jnp.where(low, inverse, 0.0), jnp.where(low, 0.0, turned)], axis=0)
    high, small = split(double, 2)
    right_ref[:LANES, :LANES] = high
    right_ref[:LANES, LANES:] = small
    right_ref[LANES:, :LANES] = high
    right_ref[LANES:, LANES:] = jnp.zeros_like(small)


def inverse_factors(cov, total_count):
    return pl.pallas_call(
        functools.partial(inverse_kernel, total_count),
        out_shape=(
            jax.ShapeDtypeStruct((3 * K_OUT, K_OUT), BF16),
            jax.ShapeDtypeStruct((2 * LANES, 2 * LANES), BF16),
        ),
        in_specs=[pl.BlockSpec(memory_space=pltpu.VMEM)],
        out_specs=(pl.BlockSpec(memory_space=pltpu.VMEM), pl.BlockSpec(memory_space=pltpu.VMEM)),
        compiler_params=pltpu.CompilerParams(vmem_limit_bytes=VMEM_LIMIT),
        cost_estimate=pl.CostEstimate(flops=INVERSE_COST, bytes_accessed=0, transcendentals=0),
        name="inverses",
    )(cov)


def score_kernel(route_ref, left_ref, right_ref, first_ref, second_ref, train_ref, out_ref, solved, wide, ready):
    blocks = K_OUT // 2
    pairs = HALF // 2
    pitch = solved.shape[0] // (2 * pairs)
    step = pl.program_id(0)
    group = 8
    for side, turned_ref in enumerate((first_ref, second_ref)):
        for g in range(pairs // group):
            block = turned_ref[:, g * group * LANES:(g + 1) * group * LANES]
            terms = jnp.dot(left_ref[...], block, preferred_element_type=F32)
            once = terms[:K_OUT, :] + (terms[K_OUT:2 * K_OUT, :] + terms[2 * K_OUT:, :])
            for k in range(group):
                high, small = split(once[:, k * LANES:(k + 1) * LANES], 2)
                at = (side * pairs + g * group + k) * K_OUT
                wide[at:at + K_OUT, :LANES] = high
                wide[at:at + K_OUT, LANES:] = small
    twice = jnp.dot(wide[...], right_ref[...], preferred_element_type=F32)
    for p in range(2 * pairs):
        part = twice[p * K_OUT:(p + 1) * K_OUT, :]
        solved[p * pitch:p * pitch + K_OUT, :] = part[:, :LANES] + part[:, LANES:]
    for c in range(blocks):
        first = solved[pl.ds(c, 2 * pairs, stride=pitch), :]
        second = solved[pl.ds(c + blocks, 2 * pairs, stride=pitch), :]
        even, odd = swap_pair(first, second)
        columns = slice(c * LANES, (c + 1) * LANES)
        for side in range(2):
            at = side * HALF
            ready[at:at + pairs, columns] = even[side * pairs:(side + 1) * pairs, :].astype(BF16)
            ready[at + pairs:at + HALF, columns] = odd[side * pairs:(side + 1) * pairs, :].astype(BF16)
    scores = lax.dot_general(ready[...], train_ref[...], NT, preferred_element_type=F32)
    per_query = out_ref.shape[2]
    parts = out_ref.shape[1]
    for s in range(CHUNK // per_query):
        owner = route_ref[step * (CHUNK // per_query) + s]
        for part in range(parts):
            piece = scores[s * per_query:(s + 1) * per_query, part * LANES:(part + 1) * LANES]
            out_ref[owner, part, :, :] = piece


def all_scores(route, factors, turned, train, per_query):
    shard_count = route.shape[0]
    examples, width = train.shape
    steps = shard_count * per_query // CHUNK
    parts = examples // LANES
    if len(turned) == 2:
        places = [lambda step: (0, 0), lambda step: (0, 0)]
    else:
        turned = turned * 2
        places = [lambda step: (0, 2 * step), lambda step: (0, 2 * step + 1)]
    return pl.pallas_call(
        score_kernel,
        out_shape=jax.ShapeDtypeStruct((shard_count, parts, per_query, LANES), F32),
        grid=(steps,),
        in_specs=[
            pl.BlockSpec(memory_space=pltpu.SMEM),
            pl.BlockSpec((3 * K_OUT, K_OUT), lambda step: (0, 0)),
            pl.BlockSpec((2 * LANES, 2 * LANES), lambda step: (0, 0)),
            pl.BlockSpec((K_OUT, HALF * K_IN), places[0]),
            pl.BlockSpec((K_OUT, HALF * K_IN), places[1]),
            pl.BlockSpec((examples, width), lambda step: (0, 0)),
        ],
        out_specs=pl.BlockSpec((shard_count, parts, per_query, LANES), lambda step: (0, 0, 0, 0)),
        scratch_shapes=[
            pltpu.VMEM((HALF * (K_OUT + 8), LANES), F32),
            pltpu.VMEM((HALF * K_OUT, 2 * LANES), BF16),
            pltpu.VMEM((CHUNK, width), BF16),
        ],
        compiler_params=pltpu.CompilerParams(vmem_limit_bytes=VMEM_LIMIT),
        cost_estimate=pl.CostEstimate(
            flops=2 * shard_count * per_query * width * (examples + 128), bytes_accessed=2 * examples * width, transcendentals=0
        ),
        name="products_and_scores",
    )(route, *factors, *turned, train)


def exchange(values, distance, count):
    return lax.ppermute(values, "dp", [(k, k ^ distance) for k in range(count)])


def shards(train_grads, query_grads, listed):
    shard_count = lax.axis_size("dp")
    layers = lax.axis_size("layer")
    own_index = lax.axis_index("dp").astype(jnp.int32)
    examples = train_grads.shape[0]
    per_query = query_grads.shape[0]
    train = train_grads.reshape(examples, train_grads.shape[2])
    own_queries = query_grads.reshape(per_query, query_grads.shape[2])
    total_count = float(examples * shard_count)
    order = jnp.arange(shard_count, dtype=jnp.int32)
    if shard_count == 8:
        far = exchange(own_queries, 4, shard_count)
        cov = covariance_sums(train)
        far, _ = lax.optimization_barrier((far, cov))
        column = jnp.concatenate([own_queries, far], axis=0)
        cov = cov + exchange(cov, 1, shard_count)
        near = exchange(column, 2, shard_count)
        column = jnp.concatenate([column, near], axis=0)
        cov = cov + exchange(cov, 4, shard_count)
        beside = exchange(column, 1, shard_count)
        last = exchange(cov, 2, shard_count)
        here, cov = lax.optimization_barrier((turned_queries(column), cov))
        factors = inverse_factors(cov + last, total_count)
        beside, _ = lax.optimization_barrier((beside, factors[0]))
        turned = [here, turned_queries(beside)]
        order = jnp.array([0, 4, 2, 6, 1, 5, 3, 7], jnp.int32)
        route = own_index ^ order
    else:
        turned = [turned_queries(lax.all_gather(own_queries, "dp", axis=0, tiled=True))]
        cov = lax.psum(covariance_sums(train), "dp")
        factors = inverse_factors(cov, total_count)
        route = order
    scores = all_scores(route, factors, turned, train, per_query)
    outgoing = scores.reshape(shard_count * layers, per_query, examples // layers)
    wanted = listed[0][:, None] == jnp.arange(shard_count, dtype=jnp.int32)[None, :]
    wanted, outgoing = lax.optimization_barrier((wanted, outgoing))
    received = lax.all_to_all(outgoing, ("dp", "layer"), split_axis=0, concat_axis=0, tiled=True)
    received = received.reshape(1, shard_count, layers, per_query, examples // layers)
    return jnp.sum(jnp.where(wanted[:, :, None, None, None], received, 0.0), axis=(1, 2))


def solution(mesh):
    in_specs = (
        P(("groups", "dp"), "layer", None),
        P(("groups", "dp"), "layer", None),
        P(("groups", "dp"), None),
    )
    out_specs = P(("groups", "dp"), None, "layer")
    return jax.shard_map(shards, mesh=mesh, in_specs=in_specs, out_specs=out_specs, check_vma=False)
```

```python
import functools
import jax
import jax.numpy as jnp
from jax import lax
from jax.experimental import pallas as pl
from jax.experimental.pallas import tpu as pltpu
from jax.sharding import PartitionSpec as P

K_OUT = 64
K_IN = 64
LANES = 128
CHUNK = 64
HALF = CHUNK // 2
PIVOT = 4
F32 = jnp.float32
BF16 = jnp.bfloat16
VMEM_LIMIT = 48 * 1024 * 1024
INVERSE_COST = 2 * 10**9
STAGE_VMEM_LIMIT = 105 * 512 * 1024

NT = (((1,), (1,)), ((), ()))


def low_half(rows):
    return lax.broadcasted_iota(jnp.int32, (rows, LANES), 1) < LANES // 2


def swap_pair(first, second):
    low = low_half(first.shape[0])
    even = jnp.where(low, first, pltpu.roll(second, LANES // 2, 1))
    odd = jnp.where(low, pltpu.roll(first, LANES // 2, 1), second)
    return even, odd


def split(values, terms):
    parts = []
    for _ in range(terms):
        part = values.astype(BF16)
        parts.append(part)
        values = values - part.astype(F32)
    return parts


def covariance_kernel(train_ref, cov_ref, held, turned, by_in, by_out, arrived):
    examples, width = train_ref.shape
    blocks = width // LANES
    parts = examples // LANES
    pitch = turned.shape[1] // blocks
    chunks, _, chunk = held.shape
    copies = []
    for g in range(chunks):
        source = train_ref.at[:, pl.ds(g * chunk, chunk)]
        copies.append(pltpu.make_async_copy(source, held.at[g], arrived.at[g]))
        copies[-1].start()
    for c in range(blocks):
        if c * LANES % chunk == 0:
            copies[c * LANES // chunk].wait()
        begin = c * LANES % chunk
        block = held[c * LANES // chunk, :, begin:begin + LANES].astype(F32).T
        for part in range(parts):
            turned[part, c * pitch:c * pitch + LANES, :] = block[:, part * LANES:(part + 1) * LANES]
        for half in range(2):
            start = (2 * c + half) * examples
            by_in[:, start:start + examples] = block[half * K_IN:(half + 1) * K_IN, :].astype(BF16)
    for j in range(K_IN):
        for part in range(parts):
            start = j * examples + part * LANES
            for half in range(2):
                rows = turned[part, pl.ds(half * K_IN + j, blocks, stride=pitch), :]
                by_out[half * blocks:(half + 1) * blocks, start:start + LANES] = rows.astype(BF16)
    in_sum = lax.dot_general(by_in[...], by_in[...], NT, preferred_element_type=F32)
    out_sum = lax.dot_general(by_out[...], by_out[...], NT, preferred_element_type=F32)
    cov_ref[...] = jnp.concatenate([in_sum, out_sum], axis=1)


def covariance_sums(train):
    examples, width = train.shape
    chunks = 4 if width % (4 * LANES) == 0 else 1
    return pl.pallas_call(
        covariance_kernel,
        out_shape=jax.ShapeDtypeStruct((K_OUT, 2 * K_IN), F32),
        in_specs=[pl.BlockSpec(memory_space=pltpu.HBM)],
        out_specs=pl.BlockSpec(memory_space=pltpu.VMEM),
        scratch_shapes=[
            pltpu.VMEM((chunks, examples, width // chunks), BF16),
            pltpu.VMEM((examples // LANES, width // LANES * (LANES + 8), LANES), F32),
            pltpu.VMEM((K_IN, K_OUT * examples), BF16),
            pltpu.VMEM((K_OUT, K_IN * examples), BF16),
            pltpu.SemaphoreType.DMA((chunks,)),
        ],
        compiler_params=pltpu.CompilerParams(vmem_limit_bytes=STAGE_VMEM_LIMIT),
        cost_estimate=pl.CostEstimate(flops=64 * examples * 64**3, bytes_accessed=2 * examples * width, transcendentals=0),
        name="covariance",
    )(train)


def turn_kernel(query_ref, out_ref, spread):
    count, width = query_ref.shape
    blocks = width // LANES
    pairs = count // 2
    pitch = spread.shape[0] // blocks
    for c in range(blocks):
        spread[c * pitch:c * pitch + count, :] = query_ref[:, c * LANES:(c + 1) * LANES].astype(F32)
    for p in range(pairs):
        first = spread[pl.ds(p, blocks, stride=pitch), :]
        second = spread[pl.ds(p + pairs, blocks, stride=pitch), :]
        even, odd = swap_pair(first, second)
        out_ref[:blocks, p * LANES:(p + 1) * LANES] = even.astype(BF16)
        out_ref[blocks:, p * LANES:(p + 1) * LANES] = odd.astype(BF16)


def turned_queries(queries):
    total, width = queries.shape
    return pl.pallas_call(
        turn_kernel,
        out_shape=jax.ShapeDtypeStruct((K_OUT, total * K_IN), BF16),
        grid=(total // HALF,),
        in_specs=[pl.BlockSpec((HALF, width), lambda step: (step, 0))],
        out_specs=pl.BlockSpec((K_OUT, HALF * K_IN), lambda step: (0, step)),
        scratch_shapes=[pltpu.VMEM((width // LANES * (HALF + 8), LANES), F32)],
        compiler_params=pltpu.CompilerParams(vmem_limit_bytes=VMEM_LIMIT),
        cost_estimate=pl.CostEstimate(flops=4096 * total * width, bytes_accessed=4 * total * width, transcendentals=0),
        name="turn_queries",
    )(queries)


def damped(cov, total_count):
    rows = lax.broadcasted_iota(jnp.int32, (K_OUT, LANES), 0)
    lanes = lax.broadcasted_iota(jnp.int32, (K_OUT, LANES), 1)
    low = lanes < K_IN
    diagonal = rows == jnp.where(low, lanes, lanes - K_IN)
    cov = cov * (1.0 / total_count)
    on_diagonal = jnp.sum(jnp.where(diagonal, cov, 0.0), axis=0, keepdims=True)
    low_row = low_half(1)
    in_mean = jnp.sum(jnp.where(low_row, on_diagonal, 0.0), axis=1, keepdims=True) / K_IN
    out_mean = jnp.sum(jnp.where(low_row, 0.0, on_diagonal), axis=1, keepdims=True) / K_OUT
    scale = jnp.where(low_row, 1.0 / in_mean, 1.0)
    added = jnp.where(low_row, 0.1, 0.1 * out_mean)
    return cov * scale + jnp.where(diagonal, added, 0.0)


def reciprocal(values):
    estimate = pl.reciprocal(values, approx=True)
    for _ in range(2):
        estimate = estimate * (2.0 - values * estimate)
    return estimate


def inverses(matrix):
    size = matrix.shape[0]
    sub = 8
    lanes = lax.broadcasted_iota(jnp.int32, (sub, LANES), 1)
    offset = jnp.where(lanes < size, 0, size)
    place = lanes - offset
    row = lax.broadcasted_iota(jnp.int32, (sub, LANES), 0)
    tiles = [matrix[k:k + sub, :] for k in range(0, size, sub)]

    def spread_row(values, at):
        return jnp.broadcast_to(values[at:at + 1, :], (sub, LANES))

    def column(values, lane):
        return jnp.take_along_axis(values, offset + lane, axis=1, mode="promise_in_bounds")

    for begin in range(0, size, PIVOT):
        owner, first_row = begin // sub, begin % sub
        inside = (place >= begin) & (place < begin + PIVOT)
        columns = [[column(tile, begin + a) for a in range(PIVOT)] for tile in tiles]
        p = [[None] * PIVOT for _ in range(PIVOT)]
        for a in range(PIVOT):
            for b in range(a, PIVOT):
                p[a][b] = p[b][a] = spread_row(columns[owner][b], first_row + a)
        r = []
        for a in range(PIVOT):
            unit = jnp.where(place == begin + a, 1.0, 0.0)
            r.append(jnp.where(inside, unit, spread_row(tiles[owner], first_row + a)))
        det = reciprocal(p[0][0] * p[1][1] - p[0][1] * p[1][0])
        across = -p[0][1] * det
        e = [[p[1][1] * det, across], [across, p[0][0] * det]]
        u = [[e[a][0] * p[0][b] + e[a][1] * p[1][b] for b in (2, 3)] for a in (0, 1)]
        s = [p[a][b + 2] - (p[a][0] * u[0][b] + p[a][1] * u[1][b]) for a, b in ((2, 0), (2, 1), (3, 1))]
        det = reciprocal(s[0] * s[2] - s[1] * s[1])
        across = -s[1] * det
        f = [[s[2] * det, across], [across, s[0] * det]]
        w = [e[a][0] * r[0] + e[a][1] * r[1] for a in (0, 1)]
        t = [r[a] - (p[a][0] * w[0] + p[a][1] * w[1]) for a in (2, 3)]
        last = [f[a][0] * t[0] + f[a][1] * t[1] for a in (0, 1)]
        first = [w[a] - (u[a][0] * last[0] + u[a][1] * last[1]) for a in (0, 1)]
        solved = first + last
        for k in range(len(tiles)):
            rest = jnp.where(inside, 0.0, tiles[k])
            part = [columns[k][a] * solved[a] for a in range(PIVOT)]
            rest = (rest - (part[0] + part[1])) - (part[2] + part[3])
            if k == owner:
                for a in range(PIVOT):
                    rest = jnp.where(row == first_row + a, solved[a], rest)
            tiles[k] = rest
    return jnp.concatenate(tiles, axis=0)


def inverse_kernel(total_count, cov_ref, left_ref, right_ref):
    inverse = inverses(damped(cov_ref[...], total_count))
    turned = pltpu.roll(inverse, LANES // 2, 1)
    low = low_half(K_OUT)
    left_ref[...] = jnp.concatenate(split(turned[:, :K_OUT], 3), axis=0)
    double = jnp.concatenate([jnp.where(low, inverse, 0.0), jnp.where(low, 0.0, turned)], axis=0)
    high, small = split(double, 2)
    right_ref[:LANES, :LANES] = high
    right_ref[:LANES, LANES:] = small
    right_ref[LANES:, :LANES] = high
    right_ref[LANES:, LANES:] = jnp.zeros_like(small)


def inverse_factors(cov, total_count):
    return pl.pallas_call(
        functools.partial(inverse_kernel, total_count),
        out_shape=(
            jax.ShapeDtypeStruct((3 * K_OUT, K_OUT), BF16),
            jax.ShapeDtypeStruct((2 * LANES, 2 * LANES), BF16),
        ),
        in_specs=[pl.BlockSpec(memory_space=pltpu.VMEM)],
        out_specs=(pl.BlockSpec(memory_space=pltpu.VMEM), pl.BlockSpec(memory_space=pltpu.VMEM)),
        compiler_params=pltpu.CompilerParams(vmem_limit_bytes=VMEM_LIMIT),
        cost_estimate=pl.CostEstimate(flops=INVERSE_COST, bytes_accessed=0, transcendentals=0),
        name="inverses",
    )(cov)


def score_kernel(route_ref, left_ref, right_ref, first_ref, second_ref, train_ref, out_ref, solved, wide, ready):
    blocks = K_OUT // 2
    pairs = HALF // 2
    pitch = solved.shape[0] // (2 * pairs)
    step = pl.program_id(0)
    group = 4
    for side, turned_ref in enumerate((first_ref, second_ref)):
        for g in range(pairs // group):
            block = turned_ref[:, g * group * LANES:(g + 1) * group * LANES]
            terms = jnp.dot(left_ref[...], block, preferred_element_type=F32)
            once = terms[:K_OUT, :] + (terms[K_OUT:2 * K_OUT, :] + terms[2 * K_OUT:, :])
            for k in range(group):
                high, small = split(once[:, k * LANES:(k + 1) * LANES], 2)
                at = (side * pairs + g * group + k) * K_OUT
                wide[at:at + K_OUT, :LANES] = high
                wide[at:at + K_OUT, LANES:] = small
    twice = jnp.dot(wide[...], right_ref[...], preferred_element_type=F32)
    for p in range(2 * pairs):
        part = twice[p * K_OUT:(p + 1) * K_OUT, :]
        solved[p * pitch:p * pitch + K_OUT, :] = part[:, :LANES] + part[:, LANES:]
    for c in range(blocks):
        first = solved[pl.ds(c, 2 * pairs, stride=pitch), :]
        second = solved[pl.ds(c + blocks, 2 * pairs, stride=pitch), :]
        even, odd = swap_pair(first, second)
        columns = slice(c * LANES, (c + 1) * LANES)
        for side in range(2):
            at = side * HALF
            ready[at:at + pairs, columns] = even[side * pairs:(side + 1) * pairs, :].astype(BF16)
            ready[at + pairs:at + HALF, columns] = odd[side * pairs:(side + 1) * pairs, :].astype(BF16)
    scores = lax.dot_general(ready[...], train_ref[...], NT, preferred_element_type=F32)
    per_query = out_ref.shape[2]
    parts = out_ref.shape[1]
    for s in range(CHUNK // per_query):
        owner = route_ref[step * (CHUNK // per_query) + s]
        for part in range(parts):
            piece = scores[s * per_query:(s + 1) * per_query, part * LANES:(part + 1) * LANES]
            out_ref[owner, part, :, :] = piece


def all_scores(route, factors, turned, train, per_query):
    shard_count = route.shape[0]
    examples, width = train.shape
    steps = shard_count * per_query // CHUNK
    parts = examples // LANES
    if len(turned) == 2:
        places = [lambda step: (0, 0), lambda step: (0, 0)]
    else:
        turned = turned * 2
        places = [lambda step: (0, 2 * step), lambda step: (0, 2 * step + 1)]
    return pl.pallas_call(
        score_kernel,
        out_shape=jax.ShapeDtypeStruct((shard_count, parts, per_query, LANES), F32),
        grid=(steps,),
        in_specs=[
            pl.BlockSpec(memory_space=pltpu.SMEM),
            pl.BlockSpec((3 * K_OUT, K_OUT), lambda step: (0, 0)),
            pl.BlockSpec((2 * LANES, 2 * LANES), lambda step: (0, 0)),
            pl.BlockSpec((K_OUT, HALF * K_IN), places[0]),
            pl.BlockSpec((K_OUT, HALF * K_IN), places[1]),
            pl.BlockSpec((examples, width), lambda step: (0, 0)),
        ],
        out_specs=pl.BlockSpec((shard_count, parts, per_query, LANES), lambda step: (0, 0, 0, 0)),
        scratch_shapes=[
            pltpu.VMEM((HALF * (K_OUT + 8), LANES), F32),
            pltpu.VMEM((HALF * K_OUT, 2 * LANES), BF16),
            pltpu.VMEM((CHUNK, width), BF16),
        ],
        compiler_params=pltpu.CompilerParams(vmem_limit_bytes=VMEM_LIMIT),
        cost_estimate=pl.CostEstimate(
            flops=2 * shard_count * per_query * width * (examples + 128), bytes_accessed=2 * examples * width, transcendentals=0
        ),
        name="products_and_scores",
    )(route, *factors, *turned, train)


def exchange(values, distance, count):
    return lax.ppermute(values, "dp", [(k, k ^ distance) for k in range(count)])


def shards(train_grads, query_grads, listed):
    shard_count = lax.axis_size("dp")
    layers = lax.axis_size("layer")
    own_index = lax.axis_index("dp").astype(jnp.int32)
    examples = train_grads.shape[0]
    per_query = query_grads.shape[0]
    train = train_grads.reshape(examples, train_grads.shape[2])
    own_queries = query_grads.reshape(per_query, query_grads.shape[2])
    total_count = float(examples * shard_count)
    order = jnp.arange(shard_count, dtype=jnp.int32)
    if shard_count == 8:
        far = exchange(own_queries, 4, shard_count)
        cov = covariance_sums(train)
        far, _ = lax.optimization_barrier((far, cov))
        column = jnp.concatenate([own_queries, far], axis=0)
        cov = cov + exchange(cov, 1, shard_count)
        near = exchange(column, 2, shard_count)
        column = jnp.concatenate([column, near], axis=0)
        cov = cov + exchange(cov, 4, shard_count)
        beside = exchange(column, 1, shard_count)
        last = exchange(cov, 2, shard_count)
        here, cov = lax.optimization_barrier((turned_queries(column), cov))
        factors = inverse_factors(cov + last, total_count)
        beside, _ = lax.optimization_barrier((beside, factors[0]))
        turned = [here, turned_queries(beside)]
        order = jnp.array([0, 4, 2, 6, 1, 5, 3, 7], jnp.int32)
        route = own_index ^ order
    else:
        turned = [turned_queries(lax.all_gather(own_queries, "dp", axis=0, tiled=True))]
        cov = lax.psum(covariance_sums(train), "dp")
        factors = inverse_factors(cov, total_count)
        route = order
    scores = all_scores(route, factors, turned, train, per_query)
    outgoing = scores.reshape(shard_count * layers, per_query, examples // layers)
    wanted = listed[0][:, None] == jnp.arange(shard_count, dtype=jnp.int32)[None, :]
    wanted, outgoing = lax.optimization_barrier((wanted, outgoing))
    received = lax.all_to_all(outgoing, ("dp", "layer"), split_axis=0, concat_axis=0, tiled=True)
    received = received.reshape(1, shard_count, layers, per_query, examples // layers)
    return jnp.sum(jnp.where(wanted[:, :, None, None, None], received, 0.0), axis=(1, 2))


def solution(mesh):
    in_specs = (
        P(("groups", "dp"), "layer", None),
        P(("groups", "dp"), "layer", None),
        P(("groups", "dp"), None),
    )
    out_specs = P(("groups", "dp"), None, "layer")
    return jax.shard_map(shards, mesh=mesh, in_specs=in_specs, out_specs=out_specs, check_vma=False)
```

```python
import functools
import jax
import jax.numpy as jnp
from jax import lax
from jax.experimental import pallas as pl
from jax.experimental.pallas import tpu as pltpu
from jax.sharding import PartitionSpec as P

K_OUT = 64
K_IN = 64
LANES = 128
CHUNK = 64
HALF = CHUNK // 2
PIVOT = 4
F32 = jnp.float32
BF16 = jnp.bfloat16
VMEM_LIMIT = 48 * 1024 * 1024
INVERSE_COST = 2 * 10**9
STAGE_VMEM_LIMIT = 105 * 512 * 1024

NT = (((1,), (1,)), ((), ()))


def low_half(rows):
    return lax.broadcasted_iota(jnp.int32, (rows, LANES), 1) < LANES // 2


def swap_pair(first, second):
    low = low_half(first.shape[0])
    even = jnp.where(low, first, pltpu.roll(second, LANES // 2, 1))
    odd = jnp.where(low, pltpu.roll(first, LANES // 2, 1), second)
    return even, odd


def split(values, terms):
    parts = []
    for _ in range(terms):
        part = values.astype(BF16)
        parts.append(part)
        values = values - part.astype(F32)
    return parts


def covariance_kernel(train_ref, cov_ref, held, turned, by_in, by_out, arrived):
    examples, width = train_ref.shape
    blocks = width // LANES
    parts = examples // LANES
    pitch = turned.shape[1] // blocks
    chunks, _, chunk = held.shape
    copies = []
    for g in range(chunks):
        source = train_ref.at[:, pl.ds(g * chunk, chunk)]
        copies.append(pltpu.make_async_copy(source, held.at[g], arrived.at[g]))
        copies[-1].start()
    for c in range(blocks):
        if c * LANES % chunk == 0:
            copies[c * LANES // chunk].wait()
        begin = c * LANES % chunk
        block = held[c * LANES // chunk, :, begin:begin + LANES].astype(F32).T
        for part in range(parts):
            turned[part, c * pitch:c * pitch + LANES, :] = block[:, part * LANES:(part + 1) * LANES]
        for half in range(2):
            start = (2 * c + half) * examples
            by_in[:, start:start + examples] = block[half * K_IN:(half + 1) * K_IN, :].astype(BF16)
    for j in range(K_IN):
        for part in range(parts):
            start = j * examples + part * LANES
            for half in range(2):
                rows = turned[part, pl.ds(half * K_IN + j, blocks, stride=pitch), :]
                by_out[half * blocks:(half + 1) * blocks, start:start + LANES] = rows.astype(BF16)
    in_sum = lax.dot_general(by_in[...], by_in[...], NT, preferred_element_type=F32)
    out_sum = lax.dot_general(by_out[...], by_out[...], NT, preferred_element_type=F32)
    cov_ref[...] = jnp.concatenate([in_sum, out_sum], axis=1)


def covariance_sums(train):
    examples, width = train.shape
    chunks = 4 if width % (4 * LANES) == 0 else 1
    return pl.pallas_call(
        covariance_kernel,
        out_shape=jax.ShapeDtypeStruct((K_OUT, 2 * K_IN), F32),
        in_specs=[pl.BlockSpec(memory_space=pltpu.HBM)],
        out_specs=pl.BlockSpec(memory_space=pltpu.VMEM),
        scratch_shapes=[
            pltpu.VMEM((chunks, examples, width // chunks), BF16),
            pltpu.VMEM((examples // LANES, width // LANES * (LANES + 8), LANES), F32),
            pltpu.VMEM((K_IN, K_OUT * examples), BF16),
            pltpu.VMEM((K_OUT, K_IN * examples), BF16),
            pltpu.SemaphoreType.DMA((chunks,)),
        ],
        compiler_params=pltpu.CompilerParams(vmem_limit_bytes=STAGE_VMEM_LIMIT),
        cost_estimate=pl.CostEstimate(flops=64 * examples * 64**3, bytes_accessed=2 * examples * width, transcendentals=0),
        name="covariance",
    )(train)


def turn_kernel(query_ref, out_ref, spread):
    count, width = query_ref.shape
    blocks = width // LANES
    pairs = count // 2
    pitch = spread.shape[0] // blocks
    for c in range(blocks):
        spread[c * pitch:c * pitch + count, :] = query_ref[:, c * LANES:(c + 1) * LANES].astype(F32)
    for p in range(pairs):
        first = spread[pl.ds(p, blocks, stride=pitch), :]
        second = spread[pl.ds(p + pairs, blocks, stride=pitch), :]
        even, odd = swap_pair(first, second)
        out_ref[:blocks, p * LANES:(p + 1) * LANES] = even.astype(BF16)
        out_ref[blocks:, p * LANES:(p + 1) * LANES] = odd.astype(BF16)


def turned_queries(queries):
    total, width = queries.shape
    return pl.pallas_call(
        turn_kernel,
        out_shape=jax.ShapeDtypeStruct((K_OUT, total * K_IN), BF16),
        grid=(total // HALF,),
        in_specs=[pl.BlockSpec((HALF, width), lambda step: (step, 0))],
        out_specs=pl.BlockSpec((K_OUT, HALF * K_IN), lambda step: (0, step)),
        scratch_shapes=[pltpu.VMEM((width // LANES * (HALF + 8), LANES), F32)],
        compiler_params=pltpu.CompilerParams(vmem_limit_bytes=VMEM_LIMIT),
        cost_estimate=pl.CostEstimate(flops=4096 * total * width, bytes_accessed=4 * total * width, transcendentals=0),
        name="turn_queries",
    )(queries)


def damped(cov, total_count):
    rows = lax.broadcasted_iota(jnp.int32, (K_OUT, LANES), 0)
    lanes = lax.broadcasted_iota(jnp.int32, (K_OUT, LANES), 1)
    low = lanes < K_IN
    diagonal = rows == jnp.where(low, lanes, lanes - K_IN)
    cov = cov * (1.0 / total_count)
    on_diagonal = jnp.sum(jnp.where(diagonal, cov, 0.0), axis=0, keepdims=True)
    low_row = low_half(1)
    in_mean = jnp.sum(jnp.where(low_row, on_diagonal, 0.0), axis=1, keepdims=True) / K_IN
    out_mean = jnp.sum(jnp.where(low_row, 0.0, on_diagonal), axis=1, keepdims=True) / K_OUT
    scale = jnp.where(low_row, 1.0 / in_mean, 1.0)
    added = jnp.where(low_row, 0.1, 0.1 * out_mean)
    return cov * scale + jnp.where(diagonal, added, 0.0)


def inverses(matrix):
    size = matrix.shape[0]
    sub = 8
    lanes = lax.broadcasted_iota(jnp.int32, (sub, LANES), 1)
    offset = jnp.where(lanes < size, 0, size)
    place = lanes - offset
    row = lax.broadcasted_iota(jnp.int32, (sub, LANES), 0)
    tiles = [matrix[k:k + sub, :] for k in range(0, size, sub)]

    def spread_row(values, at):
        return jnp.broadcast_to(values[at:at + 1, :], (sub, LANES))

    def column(values, lane):
        return jnp.take_along_axis(values, offset + lane, axis=1, mode="promise_in_bounds")

    for begin in range(0, size, PIVOT):
        owner, first_row = begin // sub, begin % sub
        inside = (place >= begin) & (place < begin + PIVOT)
        columns = [[column(tile, begin + a) for a in range(PIVOT)] for tile in tiles]
        p = [[None] * PIVOT for _ in range(PIVOT)]
        for a in range(PIVOT):
            for b in range(a, PIVOT):
                p[a][b] = p[b][a] = spread_row(columns[owner][b], first_row + a)
        r = []
        for a in range(PIVOT):
            unit = jnp.where(place == begin + a, 1.0, 0.0)
            r.append(jnp.where(inside, unit, spread_row(tiles[owner], first_row + a)))
        det = 1.0 / (p[0][0] * p[1][1] - p[0][1] * p[1][0])
        across = -p[0][1] * det
        e = [[p[1][1] * det, across], [across, p[0][0] * det]]
        u = [[e[a][0] * p[0][b] + e[a][1] * p[1][b] for b in (2, 3)] for a in (0, 1)]
        s = [p[a][b + 2] - (p[a][0] * u[0][b] + p[a][1] * u[1][b]) for a, b in ((2, 0), (2, 1), (3, 1))]
        det = 1.0 / (s[0] * s[2] - s[1] * s[1])
        across = -s[1] * det
        f = [[s[2] * det, across], [across, s[0] * det]]
        w = [e[a][0] * r[0] + e[a][1] * r[1] for a in (0, 1)]
        t = [r[a] - (p[a][0] * w[0] + p[a][1] * w[1]) for a in (2, 3)]
        last = [f[a][0] * t[0] + f[a][1] * t[1] for a in (0, 1)]
        first = [w[a] - (u[a][0] * last[0] + u[a][1] * last[1]) for a in (0, 1)]
        solved = first + last
        even = (row & 1) == 0
        upper = (row & 2) == 0
        stored = jnp.where(upper, jnp.where(even, solved[0], solved[1]), jnp.where(even, solved[2], solved[3]))
        mine = (row >= first_row) & (row < first_row + PIVOT)
        for k in range(len(tiles)):
            part = [columns[k][a] * solved[a] for a in range(PIVOT)]
            rest = jnp.where(inside, 0.0, tiles[k]) - (part[2] + part[3])
            rest = rest - (part[0] + part[1])
            tiles[k] = jnp.where(mine, stored, rest) if k == owner else rest
    return jnp.concatenate(tiles, axis=0)


def inverse_kernel(total_count, cov_ref, left_ref, right_ref):
    inverse = inverses(damped(cov_ref[...], total_count))
    turned = pltpu.roll(inverse, LANES // 2, 1)
    low = low_half(K_OUT)
    left_ref[...] = jnp.concatenate(split(turned[:, :K_OUT], 3), axis=0)
    double = jnp.concatenate([jnp.where(low, inverse, 0.0), jnp.where(low, 0.0, turned)], axis=0)
    high, small = split(double, 2)
    right_ref[:LANES, :LANES] = high
    right_ref[:LANES, LANES:] = small
    right_ref[LANES:, :LANES] = high
    right_ref[LANES:, LANES:] = jnp.zeros_like(small)


def inverse_factors(cov, total_count):
    return pl.pallas_call(
        functools.partial(inverse_kernel, total_count),
        out_shape=(
            jax.ShapeDtypeStruct((3 * K_OUT, K_OUT), BF16),
            jax.ShapeDtypeStruct((2 * LANES, 2 * LANES), BF16),
        ),
        in_specs=[pl.BlockSpec(memory_space=pltpu.VMEM)],
        out_specs=(pl.BlockSpec(memory_space=pltpu.VMEM), pl.BlockSpec(memory_space=pltpu.VMEM)),
        compiler_params=pltpu.CompilerParams(vmem_limit_bytes=VMEM_LIMIT),
        cost_estimate=pl.CostEstimate(flops=INVERSE_COST, bytes_accessed=0, transcendentals=0),
        name="inverses",
    )(cov)


def score_kernel(route_ref, left_ref, right_ref, first_ref, second_ref, train_ref, out_ref, solved, wide, ready):
    blocks = K_OUT // 2
    pairs = HALF // 2
    pitch = solved.shape[0] // (2 * pairs)
    step = pl.program_id(0)
    group = 4
    for side, turned_ref in enumerate((first_ref, second_ref)):
        for g in range(pairs // group):
            block = turned_ref[:, g * group * LANES:(g + 1) * group * LANES]
            terms = jnp.dot(left_ref[...], block, preferred_element_type=F32)
            once = terms[:K_OUT, :] + (terms[K_OUT:2 * K_OUT, :] + terms[2 * K_OUT:, :])
            for k in range(group):
                high, small = split(once[:, k * LANES:(k + 1) * LANES], 2)
                at = (side * pairs + g * group + k) * K_OUT
                wide[at:at + K_OUT, :LANES] = high
                wide[at:at + K_OUT, LANES:] = small
    twice = jnp.dot(wide[...], right_ref[...], preferred_element_type=F32)
    for p in range(2 * pairs):
        part = twice[p * K_OUT:(p + 1) * K_OUT, :]
        solved[p * pitch:p * pitch + K_OUT, :] = part[:, :LANES] + part[:, LANES:]
    for c in range(blocks):
        first = solved[pl.ds(c, 2 * pairs, stride=pitch), :]
        second = solved[pl.ds(c + blocks, 2 * pairs, stride=pitch), :]
        even, odd = swap_pair(first, second)
        columns = slice(c * LANES, (c + 1) * LANES)
        for side in range(2):
            at = side * HALF
            ready[at:at + pairs, columns] = even[side * pairs:(side + 1) * pairs, :].astype(BF16)
            ready[at + pairs:at + HALF, columns] = odd[side * pairs:(side + 1) * pairs, :].astype(BF16)
    scores = lax.dot_general(ready[...], train_ref[...], NT, preferred_element_type=F32)
    per_query = out_ref.shape[2]
    parts = out_ref.shape[1]
    for s in range(CHUNK // per_query):
        owner = route_ref[step * (CHUNK // per_query) + s]
        for part in range(parts):
            piece = scores[s * per_query:(s + 1) * per_query, part * LANES:(part + 1) * LANES]
            out_ref[owner, part, :, :] = piece


def all_scores(route, factors, turned, train, per_query):
    shard_count = route.shape[0]
    examples, width = train.shape
    steps = shard_count * per_query // CHUNK
    parts = examples // LANES
    if len(turned) == 2:
        places = [lambda step: (0, 0), lambda step: (0, 0)]
    else:
        turned = turned * 2
        places = [lambda step: (0, 2 * step), lambda step: (0, 2 * step + 1)]
    return pl.pallas_call(
        score_kernel,
        out_shape=jax.ShapeDtypeStruct((shard_count, parts, per_query, LANES), F32),
        grid=(steps,),
        in_specs=[
            pl.BlockSpec(memory_space=pltpu.SMEM),
            pl.BlockSpec((3 * K_OUT, K_OUT), lambda step: (0, 0)),
            pl.BlockSpec((2 * LANES, 2 * LANES), lambda step: (0, 0)),
            pl.BlockSpec((K_OUT, HALF * K_IN), places[0]),
            pl.BlockSpec((K_OUT, HALF * K_IN), places[1]),
            pl.BlockSpec((examples, width), lambda step: (0, 0)),
        ],
        out_specs=pl.BlockSpec((shard_count, parts, per_query, LANES), lambda step: (0, 0, 0, 0)),
        scratch_shapes=[
            pltpu.VMEM((HALF * (K_OUT + 8), LANES), F32),
            pltpu.VMEM((HALF * K_OUT, 2 * LANES), BF16),
            pltpu.VMEM((CHUNK, width), BF16),
        ],
        compiler_params=pltpu.CompilerParams(vmem_limit_bytes=VMEM_LIMIT),
        cost_estimate=pl.CostEstimate(
            flops=2 * shard_count * per_query * width * (examples + 128), bytes_accessed=2 * examples * width, transcendentals=0
        ),
        name="products_and_scores",
    )(route, *factors, *turned, train)


def exchange(values, distance, count):
    return lax.ppermute(values, "dp", [(k, k ^ distance) for k in range(count)])


def shards(train_grads, query_grads, listed):
    shard_count = lax.axis_size("dp")
    layers = lax.axis_size("layer")
    own_index = lax.axis_index("dp").astype(jnp.int32)
    examples = train_grads.shape[0]
    per_query = query_grads.shape[0]
    train = train_grads.reshape(examples, train_grads.shape[2])
    own_queries = query_grads.reshape(per_query, query_grads.shape[2])
    total_count = float(examples * shard_count)
    order = jnp.arange(shard_count, dtype=jnp.int32)
    if shard_count == 8:
        far = exchange(own_queries, 4, shard_count)
        cov = covariance_sums(train)
        far, _ = lax.optimization_barrier((far, cov))
        column = jnp.concatenate([own_queries, far], axis=0)
        cov = cov + exchange(cov, 1, shard_count)
        near = exchange(column, 2, shard_count)
        column = jnp.concatenate([column, near], axis=0)
        cov = cov + exchange(cov, 4, shard_count)
        beside = exchange(column, 1, shard_count)
        last = exchange(cov, 2, shard_count)
        here, cov = lax.optimization_barrier((turned_queries(column), cov))
        factors = inverse_factors(cov + last, total_count)
        beside, _ = lax.optimization_barrier((beside, factors[0]))
        turned = [here, turned_queries(beside)]
        order = jnp.array([0, 4, 2, 6, 1, 5, 3, 7], jnp.int32)
        route = own_index ^ order
    else:
        turned = [turned_queries(lax.all_gather(own_queries, "dp", axis=0, tiled=True))]
        cov = lax.psum(covariance_sums(train), "dp")
        factors = inverse_factors(cov, total_count)
        route = order
    scores = all_scores(route, factors, turned, train, per_query)
    outgoing = scores.reshape(shard_count * layers, per_query, examples // layers)
    wanted = listed[0][:, None] == jnp.arange(shard_count, dtype=jnp.int32)[None, :]
    wanted, outgoing = lax.optimization_barrier((wanted, outgoing))
    received = lax.all_to_all(outgoing, ("dp", "layer"), split_axis=0, concat_axis=0, tiled=True)
    received = received.reshape(1, shard_count, layers, per_query, examples // layers)
    return jnp.sum(jnp.where(wanted[:, :, None, None, None], received, 0.0), axis=(1, 2))


def solution(mesh):
    in_specs = (
        P(("groups", "dp"), "layer", None),
        P(("groups", "dp"), "layer", None),
        P(("groups", "dp"), None),
    )
    out_specs = P(("groups", "dp"), None, "layer")
    return jax.shard_map(shards, mesh=mesh, in_specs=in_specs, out_specs=out_specs, check_vma=False)
```
